32 devices in a mesh: wide: 8 (over z, x), narrow: 4 (over y, core).
Axes of the slice: x: 2, y: 2, z: 4, core: 2. Of those that a mesh axis runs over, the one named last changes fastest.
Arguments:
- tokens: bfloat16 [32768, 1024], P(('wide', 'narrow')), may hold values from -6 to 6
- attn_gain: bfloat16 [1024], P(('wide', 'narrow')), may hold values from 0.099609375 to 1.8984375
- attn_shift: bfloat16 [1024], P(('wide', 'narrow')), may hold values from -3 to 3
- qkv_weight: bfloat16 [1024, 3072], P(('wide', 'narrow')), may hold values from -0.1875 to 0.1875
- qv_bias: bfloat16 [2048], P(('wide', 'narrow')), may hold values from -3 to 3
- out_weight: bfloat16 [1024, 1024], P(('wide', 'narrow')), may hold values from -3 to 3
- out_bias: bfloat16 [1024], P(('wide', 'narrow')), may hold values from -3 to 3
- mlp_gain: bfloat16 [1024], P(('wide', 'narrow')), may hold values from 0.099609375 to 1.8984375
- mlp_shift: bfloat16 [1024], P(('wide', 'narrow')), may hold values from -3 to 3
- up_weight: bfloat16 [1024, 4096], P(('wide', 'narrow')), may hold values from -0.1875 to 0.1875
- up_bias: bfloat16 [4096], P(('wide', 'narrow')), may hold values from -3 to 3
- down_weight: bfloat16 [4096, 1024], P(('wide', 'narrow')), may hold values from -0.125 to 0.125
- down_bias: bfloat16 [1024], P(('wide', 'narrow')), may hold values from -3 to 3
- cotangent: bfloat16 [32768, 1024], P(('wide', 'narrow')), may hold values from -6 to 6
Outputs:
- output: bfloat16 [32768, 1024], P(('wide', 'narrow'))
- grad_tokens: bfloat16 [32768, 1024], P(('wide', 'narrow'))
- grad_attn_gain: float32 [1024], P(('wide', 'narrow'))
- grad_attn_shift: float32 [1024], P(('wide', 'narrow'))
- grad_qkv_weight: float32 [1024, 3072], P(('wide', 'narrow'))
- grad_qv_bias: float32 [2048], P(('wide', 'narrow'))
- grad_out_weight: float32 [1024, 1024], P(('wide', 'narrow'))
- grad_out_bias: float32 [1024], P(('wide', 'narrow'))
- grad_mlp_gain: float32 [1024], P(('wide', 'narrow'))
- grad_mlp_shift: float32 [1024], P(('wide', 'narrow'))
- grad_up_weight: float32 [1024, 4096], P(('wide', 'narrow'))
- grad_up_bias: float32 [4096], P(('wide', 'narrow'))
- grad_down_weight: float32 [4096, 1024], P(('wide', 'narrow'))
- grad_down_bias: float32 [1024], P(('wide', 'narrow'))
The draws below stay inside these ranges and needn't reach their ends.
All inputs are finite; a program needn't handle non-finite values.
Results may differ from the reference program's by a relative error of at most 0.012.
The reference program's roundings to bfloat16 on the way count: a program that leaves them out, or rounds other values in their place, can miss the bound.
Values may be sent and summed in bfloat16 or wider, within the bound.
A program may use at most 320 MiB of HBM per device.

```python
import math
import jax
import jax.numpy as jnp
from jax import lax

D = 1024
H = 16
HD = 64
FF = 4096
SEQ = 1024
TOKENS = 32768


def level_of(stream_key, dims, shards, low, largest):
    gain, own = 1.0, jax.random.fold_in(stream_key, 6)
    for dim, parts in shards:
        steps = jnp.exp(jax.random.uniform(jax.random.fold_in(own, dim), (parts,), jnp.float32, low / len(shards), largest / len(shards)))
        gain = gain * jnp.repeat(steps, dims[dim] // parts).reshape([-1 if axis == dim else 1 for axis in range(len(dims))])
    return gain


def bell_draw(own_key, extent, width, most, cuts=(), kind=jnp.bfloat16):
    drawn = jax.random.normal(own_key, extent, jnp.float32) * width
    if len(cuts) > 0:
        drawn = level_of(own_key, extent, cuts, -0.22, 0.18) * drawn
    return jnp.clip(drawn, min=-most, max=most).astype(kind)


def setup_inputs(seed: int = 0) -> dict:
    keys = jax.random.split(jax.random.key(seed), 15)
    return {
        "tokens": bell_draw(keys[0], (TOKENS, D), 1.0, 6.0, ((0, 32),)),
        "attn_gain": jnp.clip(1.0 + 0.18 * jax.random.normal(keys[1], (D,), jnp.float32), 0.099609375, 1.8984375).astype(jnp.bfloat16),
        "attn_shift": bell_draw(keys[2], (D,), 0.5, 3.0, ((0, 32),)),
        "qkv_weight": bell_draw(keys[3], (D, 3 * D), D ** -0.5, 0.1875, ((0, 32),)),
        "qv_bias": bell_draw(keys[4], (2 * D,), 0.5, 3.0, ((0, 32),)),
        "out_weight": bell_draw(keys[5], (D, D), (max(D * 4 // SEQ, 1)) ** -0.5, 3.0, ((0, 32),)),
        "out_bias": bell_draw(keys[6], (D,), 0.5, 3.0, ((0, 32),)),
        "mlp_gain": jnp.clip(1.0 + 0.18 * jax.random.normal(keys[7], (D,), jnp.float32), 0.099609375, 1.8984375).astype(jnp.bfloat16),
        "mlp_shift": bell_draw(keys[8], (D,), 0.5, 3.0, ((0, 32),)),
        "up_weight": bell_draw(keys[9], (D, FF), D ** -0.5, 0.1875, ((0, 32),)),
        "up_bias": bell_draw(keys[10], (FF,), 0.5, 3.0, ((0, 32),)),
        "down_weight": bell_draw(keys[11], (FF, D), (FF // 2) ** -0.5, 0.125, ((0, 32),)),
        "down_bias": bell_draw(keys[12], (D,), 0.5, 3.0, ((0, 32),)),
        "cotangent": bell_draw(keys[13], (TOKENS, D), 1.0, 6.0, ((0, 32),)),
    }


epsilon = 1e-05

@jax.custom_vjp
def low(v):
    return lax.optimization_barrier(v.astype(jnp.bfloat16)).astype(jnp.float32)

@jax.custom_vjp
def low_back(v):
    return v

def low_keep(v):
    return (low(v), None)

def low_pass(kept, grad):
    return (grad,)

def back_keep(v):
    return (v, None)

def back_low(kept, grad):
    return (low(grad),)
low.defvjp(low_keep, low_pass)
low_back.defvjp(back_keep, back_low)

def product(left, right):
    return jnp.matmul(left, right, precision=lax.Precision.HIGHEST)

def layer_norm(values_in, gain_vec, bias_vec):
    row_mean = lax.optimization_barrier(jnp.mean(values_in, axis=-1, keepdims=True))
    centred = values_in - row_mean
    spread = lax.optimization_barrier(jnp.mean(centred * centred, axis=-1, keepdims=True))
    return centred * lax.rsqrt(spread + epsilon) * gain_vec + bias_vec

def forward(inputs, attn_gain, attn_shift, qkv_weight, qv_bias, out_weight, out_bias, mlp_gain, mlp_shift, up_weight, up_bias, down_weight, down_bias):
    groups, length, model_width = inputs.shape
    act_a = low(layer_norm(inputs, attn_gain, attn_shift))
    bias_full = jnp.concatenate([qv_bias[:model_width], jnp.zeros((model_width,), jnp.float32), qv_bias[model_width:]])
    projected = low(low_back(product(act_a, qkv_weight) + bias_full))

    def heads_of(part):
        return part.reshape(groups, length, H, HD).transpose(0, 2, 1, 3)
    query_rows = heads_of(projected[..., :model_width])
    key_rows = heads_of(projected[..., model_width:2 * model_width])
    value_rows = heads_of(projected[..., 2 * model_width:])
    block_rows = min(512, length)
    block_count = length // block_rows
    query_blocks = query_rows.reshape(groups, H, block_count, block_rows, HD).transpose(2, 0, 1, 3, 4)

    def attend_block(query_block):
        scores = jnp.einsum('ghqe,ghke->ghqk', query_block, key_rows, precision=lax.Precision.HIGHEST) * HD ** (-0.5)
        scores = low_back(scores)
        row_max = lax.optimization_barrier(jnp.max(scores, axis=-1, keepdims=True))
        exp_scores = jnp.exp(scores - row_max)
        attn_probs = exp_scores / lax.optimization_barrier(jnp.sum(exp_scores, axis=-1, keepdims=True))
        return jnp.einsum('ghqk,ghke->ghqe', low(attn_probs), value_rows, precision=lax.Precision.HIGHEST)
    mixed_blocks = lax.map(jax.checkpoint(attend_block), query_blocks)
    mixed = low(low_back(mixed_blocks.transpose(1, 0, 3, 2, 4).reshape(groups, length, model_width)))
    hidden = inputs + low_back(product(mixed, out_weight) + out_bias)
    act_b = low(layer_norm(hidden, mlp_gain, mlp_shift))
    pre_up = low_back(product(act_b, up_weight) + up_bias)
    act_c = low(jax.nn.gelu(pre_up, approximate=False))
    return hidden + low_back(product(act_c, down_weight) + down_bias)

def reference(tokens, attn_gain, attn_shift, qkv_weight, qv_bias, out_weight, out_bias, mlp_gain, mlp_shift, up_weight, up_bias, down_weight, down_bias, cotangent):
    params = tuple((p.astype(jnp.float32) for p in (attn_gain, attn_shift, qkv_weight, qv_bias, out_weight, out_bias, mlp_gain, mlp_shift, up_weight, up_bias, down_weight, down_bias)))
    total_rows, model_width = tokens.shape
    seq_count = total_rows // SEQ
    group_size = math.gcd(max(1, 4096 // SEQ), seq_count)
    inputs = tokens.astype(jnp.float32).reshape(seq_count // group_size, group_size, SEQ, model_width)
    grads_in = cotangent.astype(jnp.float32).reshape(seq_count // group_size, group_size, SEQ, model_width)

    def one_group(totals, scan_pair):
        group_in, group_grad = scan_pair
        result, pull_back = jax.vjp(forward, group_in, *params)
        pulled = pull_back(group_grad)
        return (tuple((a + b for a, b in zip(totals, pulled[1:]))), (result, pulled[0]))
    zero_grads = tuple((jnp.zeros_like(p) for p in params))
    totals, (results, input_grads) = lax.scan(one_group, zero_grads, (inputs, grads_in))
    return (results.reshape(total_rows, model_width).astype(jnp.bfloat16), input_grads.reshape(total_rows, model_width).astype(jnp.bfloat16), totals[0], totals[1], totals[2], totals[3], totals[4], totals[5], totals[6], totals[7], totals[8], totals[9], totals[10], totals[11])
```

```python
import functools
import jax
import jax.numpy as jnp
from jax import lax
from jax.experimental import pallas as pl
from jax.experimental.pallas import tpu as pltpu
from jax.sharding import PartitionSpec as P

H = 16
HD = 64
epsilon = 1e-05
bf16 = jnp.bfloat16
f32 = jnp.float32
NN = (((1,), (0,)), ((), ()))
NT = (((1,), (1,)), ((), ()))
TN = (((0,), (0,)), ((), ()))
ALL = slice(None)
MESH = pl.DeviceIdType.MESH
HBM = pl.BlockSpec(memory_space=pltpu.HBM)

ORDERS = ((0, 2, 1, 3), (0, 3, 1, 2))
PIECES = 12
LAG_F = 2
LAG_B = 1


def dot(a, b, dims):
    return lax.dot_general(a, b, dims, preferred_element_type=f32)


def device_bits():
    w = lax.axis_index("wide")
    n = lax.axis_index("narrow")
    return (w // 4, (w // 2) % 2, w % 2, n // 2, n % 2)


def flipped(b, dim):
    t = tuple(1 - v if i == dim else v for i, v in enumerate(b))
    return (t[0] * 4 + t[1] * 2 + t[2], t[3] * 2 + t[4])


def enter(b):
    barrier = pltpu.get_barrier_semaphore()
    for dim in range(5):
        pl.semaphore_signal(barrier, inc=1, device_id=flipped(b, dim), device_id_type=MESH)
    return lambda: pl.semaphore_wait(barrier, 5)


def head_mask(head, rows):
    return lax.shift_right_logical(lax.broadcasted_iota(jnp.int32, (rows, 256), 1), 6) == head


def norm_stats(v):
    mean = jnp.mean(v, axis=1, keepdims=True)
    centred = v - mean
    rstd = lax.rsqrt(jnp.mean(centred * centred, axis=1, keepdims=True) + epsilon)
    return centred, rstd


def quarter(kind, group):
    return group + (0, 2, 4)[kind] if group < 2 else group + (4, 6, 8)[kind]


def forward_kernel(
    tok_h, vec_h, qkv_h, out_h, up_h, down_h,
    gw, rows_o, upb_o, actt_o, proj_o, mixt_o, lse_o, hid_o, actb_o, actbt_o,
    gv, tok, act, wbuf, proj, mixed, trans, oacc, lse, hid, rows, upb,
    lsem, ssem, rsem, vssem, vrsem, osem, wsem,
):
    b = device_bits()
    ready = enter(b)
    sources = [
        [(qkv_h.at[:, 0:512], 0), (qkv_h.at[:, 1024:1536], 512)],
        [(qkv_h.at[:, 2048:2560], 0), (qkv_h.at[:, 512:1024], 512)],
        [(qkv_h.at[:, 1536:2048], 0), (qkv_h.at[:, 2560:3072], 512)],
        [(out_h, None)],
    ]
    sources += [[(down_h.at[pl.ds(32 * i, 32)], None)] for i in range(4)]
    sources += [[(up_h.at[:, pl.ds(1024 * i, 1024)], None)] for i in range(4)]
    vec_in = pltpu.make_async_copy(vec_h, gv.at[b], lsem.at[0])
    vec_in.start()
    tok_in = pltpu.make_async_copy(tok_h, tok, lsem.at[1])
    own, k = [], 2
    for p in range(PIECES):
        own.append([])
        for src, col in sources[p]:
            dst = gw.at[(p,) + b] if col is None else gw.at[(p,) + b + (ALL, pl.ds(col, 512))]
            cp = pltpu.make_async_copy(src, dst, lsem.at[k])
            cp.start()
            own[p].append(cp)
            k += 1
    tok_in.start()
    ready()
    pend = {}

    def send(p, dim, sub, s):
        cp = pltpu.make_async_remote_copy(
            src_ref=gw.at[(p,) + sub], dst_ref=gw.at[(p,) + sub], send_sem=ssem.at[p, s], recv_sem=rsem.at[p, s],
            device_id=flipped(b, dim), device_id_type=MESH)
        cp.start()
        pend[(p, s)] = cp

    def stage(p, r):
        if r == 0:
            for cp in own[p]:
                cp.wait()
        for h in range(2):
            order = ORDERS[h]
            cols = (ALL, pl.ds(h * 512, 512))
            if r > 0:
                pend[(p, h * 6 + r - 1)].wait_recv()
            sub = tuple(ALL if i in order[:r] else b[i] for i in range(5)) + cols
            if r < 4:
                send(p, order[r], sub, h * 6 + r)
            if r == 3:
                send(p, 4, sub, h * 6 + 4)
            if r == 4:
                last = tuple(ALL if i in order[:3] else (1 - b[i] if i == order[3] else b[i]) for i in range(5))
                send(p, 4, last + cols, h * 6 + 5)

    def tick(t):
        for r in range(4, -1, -1):
            if 0 <= t - r * LAG_F < PIECES:
                stage(t - r * LAG_F, r)

    def arrive(p):
        for s in (4, 5, 10, 11):
            pend[(p, s)].wait_recv()

    vec_order = (0, 2, 1, 3, 4)
    vpend = []

    def vec_round(r):
        if r == 0:
            vec_in.wait()
        else:
            vpend[r - 1].wait_recv()
        if r < 5:
            sub = tuple(ALL if i in vec_order[:r] else b[i] for i in range(5))
            cp = pltpu.make_async_remote_copy(
                src_ref=gv.at[sub], dst_ref=gv.at[sub], send_sem=vssem.at[r], recv_sem=vrsem.at[r],
                device_id=flipped(b, vec_order[r]), device_id_type=MESH)
            cp.start()
            vpend.append(cp)

    outs = []

    def put(src, dst):
        cp = pltpu.make_async_copy(src, dst, osem.at[len(outs)])
        cp.start()
        outs.append(cp)

    for t in range(6):
        tick(t)
        vec_round(t)

    table = gv[...].reshape(32, 8, 128)
    sub_index = lax.broadcasted_iota(jnp.int32, (32, 8, 128), 1)
    lines = [jnp.sum(jnp.where(sub_index == r, table, 0.0), axis=1) for r in range(3)]

    def spread(line, offset, log, base):
        j = lax.broadcasted_iota(jnp.int32, (128, 1024), 0)
        n = lax.broadcasted_iota(jnp.int32, (128, 1024), 1)
        pick = jnp.where(j == offset + (n & ((1 << log) - 1)), 1.0, 0.0).astype(bf16)
        wide = dot(line.astype(bf16), pick, NN)
        d = lax.broadcasted_iota(jnp.int32, (32, 1024), 0)
        n = lax.broadcasted_iota(jnp.int32, (32, 1024), 1)
        return jnp.sum(jnp.where(d == base + lax.shift_right_logical(n, log), wide, 0.0), axis=0, keepdims=True)

    places = ((0, 0, 5, 0), (0, 32, 5, 0), (0, 64, 5, 0), (0, 96, 5, 0), (1, 0, 5, 0), (1, 32, 5, 0), (1, 64, 6, 0), (1, 64, 6, 16))
    for i, (line, offset, log, base) in enumerate(places):
        rows[i : i + 1, :] = spread(lines[line], offset, log, base)
    for d in range(32):
        upb[d // 4, :, (d % 4) * 128 : (d % 4) * 128 + 128] = jnp.broadcast_to(lines[2][d : d + 1, :], (8, 128))
    put(rows, rows_o)
    put(upb, upb_o)

    tok_in.wait()
    for i in range(4):
        r = pl.ds(256 * i, 256)
        centred, rstd = norm_stats(tok[r, :].astype(f32))
        a = (centred * rstd * rows[0:1, :] + rows[1:2, :]).astype(bf16)
        act[r, :] = a
        trans[0, :, r] = a.T
    put(trans.at[0], actt_o)

    def load_weight(p, slot):
        arrive(p)
        cp = pltpu.make_async_copy(gw.at[p], wbuf.at[slot], wsem.at[slot])
        cp.start()
        cp.wait()

    def project(p, slot):
        zero = jnp.zeros((1, 512), f32)
        q_lo, q_hi, v_lo, v_hi = rows[6:7, 0:512], rows[6:7, 512:1024], rows[7:8, 0:512], rows[7:8, 512:1024]
        bias = jnp.concatenate(((q_lo, zero), (v_lo, q_hi), (zero, v_hi))[p], axis=1)

        def block(i, carry):
            r = pl.ds(pl.multiple_of(i * 256, 256), 256)
            x = (dot(act[r, :], wbuf[slot].reshape(1024, 1024), NN) + bias).astype(bf16)
            for j in range(4):
                proj[4 * p + j, r, :] = x[:, 256 * j : 256 * j + 256]
            return carry

        lax.fori_loop(0, 4, block, 0)

    def attend(group, first):
        q, k, v = (proj.at[quarter(kind, group)] for kind in range(3))

        def one(i, carry):
            head = first + i
            mask = head_mask(head, 1024)
            vm = jnp.where(mask, v[...], bf16(0))
            lane = lax.broadcasted_iota(jnp.int32, (512, 128), 1)
            for j in range(2):
                r = pl.ds(512 * j, 512)
                qm = jnp.where(mask[:512], q[r, :], bf16(0)) * bf16(0.125)
                s = dot(qm, k[...], NT)
                m = jnp.max(s, axis=1, keepdims=True)
                p = jnp.exp(s - m)
                total = jnp.sum(p, axis=1, keepdims=True)
                o = dot(p.astype(bf16), vm, NN) * (1.0 / total)
                oacc[r, :] = jnp.where(mask[:512], o, oacc[r, :])
                lse[r, :] = jnp.where(lane == group * 4 + head, m + jnp.log(total), lse[r, :])
            return carry

        lax.fori_loop(0, 2, one, 0)

    lse[...] = jnp.zeros_like(lse)
    t = 6
    for t in range(6, 10):
        tick(t)
    load_weight(0, 0)
    project(0, 0)
    tick(10)
    load_weight(1, 1)
    project(1, 1)
    t = 11
    for group in range(4):
        if group == 2:
            load_weight(2, 0)
            project(2, 0)
        for first in (0, 2):
            attend(group, first)
            tick(t)
            t += 1
        mixed[:, 256 * group : 256 * group + 256] = oacc[...].astype(bf16)
    put(proj, proj_o)
    put(lse, lse_o)
    load_weight(3, 1)
    outs[2].wait()
    for i in range(4):
        r = pl.ds(256 * i, 256)
        v = tok[r, :].astype(f32) + dot(mixed[r, :], wbuf[1].reshape(1024, 1024), NN) + rows[2:3, :]
        hid[r, :] = v
        centred, rstd = norm_stats(v)
        a = (centred * rstd * rows[3:4, :] + rows[4:5, :]).astype(bf16)
        act[r, :] = a
        trans[0, :, r] = a.T
        trans[1, :, r] = mixed[r, :].T
    put(hid, hid_o)
    put(act, actb_o)
    put(trans.at[0], actbt_o)
    put(trans.at[1], mixt_o)
    while t < PIECES + 4 * LAG_F:
        tick(t)
        t += 1
    for p in range(4, PIECES):
        arrive(p)
    for cp in pend.values():
        cp.wait_send()
    for cp in vpend:
        cp.wait_send()
    for i, cp in enumerate(outs):
        if i != 2:
            cp.wait()


def forward_call(tok, vec, qkv, out, up, down):
    S = jax.ShapeDtypeStruct
    sem = pltpu.SemaphoreType.DMA
    big = (2, 2, 2, 2, 2, 32, 1024)
    return pl.pallas_call(
        forward_kernel,
        out_shape=(
            S((PIECES,) + big, bf16), S((16, 1024), f32), S((8, 8, 512), f32), S((1024, 1024), bf16), S((12, 1024, 256), bf16),
            S((1024, 1024), bf16), S((1024, 128), f32), S((1024, 1024), f32), S((1024, 1024), bf16), S((1024, 1024), bf16)),
        in_specs=[HBM] * 6,
        out_specs=(HBM,) * 10,
        scratch_shapes=[
            pltpu.VMEM((2, 2, 2, 2, 2, 8, 128), f32), pltpu.VMEM((1024, 1024), bf16), pltpu.VMEM((1024, 1024), bf16),
            pltpu.VMEM((2,) + big, bf16), pltpu.VMEM((12, 1024, 256), bf16), pltpu.VMEM((1024, 1024), bf16),
            pltpu.VMEM((2, 1024, 1024), bf16), pltpu.VMEM((1024, 256), f32), pltpu.VMEM((1024, 128), f32),
            pltpu.VMEM((1024, 1024), f32), pltpu.VMEM((16, 1024), f32), pltpu.VMEM((8, 8, 512), f32),
            sem((17,)), sem((PIECES, 12)), sem((PIECES, 12)), sem((5,)), sem((5,)), sem((10,)), sem((2,))],
        compiler_params=pltpu.CompilerParams(collective_id=1, has_side_effects=True, vmem_limit_bytes=60 << 20),
        name="forward",
    )(tok, vec, qkv, out, up, down)


def mlp_kernel(actb, actbt, cot, hid, rows, upb, up_w, down_w, out_o, ghid_o, gbr_o, vr_o, ggd_o, ggu_o, total, gab, actc, gpre, down):
    j = pl.program_id(0)

    @pl.when(j == 0)
    def _():
        total[...] = jnp.zeros_like(total)
        gab[...] = jnp.zeros_like(gab)

    for d in range(4):
        for i in range(4):
            down[pl.ds(128 * d + 32 * i, 32), :] = down_w[i, d]
    bias_sum = jnp.zeros((1, 512), f32)
    for i in range(4):
        r = pl.ds(256 * i, 256)
        up = up_w[0].reshape(1024, 512)
        v = dot(actb[r, :], up, NN) + upb[0, 0:1, :]
        back = dot(cot[r, :], down[...], NT)
        cdf = 0.5 * (1.0 + lax.erf(v * 0.7071067811865476))
        slope = cdf + v * jnp.exp(-0.5 * v * v) * 0.3989422804014327
        c = (v * cdf).astype(bf16)
        g = (back * slope).astype(bf16)
        actc[r, :] = c
        gpre[r, :] = g
        bias_sum = bias_sum + jnp.sum(g.astype(f32), axis=0, keepdims=True)
        total[r, :] += dot(c, down[...], NN)
        gab[r, :] += dot(g, up, NT)
    vr_o[pl.ds(4 + j // 2, 1), pl.ds(pl.multiple_of((j % 2) * 512, 512), 512)] = bias_sum
    gd = dot(actc[...], cot[...], TN).astype(bf16)
    for d in range(4):
        for i in range(4):
            ggd_o[i, d] = gd[128 * d + 32 * i : 128 * d + 32 * i + 32]
    ggu_o[...] = dot(actbt[...], gpre[...], NN).astype(bf16).reshape(1, 32, 32, 512)

    @pl.when(j == pl.num_programs(0) - 1)
    def _():
        sums = [jnp.zeros((1, 1024), f32)] * 4
        for i in range(4):
            r = pl.ds(256 * i, 256)
            h = hid[r, :]
            out_o[r, :] = (h + total[r, :] + rows[5:6, :]).astype(bf16)
            centred, rstd = norm_stats(h)
            xhat = centred * rstd
            e = gab[r, :]
            eg = e * rows[3:4, :]
            back = rstd * (eg - jnp.mean(eg, axis=1, keepdims=True) - xhat * jnp.mean(eg * xhat, axis=1, keepdims=True))
            y = cot[r, :].astype(f32)
            gh = y + back
            ghid_o[r, :] = gh
            gb = gh.astype(bf16)
            gbr_o[r, :] = gb
            parts = (e * xhat, e, y, gb.astype(f32))
            sums = [s + jnp.sum(x, axis=0, keepdims=True) for s, x in zip(sums, parts)]
        for i in range(4):
            vr_o[i : i + 1, :] = sums[i]


def mlp_call(actb, actbt, cot, hid, rows, upb, gw):
    S = jax.ShapeDtypeStruct
    once = lambda shape: pl.BlockSpec(shape, lambda j: (0,) * len(shape), pipeline_mode=pl.Buffered(1))
    return pl.pallas_call(
        mlp_kernel,
        grid=(8,),
        out_shape=(
            S((1024, 1024), bf16), S((1024, 1024), f32), S((1024, 1024), bf16), S((8, 1024), f32),
            S((4, 32, 32, 1024), bf16), S((4, 32, 32, 1024), bf16)),
        in_specs=[
            once((1024, 1024)), once((1024, 1024)), once((1024, 1024)), once((1024, 1024)), once((16, 1024)),
            pl.BlockSpec((1, 8, 512), lambda j: (j, 0, 0)),
            pl.BlockSpec((1, 32, 32, 512), lambda j: (8 + j // 2, 0, 0, j % 2)),
            pl.BlockSpec((4, 4, 32, 1024), lambda j: (1, j, 0, 0))],
        out_specs=(
            pl.BlockSpec((1024, 1024), lambda j: (0, 0)), pl.BlockSpec((1024, 1024), lambda j: (0, 0)),
            pl.BlockSpec((1024, 1024), lambda j: (0, 0)), pl.BlockSpec((8, 1024), lambda j: (0, 0)),
            pl.BlockSpec((4, 4, 32, 1024), lambda j: (0, j, 0, 0)),
            pl.BlockSpec((1, 32, 32, 512), lambda j: (j // 2, 0, 0, j % 2))),
        scratch_shapes=[
            pltpu.VMEM((1024, 1024), f32), pltpu.VMEM((1024, 1024), f32), pltpu.VMEM((1024, 512), bf16),
            pltpu.VMEM((1024, 512), bf16), pltpu.VMEM((512, 1024), bf16)],
        compiler_params=pltpu.CompilerParams(vmem_limit_bytes=60 << 20),
        name="mlp",
    )(actb, actbt, cot, hid, rows, upb, gw, gw)


RC = 4
AC = 4


def backward_kernel(
    proj_h, actt_h, mixt_h, lse_h, gbr_h, ghid_h, tok_h, gw, ggd, ggu, rows_h, vr_h,
    gtok_o, gqkv_o, gout_o, gup_o, gdown_o, vec_o,
    acc, rc, r1, r2, r3, r4, fin, stag, dout, gp, qkv, tok, wide, actt, w, gaa, lse, rows, vsum, vrecv,
    lsem, accsem, ssem, rsem, credit, vssem, vrsem, fsem,
):
    b = device_bits()
    zh, zl, x, y, c = b
    ready = enter(b)
    loads = []

    def load(src, dst):
        cp = pltpu.make_async_copy(src, dst, lsem.at[len(loads)])
        cp.start()
        loads.append(cp)
        return cp

    rows_in = load(rows_h, rows)
    vr_in = load(vr_h, vsum.at[pl.ds(0, 8)])
    lse_in = load(lse_h, lse)
    gbr_in = load(gbr_h, tok)
    mixt_in = load(mixt_h, actt)
    ready()
    pend = {}
    fins = []

    def source(p):
        if p == 1:
            return stag.at[0]
        if p < 5:
            return ggd.at[max(p - 1, 0)]
        if p < 9:
            return ggu.at[p - 5]
        return stag.at[p % 2]

    def send(p, s, dim, src, dst):
        cp = pltpu.make_async_remote_copy(
            src_ref=src, dst_ref=dst, send_sem=ssem.at[p, s], recv_sem=rsem.at[p, s], device_id=flipped(b, dim), device_id_type=MESH)
        cp.start()
        pend[(p, s)] = cp

    def sent(p, s):
        pend[(p, s)].wait_send()
        pend.pop((p, s))

    recv = {}

    def got(p, s):
        recv[(p, s)].wait_recv()

    def final_places(p):
        if p == 1:
            return [(gout_o, 0, 1024)]
        if p < 5:
            return [(gdown_o.at[pl.ds(32 * max(p - 1, 0), 32)], 0, 1024)]
        if p < 9:
            return [(gup_o.at[:, pl.ds(1024 * (p - 5), 1024)], 0, 1024)]
        first, second = ((0, 1024), (2048, 512), (1536, 2560))[p - 9]
        return [(gqkv_o.at[:, pl.ds(first, 512)], 0, 512), (gqkv_o.at[:, pl.ds(second, 512)], 512, 512)]

    half = (pl.ds(0, 512), pl.ds(512, 512))

    def stage(p, r):
        a = acc.at[p % AC]
        if r == 0:
            if p >= RC:
                pl.semaphore_wait(credit, 1)
            if p >= AC:
                sent(p - AC, 1)
                sent(p - AC, 2)
            send(p, 0, 4, source(p).at[:, :, :, :, 1 - c], rc.at[p % RC])
            recv[(p, 0)] = pend[(p, 0)]
            cp = pltpu.make_async_copy(source(p).at[:, :, :, :, c], a, accsem.at[p])
            cp.start()
            recv[(p, "own")] = cp
        if r == 1:
            got(p, 0)
            recv[(p, "own")].wait()
            in_slot = rc.at[p % RC]

            def add(i, carry):
                k = (i // 8, (i // 4) % 2, (i // 2) % 2, i % 2)
                a[k] = a[k] + in_slot[k]
                return carry

            lax.fori_loop(0, 16, add, 0)
            if p + RC < PIECES:
                pl.semaphore_signal(credit, inc=1, device_id=flipped(b, 4), device_id_type=MESH)
            send(p, 1, 3, a.at[:, :, :, 1 - y, :, half[0]], r1.at[p, 0])
            send(p, 2, 2, a.at[:, :, 1 - x, :, :, half[1]], r1.at[p, 1])
            recv[(p, 1)], recv[(p, 2)] = pend[(p, 1)], pend[(p, 2)]
        if r == 2:
            for h in range(2):
                got(p, 1 + h)

                def add(i, carry, h=h):
                    k = (i // 4, (i // 2) % 2, i % 2)
                    full = (k[0], k[1], k[2], y) if h == 0 else (k[0], k[1], x, k[2])
                    r1[(p, h) + k] = r1[(p, h) + k] + a[full + (ALL, half[h])]
                    return carry

                lax.fori_loop(0, 8, add, 0)
                send(p, 3 + h, 1, r1.at[p, h, :, 1 - zl], r2.at[p, h])
                recv[(p, 3 + h)] = pend[(p, 3 + h)]
        if r == 3:
            for h in range(2):
                got(p, 3 + h)
                for i in range(2):
                    for j in range(2):
                        r2[p, h, i, j] = r2[p, h, i, j] + r1[p, h, i, zl, j]
                mine = (x, y)[h]
                send(p, 5 + h, 2 + h, r2.at[p, h, :, 1 - mine], r3.at[p, h])
                recv[(p, 5 + h)] = pend[(p, 5 + h)]
        if r == 4:
            for h in range(2):
                got(p, 5 + h)
                mine = (x, y)[h]
                for i in range(2):
                    r3[p, h, i] = r3[p, h, i] + r2[p, h, i, mine]
                send(p, 7 + h, 0, r3.at[p, h, 1 - zh], r4.at[p, h])
                recv[(p, 7 + h)] = pend[(p, 7 + h)]
        if r == 5:
            for h in range(2):
                got(p, 7 + h)
                fin[p, :, half[h]] = r3[p, h, zh].astype(f32) + r4[p, h].astype(f32)
            for dst, col, width in final_places(p):
                cp = pltpu.make_async_copy(fin.at[p, :, pl.ds(col, width)], dst, fsem.at[len(fins)])
                cp.start()
                fins.append(cp)

    issued = {}
    clock = [0]

    def tick(limit):
        for r in range(5, -1, -1):
            for p in range(PIECES):
                if issued.get((p, r)):
                    continue
                if r == 0:
                    if p < limit and (p == 0 or issued.get((p - 1, 0))) and not issued.get(("at", clock[0])):
                        stage(p, 0)
                        issued[(p, 0)] = clock[0] + 1
                        issued[("at", clock[0])] = True
                elif issued.get((p, r - 1)) and issued[(p, r - 1)] + LAG_B <= clock[0] + 1:
                    stage(p, r)
                    issued[(p, r)] = clock[0] + 1
        clock[0] += 1

    tick(1)

    def stage_store(slot, value, col):
        for i in range(4):
            stag[slot, i // 2, i % 2, :, :, :, :, pl.ds(col, 512)] = value(i).astype(bf16).reshape(2, 2, 2, 32, 512)

    def weight(p):
        cp = load(gw.at[p], w)
        return cp

    w_in = weight(3)
    gbr_in.wait()
    w_in.wait()
    for i in range(4):
        r = pl.ds(256 * i, 256)
        dout[r, :] = dot(tok[r, :], w[...].reshape(1024, 1024), NT).astype(bf16)
    mixt_in.wait()
    for col in (0, 512):
        stage_store(0, lambda i: dot(actt[pl.ds(256 * i, 256), :], tok[:, pl.ds(col, 512)], NN), col)
    actt_in = load(actt_h, actt)
    tok_in = load(tok_h, tok)
    tick(9)
    vr_in.wait()
    lse_in.wait()

    def half_piece(kind, upper):
        where = quarter(kind, 2 * upper)
        p, col = where // 4, (where % 4) * 256
        piece = 9 + p
        slot = piece % 2
        stage_store(slot, lambda i: dot(actt[pl.ds(256 * i, 256), :], gp[kind], NN), col)
        if kind != 1:
            vsum[8 + kind // 2 : 9 + kind // 2, pl.ds(512 * upper, 512)] = jnp.sum(gp[kind].astype(f32), axis=0, keepdims=True)
        for i in range(4):
            r = pl.ds(256 * i, 256)
            part = dot(gp[kind, r, :], w[:, :, :, :, :, :, pl.ds(col, 512)].reshape(1024, 512), NT)
            if kind == 0 and upper == 0:
                gaa[r, :] = part
            else:
                gaa[r, :] += part

    def attention_phase():
        dq, dk, dv = (wide.at[:, pl.ds(256 * i, 256)] for i in range(3))

        def fetch(group):
            return [load(proj_h.at[quarter(kind, group)], qkv.at[group % 2, kind]) for kind in range(3)]

        def back(group, first):
            q, k, v = (qkv.at[group % 2, kind] for kind in range(3))
            cols = pl.ds(256 * group, 256)

            def one(i, carry):
                head = first + i
                mask = head_mask(head, 1024)
                some = mask[:512]
                km = jnp.where(mask, k[...], bf16(0))
                lane = lax.broadcasted_iota(jnp.int32, (512, 128), 1)
                dkh, dvh = 0.0, 0.0
                for j in range(2):
                    r = pl.ds(512 * j, 512)
                    qm = jnp.where(some, q[r, :], bf16(0)) * bf16(0.125)
                    dom = jnp.where(some, dout[r, cols], bf16(0))
                    level = jnp.sum(jnp.where(lane == group * 4 + head, lse[r, :], 0.0), axis=1, keepdims=True)
                    p = jnp.exp(dot(qm, k[...], NT) - level)
                    dp = dot(dom, v[...], NT)
                    delta = jnp.sum(p * dp, axis=1, keepdims=True)
                    ds = (p * (dp - delta)).astype(bf16)
                    dvh = dvh + dot(p.astype(bf16), dom, TN)
                    dkh = dkh + dot(ds, qm, TN)
                    dq[r, :] = jnp.where(some, dot(ds, km, NN) * 0.125, dq[r, :])
                dk[...] = jnp.where(mask, dkh, dk[...])
                dv[...] = jnp.where(mask, dvh, dv[...])
                return carry

            lax.fori_loop(0, 2, one, 0)

        flights = {0: fetch(0)}
        for group in range(4):
            if group < 3:
                flights[group + 1] = fetch(group + 1)
            for cp in flights[group]:
                cp.wait()
            for first in (0, 2):
                back(group, first)
                tick(9 if group < 2 else 10)
            at = pl.ds(256 * (group % 2), 256)
            for kind, total in enumerate((dq, dk, dv)):
                gp[kind, :, at] = total[...].astype(bf16)
            if group % 2 == 1:
                upper = group // 2
                if upper == 0:
                    sent(1, 0)
                    actt_in.wait()
                    weight(0).wait()
                    half_piece(0, 0)
                    half_piece(1, 0)
                    tick(10)
                    weight(1).wait()
                    half_piece(2, 0)
                    tick(10)
                else:
                    ghid_in = load(ghid_h, wide)
                    half_piece(0, 1)
                    tick(11)
                    weight(2).wait()
                    sent(9, 0)
                    assert issued[(9, 1)]
                    half_piece(1, 1)
                    half_piece(2, 1)
                    tick(12)

        return ghid_in

    ghid_in = attention_phase()

    def last_phase():
        rows_in.wait()
        ghid_in.wait()
        tok_in.wait()
        sums = [jnp.zeros((1, 1024), f32)] * 2
        for i in range(4):
            r = pl.ds(256 * i, 256)
            centred, rstd = norm_stats(tok[r, :].astype(f32))
            xhat = centred * rstd
            e = gaa[r, :]
            eg = e * rows[0:1, :]
            back = rstd * (eg - jnp.mean(eg, axis=1, keepdims=True) - xhat * jnp.mean(eg * xhat, axis=1, keepdims=True))
            tok[r, :] = (wide[r, :] + back).astype(bf16)
            sums = [s + jnp.sum(v, axis=0, keepdims=True) for s, v in zip(sums, (e * xhat, e))]
        tok_out = load(tok, gtok_o)
        vsum[10:11, :] = sums[0]
        vsum[11:12, :] = sums[1]
        vsum[12:16, :] = jnp.zeros((4, 1024), f32)
        tick(12)
        for i, dim in enumerate((4, 3, 1, 2, 0)):
            cp = pltpu.make_async_remote_copy(
                src_ref=vsum, dst_ref=vrecv.at[i], send_sem=vssem.at[i], recv_sem=vrsem.at[i], device_id=flipped(b, dim),
                device_id_type=MESH)
            cp.start()
            tick(12)
            cp.wait()
            vsum[...] = vsum[...] + vrecv[i]
        own = ((zh * 2 + zl) * 2 + x) * 4 + y * 2 + c
        n = lax.broadcasted_iota(jnp.int32, (1024, 128), 0)
        j = lax.broadcasted_iota(jnp.int32, (1024, 128), 1)

        def cut(value, base):
            pick = jnp.where(n == base + j, 1.0, 0.0)
            return lax.dot_general(value, pick, NN, precision=lax.Precision.HIGHEST, preferred_element_type=f32)

        narrow = cut(vsum[...], 32 * own)
        middle = cut(vsum[8:16, :], 64 * (own % 16))
        broad = cut(vsum[0:8, :], 128 * (own % 8))
        for i, at in enumerate((10, 11, 3, 0, 1, 2)):
            vec_o[i : i + 1, :] = narrow[at : at + 1]
        vec_o[6:7, :] = jnp.where(own < 16, middle[0:1], middle[1:2])
        up = broad[4:5]
        for i in range(1, 4):
            up = jnp.where(own // 8 == i, broad[4 + i : 5 + i], up)
        vec_o[7:8, :] = up
        while not issued.get((PIECES - 1, 5)):
            tick(12)
        tok_out.wait()

    last_phase()
    for cp in pend.values():
        cp.wait_send()
    for cp in fins:
        cp.wait()


def backward_call(proj, actt, mixt, lse, gbr, ghid, tok, gw, ggd, ggu, rows, vr):
    S = jax.ShapeDtypeStruct
    V = pltpu.VMEM
    sem = pltpu.SemaphoreType.DMA
    big = (2, 2, 2, 2, 2, 32, 1024)
    n = PIECES
    return pl.pallas_call(
        backward_kernel,
        out_shape=(
            S((1024, 1024), bf16), S((32, 3072), f32), S((32, 1024), f32), S((32, 4096), f32), S((128, 1024), f32), S((8, 128), f32)),
        in_specs=[HBM] * 12,
        out_specs=(HBM,) * 5 + (pl.BlockSpec(memory_space=pltpu.VMEM),),
        scratch_shapes=[
            V((AC, 2, 2, 2, 2, 32, 1024), bf16), V((RC, 2, 2, 2, 2, 32, 1024), bf16), V((n, 2, 2, 2, 2, 32, 512), bf16),
            V((n, 2, 2, 2, 32, 512), bf16), V((n, 2, 2, 32, 512), bf16), V((n, 2, 32, 512), bf16), V((n, 32, 1024), f32),
            V((2,) + big, bf16), V((1024, 1024), bf16), V((3, 1024, 512), bf16), V((2, 3, 1024, 256), bf16),
            V((1024, 1024), bf16), V((1024, 1024), f32), V((1024, 1024), bf16), V(big, bf16),
            V((1024, 1024), f32), V((1024, 128), f32), V((16, 1024), f32), V((16, 1024), f32), V((5, 16, 1024), f32),
            sem((40,)), sem((n,)), sem((n, 9)), sem((n, 9)), pltpu.SemaphoreType.REGULAR, sem((5,)), sem((5,)), sem((16,))],
        compiler_params=pltpu.CompilerParams(collective_id=2, has_side_effects=True, vmem_limit_bytes=63 << 20),
        name="backward",
    )(proj, actt, mixt, lse, gbr, ghid, tok, gw, ggd, ggu, rows, vr)


def layer(
    tokens, attn_gain, attn_shift, qkv_weight, qv_bias, out_weight, out_bias, mlp_gain, mlp_shift, up_weight, up_bias, down_weight,
    down_bias, cotangent,
):
    vec = jnp.concatenate([attn_gain, attn_shift, out_bias, mlp_gain, mlp_shift, down_bias, qv_bias, up_bias]).astype(f32)
    vec = jnp.pad(vec.reshape(3, 128), ((0, 5), (0, 0)))
    gw, rows, upb, actt, proj, mixt, lse, hid, actb, actbt = forward_call(tokens, vec, qkv_weight, out_weight, up_weight, down_weight)
    output, ghid, gbr, vr, ggd, ggu = mlp_call(actb, actbt, cotangent, hid, rows, upb, gw.reshape(PIECES, 32, 32, 1024))
    big = (4, 2, 2, 2, 2, 2, 32, 1024)
    gtok, gqkv, gout, gup, gdown, gvec = backward_call(
        proj, actt, mixt, lse, gbr, ghid, tokens, gw, ggd.reshape(big), ggu.reshape(big), rows, vr)
    return (
        output, gtok, gvec[0, :32], gvec[1, :32], gqkv, gvec[6, :64], gout, gvec[2, :32], gvec[3, :32], gvec[4, :32], gup, gvec[7],
        gdown, gvec[5, :32])


def layer_norm(values_in, gain_vec, bias_vec):
    row_mean = jnp.mean(values_in, axis=-1, keepdims=True)
    centred = values_in - row_mean
    spread = jnp.mean(centred * centred, axis=-1, keepdims=True)
    return centred * lax.rsqrt(spread + epsilon) * gain_vec + bias_vec


def gelu_exact(values_in):
    return jax.nn.gelu(values_in, approximate=False)


def norm_backward(values_in, gain_vec, incoming):
    zero_shift = jnp.zeros_like(gain_vec)
    unused, pull_back = jax.vjp(layer_norm, values_in, gain_vec, zero_shift)
    return pull_back(incoming)


def general_layer(
    tokens,
    attn_gain,
    attn_shift,
    qkv_weight,
    qv_bias,
    out_weight,
    out_bias,
    mlp_gain,
    mlp_shift,
    up_weight,
    up_bias,
    down_weight,
    down_bias,
    cotangent,
):
    length, model_width = tokens.shape
    score_scale = HD ** (-0.5)
    gain_a, shift_a, qkv_full, qv_full, out_full, out_bias_full = (
        lax.all_gather(attn_gain, ("wide", "narrow"), axis=0, tiled=True),
        lax.all_gather(attn_shift, ("wide", "narrow"), axis=0, tiled=True),
        lax.all_gather(qkv_weight, ("wide", "narrow"), axis=0, tiled=True),
        lax.all_gather(qv_bias, ("wide", "narrow"), axis=0, tiled=True),
        lax.all_gather(out_weight, ("wide", "narrow"), axis=0, tiled=True),
        lax.all_gather(out_bias, ("wide", "narrow"), axis=0, tiled=True),
    )
    inputs = tokens.astype(jnp.float32)
    act_a = layer_norm(inputs, gain_a.astype(jnp.float32), shift_a.astype(jnp.float32)).astype(
        jnp.bfloat16
    )
    bias_full = jnp.concatenate(
        [qv_full[:model_width], jnp.zeros((model_width,), jnp.bfloat16), qv_full[model_width:]]
    ).astype(jnp.float32)
    projected = (jnp.dot(act_a, qkv_full, preferred_element_type=jnp.float32) + bias_full).astype(
        jnp.bfloat16
    )
    query_rows = projected[:, :model_width].reshape(length, H, HD)
    key_rows = projected[:, model_width : 2 * model_width].reshape(length, H, HD)
    value_rows = projected[:, 2 * model_width :].reshape(length, H, HD)
    block_rows = min(512, length)
    block_count = length // block_rows
    query_blocks = query_rows.reshape(block_count, block_rows, H, HD)

    def attend_block(query_block):
        scores = (
            jnp.einsum("qhe,khe->hqk", query_block, key_rows, preferred_element_type=jnp.float32)
            * score_scale
        )
        row_max = jnp.max(scores, axis=-1, keepdims=True)
        exp_scores = jnp.exp(scores - row_max)
        denominator = jnp.sum(exp_scores, axis=-1, keepdims=True)
        low_probs = (exp_scores / denominator).astype(jnp.bfloat16)
        mixed_block = jnp.einsum(
            "hqk,khe->qhe", low_probs, value_rows, preferred_element_type=jnp.float32
        )
        return (mixed_block, (row_max + jnp.log(denominator))[..., 0])

    mixed_blocks, log_sums = lax.map(attend_block, query_blocks)
    mixed = mixed_blocks.reshape(length, model_width).astype(jnp.bfloat16)
    hidden = (
        inputs
        + jnp.dot(mixed, out_full, preferred_element_type=jnp.float32)
        + out_bias_full.astype(jnp.float32)
    )
    gain_b, shift_b, up_full, up_bias_full, down_full, down_bias_full = (
        lax.all_gather(mlp_gain, ("wide", "narrow"), axis=0, tiled=True),
        lax.all_gather(mlp_shift, ("wide", "narrow"), axis=0, tiled=True),
        lax.all_gather(up_weight, ("wide", "narrow"), axis=0, tiled=True),
        lax.all_gather(up_bias, ("wide", "narrow"), axis=0, tiled=True),
        lax.all_gather(down_weight, ("wide", "narrow"), axis=0, tiled=True),
        lax.all_gather(down_bias, ("wide", "narrow"), axis=0, tiled=True),
    )
    act_b = layer_norm(hidden, gain_b.astype(jnp.float32), shift_b.astype(jnp.float32)).astype(
        jnp.bfloat16
    )
    pre_up = jnp.dot(act_b, up_full, preferred_element_type=jnp.float32) + up_bias_full.astype(
        jnp.float32
    )
    act_c = gelu_exact(pre_up).astype(jnp.bfloat16)
    output = (
        hidden
        + jnp.dot(act_c, down_full, preferred_element_type=jnp.float32)
        + down_bias_full.astype(jnp.float32)
    ).astype(jnp.bfloat16)
    gain_b_back, up_back, down_back = (
        lax.all_gather(mlp_gain, ("wide", "narrow"), axis=0, tiled=True),
        lax.all_gather(up_weight, ("wide", "narrow"), axis=0, tiled=True),
        lax.all_gather(down_weight, ("wide", "narrow"), axis=0, tiled=True),
    )
    grad_y = cotangent.astype(jnp.float32)
    grad_down_weight = jnp.einsum("sf,sd->fd", act_c, cotangent, preferred_element_type=jnp.float32)
    grad_down_bias = jnp.sum(cotangent.astype(jnp.float32), axis=0)
    grad_act = jnp.einsum("sd,fd->sf", cotangent, down_back, preferred_element_type=jnp.float32)
    unused_gelu, gelu_pull = jax.vjp(gelu_exact, pre_up)
    grad_pre = gelu_pull(grad_act)[0].astype(jnp.bfloat16)
    grad_up_weight = jnp.einsum("sd,sf->df", act_b, grad_pre, preferred_element_type=jnp.float32)
    grad_up_bias = jnp.sum(grad_pre.astype(jnp.float32), axis=0)
    grad_act_b = jnp.einsum("sf,df->sd", grad_pre, up_back, preferred_element_type=jnp.float32)
    hidden_part, grad_mlp_gain, grad_mlp_shift = norm_backward(
        hidden, gain_b_back.astype(jnp.float32), grad_act_b
    )
    grad_hidden = grad_y + hidden_part
    mlp_sums = (
        lax.psum_scatter(grad_mlp_gain, ("wide", "narrow"), scatter_dimension=0, tiled=True),
        lax.psum_scatter(grad_mlp_shift, ("wide", "narrow"), scatter_dimension=0, tiled=True),
        lax.psum_scatter(grad_up_weight, ("wide", "narrow"), scatter_dimension=0, tiled=True),
        lax.psum_scatter(grad_up_bias, ("wide", "narrow"), scatter_dimension=0, tiled=True),
        lax.psum_scatter(grad_down_weight, ("wide", "narrow"), scatter_dimension=0, tiled=True),
        lax.psum_scatter(grad_down_bias, ("wide", "narrow"), scatter_dimension=0, tiled=True),
    )
    gain_a_back, qkv_back, out_back = (
        lax.all_gather(attn_gain, ("wide", "narrow"), axis=0, tiled=True),
        lax.all_gather(qkv_weight, ("wide", "narrow"), axis=0, tiled=True),
        lax.all_gather(out_weight, ("wide", "narrow"), axis=0, tiled=True),
    )
    grad_branch = grad_hidden.astype(jnp.bfloat16)
    grad_out_weight = jnp.einsum(
        "sa,sd->ad", mixed, grad_branch, preferred_element_type=jnp.float32
    )
    grad_out_bias = jnp.sum(grad_branch.astype(jnp.float32), axis=0)
    grad_mixed = jnp.einsum(
        "sd,ad->sa", grad_branch, out_back, preferred_element_type=jnp.float32
    ).astype(jnp.bfloat16)
    grad_blocks = grad_mixed.reshape(block_count, block_rows, H, HD)

    def back_block(carry, block_inputs):
        key_total, value_total = carry
        query_block, grad_block, log_block = block_inputs
        scores = (
            jnp.einsum("qhe,khe->hqk", query_block, key_rows, preferred_element_type=jnp.float32)
            * score_scale
        )
        attn_probs = jnp.exp(scores - log_block[..., None])
        grad_probs = jnp.einsum(
            "qhe,khe->hqk", grad_block, value_rows, preferred_element_type=jnp.float32
        )
        row_delta = jnp.sum(grad_probs * attn_probs, axis=-1, keepdims=True)
        grad_scores = (attn_probs * (grad_probs - row_delta)).astype(jnp.bfloat16)
        low_probs = attn_probs.astype(jnp.bfloat16)
        value_total = value_total + jnp.einsum(
            "hqk,qhe->khe", low_probs, grad_block, preferred_element_type=jnp.float32
        )
        key_total = (
            key_total
            + jnp.einsum(
                "hqk,qhe->khe", grad_scores, query_block, preferred_element_type=jnp.float32
            )
            * score_scale
        )
        grad_query = (
            jnp.einsum("hqk,khe->qhe", grad_scores, key_rows, preferred_element_type=jnp.float32)
            * score_scale
        )
        return ((key_total, value_total), grad_query)

    zero_heads = jnp.zeros((length, H, HD), jnp.float32)
    (grad_key, grad_value), grad_query = lax.scan(
        back_block, (zero_heads, zero_heads), (query_blocks, grad_blocks, log_sums)
    )
    grad_projected = jnp.concatenate(
        [
            grad_query.reshape(length, model_width),
            grad_key.reshape(length, model_width),
            grad_value.reshape(length, model_width),
        ],
        axis=1,
    ).astype(jnp.bfloat16)
    grad_qkv_weight = jnp.einsum(
        "sa,sb->ab", act_a, grad_projected, preferred_element_type=jnp.float32
    )
    column_sums = jnp.sum(grad_projected.astype(jnp.float32), axis=0)
    grad_qv_bias = jnp.concatenate([column_sums[:model_width], column_sums[2 * model_width :]])
    grad_act_a = jnp.einsum(
        "sb,ab->sa", grad_projected, qkv_back, preferred_element_type=jnp.float32
    )
    input_part, grad_attn_gain, grad_attn_shift = norm_backward(
        inputs, gain_a_back.astype(jnp.float32), grad_act_a
    )
    grad_tokens = (grad_hidden + input_part).astype(jnp.bfloat16)
    attn_sums = (
        lax.psum_scatter(grad_attn_gain, ("wide", "narrow"), scatter_dimension=0, tiled=True),
        lax.psum_scatter(grad_attn_shift, ("wide", "narrow"), scatter_dimension=0, tiled=True),
        lax.psum_scatter(grad_qkv_weight, ("wide", "narrow"), scatter_dimension=0, tiled=True),
        lax.psum_scatter(grad_qv_bias, ("wide", "narrow"), scatter_dimension=0, tiled=True),
        lax.psum_scatter(grad_out_weight, ("wide", "narrow"), scatter_dimension=0, tiled=True),
        lax.psum_scatter(grad_out_bias, ("wide", "narrow"), scatter_dimension=0, tiled=True),
    )
    return (
        output,
        grad_tokens,
        attn_sums[0],
        attn_sums[1],
        attn_sums[2],
        attn_sums[3],
        attn_sums[4],
        attn_sums[5],
        mlp_sums[0],
        mlp_sums[1],
        mlp_sums[2],
        mlp_sums[3],
        mlp_sums[4],
        mlp_sums[5],
    )


def solution(mesh):
    placed = (
        P(("wide", "narrow"), None),
        P(("wide", "narrow")),
        P(("wide", "narrow")),
        P(("wide", "narrow"), None),
        P(("wide", "narrow")),
        P(("wide", "narrow"), None),
        P(("wide", "narrow")),
        P(("wide", "narrow")),
        P(("wide", "narrow")),
        P(("wide", "narrow"), None),
        P(("wide", "narrow")),
        P(("wide", "narrow"), None),
        P(("wide", "narrow")),
        P(("wide", "narrow"), None),
    )
    return jax.shard_map(
        layer if dict(mesh.shape) == {"wide": 8, "narrow": 4} else general_layer,
        mesh=mesh,
        in_specs=placed,
        out_specs=(
            P(("wide", "narrow"), None),
            P(("wide", "narrow"), None),
            P(("wide", "narrow")),
            P(("wide", "narrow")),
            P(("wide", "narrow"), None),
            P(("wide", "narrow")),
            P(("wide", "narrow"), None),
            P(("wide", "narrow")),
            P(("wide", "narrow")),
            P(("wide", "narrow")),
            P(("wide", "narrow"), None),
            P(("wide", "narrow")),
            P(("wide", "narrow"), None),
            P(("wide", "narrow")),
        ),
        check_vma=False,
    )
```

```python
import functools
import jax
import jax.numpy as jnp
from jax import lax
from jax.experimental import pallas as pl
from jax.experimental.pallas import tpu as pltpu
from jax.sharding import PartitionSpec as P

H = 16
HD = 64
epsilon = 1e-05
bf16 = jnp.bfloat16
f32 = jnp.float32
NN = (((1,), (0,)), ((), ()))
NT = (((1,), (1,)), ((), ()))
TN = (((0,), (0,)), ((), ()))
ALL = slice(None)
MESH = pl.DeviceIdType.MESH
HBM = pl.BlockSpec(memory_space=pltpu.HBM)
VMEM = pl.BlockSpec(memory_space=pltpu.VMEM)

ORDERS = ((0, 2, 1, 3), (0, 3, 1, 2))
PIECES = 13
GATHER_START = (0, 0, 0, 0, 15, 15, 17, 20, 24, 28, 34, 40, 47)
GATHER_LAG = (7, 7, 9, 9)
SCATTER_LAG = (4, 8, 10, 5, 6)
SCATTER_GAP = 7
SLOTS = 3
MAIL = 2
RING = 5
TURNS = 8


def dot(a, b, dims):
    return lax.dot_general(a, b, dims, preferred_element_type=f32)


def device_bits():
    w = lax.axis_index("wide")
    n = lax.axis_index("narrow")
    return (w // 4, (w // 2) % 2, w % 2, n // 2, n % 2)


def flipped(b, *dims):
    t = tuple(1 - v if i in dims else v for i, v in enumerate(b))
    return (t[0] * 4 + t[1] * 2 + t[2], t[3] * 2 + t[4])


def head_mask(head, rows):
    return lax.shift_right_logical(lax.broadcasted_iota(jnp.int32, (rows, 256), 1), 6) == head


def norm_stats(v):
    mean = jnp.mean(v, axis=1, keepdims=True)
    centred = v - mean
    rstd = lax.rsqrt(jnp.mean(centred * centred, axis=1, keepdims=True) + epsilon)
    return centred, rstd


def norm_grad(centred, rstd, gain, e):
    xhat = centred * rstd
    eg = e * gain
    return rstd * (eg - jnp.mean(eg, axis=1, keepdims=True) - xhat * jnp.mean(eg * xhat, axis=1, keepdims=True)), xhat


def column_sum(v):
    return jnp.sum(v, axis=0, keepdims=True)


def block_pick(i, transposed):
    shape = (128, 512) if transposed else (512, 128)
    unit = lax.broadcasted_iota(jnp.int32, shape, 1 if transposed else 0)
    lane = lax.broadcasted_iota(jnp.int32, shape, 0 if transposed else 1)
    return jnp.where(unit == 128 * lax.shift_right_logical(lane, 5) + 32 * i + (lane & 31), 1.0, 0.0)


def layer_kernel(
    tok_h, cot_h, qkv_h, out_h, up_h, down_h, again_v, ashift_v, obias_v, mgain_v, mshift_v, dbias_v, qvbias_v, ubias_v,
    out_o, gtok_o, gqkv_o, gout_o, gup_o, gdown_o, vec_o, gw, spill,
    gv, rows, level, delta, qkv, pb, pf, w, gup, vsum, vrecv,
    stag, mail, r1, r2, r3, r4, fin,
    insem, ownsem, wsem, spsem, outsem, ssem, rsem, vssem, vrsem, bssem, brsem, credit, ussem, ursem, finsem,
):
    b = device_bits()
    zh, zl, x, y, c = b
    barrier = pltpu.get_barrier_semaphore()
    partners = ((0,), (1,), (2,), (3,), (4,), (2, 3), (0, 1))
    for dims in partners:
        pl.semaphore_signal(barrier, inc=1, device_id=flipped(b, *dims), device_id_type=MESH)

    def copy(src, dst, sem):
        cp = pltpu.make_async_copy(src, dst, sem)
        cp.start()
        return cp

    def remote(src, dst, send_sem, recv_sem, *dims):
        cp = pltpu.make_async_remote_copy(
            src_ref=src, dst_ref=dst, send_sem=send_sem, recv_sem=recv_sem, device_id=flipped(b, *dims), device_id_type=MESH)
        cp.start()
        return cp

    def rows_at(i):
        return pl.ds(pl.multiple_of(i * 256, 256), 256)

    quarter_rows = [pl.ds(256 * i, 256) for i in range(4)]
    act, mixed, trans, gbr, dout = (pb.at[i] for i in range(5))
    tok = dout
    hid, total, gab = (pf.at[i] for i in range(3))
    lse = hid.at[:, pl.ds(0, 128)]

    shards = [gbr.at[pl.ds(32 * p, 32), pl.ds(0, 768 if p < 4 else 1024)] for p in range(9)]
    for g in range(4):
        for t in range(3):
            copy(qkv_h.at[:, pl.ds(1024 * t + 256 * g, 256)], gbr.at[pl.ds(32 * g, 32), pl.ds(256 * t, 256)], ownsem.at[g])
    copy(out_h, shards[4], ownsem.at[4])
    for i in range(4):
        copy(down_h.at[pl.ds(32 * i, 32)], shards[5 + i], ownsem.at[5 + 2 * i])
    shards[5:] = [shards[5], w.at[2, 0, 0, 0, 0, 0], shards[6], w.at[2, 0, 0, 0, 0, 1], shards[7], w.at[2, 0, 0, 0, 1, 0], shards[8], w.at[2, 0, 0, 0, 1, 1]]
    own = {}
    for i in range(4):
        copy(up_h.at[:, pl.ds(1024 * i, 1024)], mixed.at[pl.ds(32 * i, 32)], insem.at[0])
    pl.semaphore_wait(barrier, len(partners))
    sent = {}
    arrived = set()

    def store_own(p):
        if p not in own:
            if p < 5 or p % 2 == 1:
                pltpu.make_async_copy(shards[p], shards[p], ownsem.at[p]).wait()
            own[p] = copy(shards[p], gw.at[(p,) + b + (ALL, pl.ds(0, 768 if p < 4 else 1024))], ownsem.at[p])

    def own_stored(p):
        if own[p] is not None:
            own[p].wait()
            own[p] = None

    def gather_stage(p, r):
        half = 384 if p < 4 else 512
        if r == 0:
            store_own(p)
        if r == (1 if p < 2 else 0):
            own_stored(p)
        for h in range(2):
            order = ORDERS[h]
            cols = (ALL, pl.ds(h * half, half))

            def send(dim, sub, s):
                ref = gw.at[(p,) + sub + cols]
                src = shards[p].at[:, pl.ds(h * half, half)] if r == 0 and p < 2 else ref
                sent[(p, s)] = remote(src, ref, ssem.at[p], rsem.at[p % TURNS, s], dim)

            if r > 0:
                sent[(p, h * 4 + r - 1)].wait_recv()
            held = tuple(ALL if i in order[:r] else b[i] for i in range(5))
            if r < 4:
                send(order[r], held, h * 4 + r)
            if r == 3:
                send(4, held, 8)
            if r == 4:
                late = tuple(ALL if i in order[:3] else (1 - b[i] if i == order[3] else b[i]) for i in range(5))
                send(4, late, 8)

    now = [0.0]
    gathers = [[] for _ in range(PIECES)]
    scatters = [[] for _ in range(PIECES)]
    ready = [0]

    def due(issued, lags, share):
        return now[0] >= issued[-1] + share * lags[len(issued) - 1]

    def tick(spent):
        now[0] += spent
        for p, issued in enumerate(gathers):
            while len(issued) < 5 and (due(issued, GATHER_LAG, 0.75 if p < 4 else 1.1 if p < 7 else 1.3) if issued else now[0] >= GATHER_START[p]):
                gather_stage(p, len(issued))
                issued.append(now[0])
        for p, issued in enumerate(scatters[: ready[0]]):
            if not issued and p > 0 and now[0] < scatters[p - 1][0] + SCATTER_GAP and p < PIECES - 1:
                break
            while len(issued) < 6 and (not issued or due(issued, SCATTER_LAG, 0.5 if p >= 11 else 0.75 if p >= 9 else 1)):
                scatter_stage(p, len(issued))
                issued.append(now[0])

    def gather_up_to(stages):
        now[0] += 2.5
        for p, r in stages:
            gather_stage(p, r)
            gathers[p].append(now[0])

    def arrive(p):
        while len(gathers[p]) < 5:
            gather_stage(p, len(gathers[p]))
            gathers[p].append(now[0])
        if p not in arrived:
            half = spill.at[0, pl.ds(0, 512), pl.ds(0, 768 if p < 4 else 1024)]
            pltpu.make_async_copy(half, half, rsem.at[p % TURNS, 8]).wait()
            arrived.add(p)

    def all_sent(p):
        rest = spill.at[0, pl.ds(0, 992), pl.ds(0, 768 if p < 4 else 1024)]
        pltpu.make_async_copy(rest, rest, ssem.at[p]).wait()

    flights = {}

    def fetch(p, slot):
        arrive(p)
        flights[slot] = copy(gw.at[p], w.at[slot], wsem.at[slot])

    def weight(slot, cols=1024):
        return w[slot, :, :, :, :, :, :, pl.ds(0, cols)].reshape(1024, cols)

    def weight_rows(slot, i):
        return w[slot, i // 2, i % 2].reshape(256, 1024)

    vec_order = (0, 2, 1, 3, 4)
    vec_sent = []

    def vec_round(r):
        if r > 0:
            vec_sent[r - 1].wait_recv()
        if r < 5:
            ref = gv.at[tuple(ALL if i in vec_order[:r] else b[i] for i in range(5))]
            vec_sent.append(remote(ref, ref, vssem.at[r], vrsem.at[r], vec_order[r]))

    gather_up_to([(0, 0)])
    tok_in = copy(tok_h, tok, insem.at[1])
    lines = [jnp.zeros((1, 128), f32)] * 3
    for n, (vector, line, offset) in enumerate((
        (again_v, 0, 0), (ashift_v, 0, 32), (obias_v, 0, 64), (mgain_v, 0, 96), (mshift_v, 1, 0), (dbias_v, 1, 32), (qvbias_v, 1, 64),
        (ubias_v, 2, 0),
    )):
        size = vector.shape[0]
        at = lax.broadcasted_iota(jnp.int32, (size, 128), 0)
        lane = lax.broadcasted_iota(jnp.int32, (size, 128), 1)
        put = jnp.where(lane == at + offset, 1.0, 0.0).astype(bf16)
        lines[line] = lines[line] + dot(vector[...].astype(f32).reshape(1, size).astype(bf16), put, NN)
    gv[b] = jnp.concatenate(lines + [jnp.zeros((5, 128), f32)], axis=0)
    vec_round(0)
    up_shard = mixed.at[pl.ds(0, 128)]
    pltpu.make_async_copy(up_shard, up_shard, insem.at[0]).wait()
    for i in range(4):
        pick = block_pick(i, False).astype(bf16)
        for g in range(8):
            shards[6 + 2 * i][:, 128 * g : 128 * g + 128] = dot(
                mixed[32 * (g // 2) : 32 * (g // 2) + 32, 512 * (g % 2) : 512 * (g % 2) + 512], pick, NN).astype(bf16)
    for p in range(PIECES):
        store_own(p)
    gather_up_to([(0, 1), (1, 0)])
    vec_round(1)
    gather_up_to([(0, 2), (1, 1), (2, 0)])
    vec_round(2)
    gather_up_to([(0, 3), (1, 2), (2, 1), (3, 0)])
    vec_round(3)
    vec_round(4)
    gather_up_to([(0, 4), (1, 3), (2, 2), (3, 1)])
    vec_round(5)

    table = gv[...].reshape(32, 8, 128)
    sub_index = lax.broadcasted_iota(jnp.int32, (32, 8, 128), 1)
    lines = [jnp.sum(jnp.where(sub_index == r, table, 0.0), axis=1) for r in range(3)]

    def spread(line, offset, log, base):
        j = lax.broadcasted_iota(jnp.int32, (128, 1024), 0)
        n = lax.broadcasted_iota(jnp.int32, (128, 1024), 1)
        pick = jnp.where(j == offset + (n & ((1 << log) - 1)), 1.0, 0.0).astype(bf16)
        broad = dot(line.astype(bf16), pick, NN)
        d = lax.broadcasted_iota(jnp.int32, (32, 1024), 0)
        n = lax.broadcasted_iota(jnp.int32, (32, 1024), 1)
        return column_sum(jnp.where(d == base + lax.shift_right_logical(n, log), broad, 0.0))

    places = [(0, 0, 5, 0), (0, 32, 5, 0), (0, 64, 5, 0), (0, 96, 5, 0), (1, 0, 5, 0), (1, 32, 5, 0), (1, 64, 6, 0), (1, 64, 6, 16)]
    places += [(2, 32 * i, 5, 0) for i in range(4)]
    for i, (line, offset, log, base) in enumerate(places):
        rows[i : i + 1, :] = spread(lines[line], offset, log, base)

    tok_in.wait()

    def first_norm(i, carry):
        r = rows_at(i)
        centred, rstd = norm_stats(tok[r, :].astype(f32))
        a = (centred * rstd * rows[0:1, :] + rows[1:2, :]).astype(bf16)
        act[r, :] = a
        trans[:, r] = a.T
        return carry

    lax.fori_loop(0, 4, first_norm, 0)
    act_out = copy(trans, spill.at[0], spsem.at[0])
    for p in range(PIECES):
        own_stored(p)
    lse[...] = jnp.zeros_like(lse)

    def project(g, slot):
        at = pl.ds(256 * g, 256)
        bias = jnp.concatenate([rows[6:7, at], jnp.zeros((1, 256), f32), rows[7:8, at]], axis=1)

        def block(i, carry):
            r = rows_at(i)
            qkv[g, r, :] = (dot(act[r, :], weight(slot, 768), NN) + bias).astype(bf16)
            return carry

        lax.fori_loop(0, 4, block, 0)

    def attend(g, first):
        q, k, v = (qkv.at[g, :, pl.ds(256 * i, 256)] for i in range(3))

        def one(i, carry):
            head = first + i
            mask = head_mask(head, 1024)
            some = mask[:256]
            lane = lax.broadcasted_iota(jnp.int32, (256, 128), 1)
            vm = jnp.where(mask, v[...], bf16(1))

            def score(r):
                return dot(jnp.where(some, q[r, :], bf16(0)) * bf16(0.125), k[...], NT)

            def soft(s):
                m = jnp.max(s, axis=1, keepdims=True)
                return jnp.exp(s - m).astype(bf16), m

            def mix(r, p, m):
                o = dot(p, vm, NN)
                sums = pltpu.roll(o, 64, axis=1)
                gab[r, 0:256] = jnp.where(some, o / sums, gab[r, 0:256])
                level = m + jnp.log(jnp.max(jnp.where(some, sums, 0.0), axis=1, keepdims=True))
                lse[r, :] = jnp.where(lane == g * 4 + head, level, lse[r, :])

            s = score(quarter_rows[0])
            last = None
            for j, r in enumerate(quarter_rows):
                later = score(quarter_rows[j + 1]) if j < 3 else None
                p = soft(s)
                if last is not None:
                    mix(quarter_rows[j - 1], *last)
                last, s = p, later
            mix(quarter_rows[3], *last)
            return carry

        lax.fori_loop(0, 2, one, 0)

    now[0] = max(now[0], 15.0)
    tick(0)
    fetch(0, 0)
    for g in range(4):
        flights[g % 2].wait()
        project(g, g % 2)
        tick(2.3)
        attend(g, 0)
        tick(3.6)
        fetch(g + 1, (g + 1) % 2 if g < 3 else 2)
        attend(g, 2)
        tick(3.6)
        mixed[:, 256 * g : 256 * g + 256] = gab[:, 0:256].astype(bf16)
    act_out.wait()
    flights[2].wait()

    level[...] = lse[...].T
    all_sent(0)
    all_sent(1)

    def second_norm(i, carry):
        r = rows_at(i)
        v = tok[r, :].astype(f32) + dot(mixed[r, :], weight(2), NN) + rows[2:3, :]
        hid[r, :] = v
        centred, rstd = norm_stats(v)
        a = (centred * rstd * rows[3:4, :] + rows[4:5, :]).astype(bf16)
        act[r, :] = a
        trans[:, r] = a.T
        gbr[:, r] = mixed[r, :].T
        return carry

    lax.fori_loop(0, 4, second_norm, 0)
    mix_out = copy(gbr, spill.at[1], spsem.at[1])
    tick(4.5)
    cot = mixed
    cot_in = copy(cot_h, cot, insem.at[2])

    got = {}
    fins = {}

    def half_of(p):
        return 384 if p >= 9 else 512

    def scatter_stage(p, r):
        half = half_of(p)
        a = stag.at[p % SLOTS, 0]
        k = p % RING
        lanes = pl.ds(0, half)
        sides = (pl.ds(0, half), pl.ds(half, half))

        def send(s, dim, src, dst):
            got[(p, s)] = remote(src, dst, bssem.at[k, s], brsem.at[k, s], dim)

        if r == 0:
            if p >= MAIL:
                pl.semaphore_wait(credit, 1)
            full = (ALL, ALL, ALL, ALL, ALL, pl.ds(0, 2 * half))
            send(0, 4, stag.at[(p % SLOTS, 1) + full], mail.at[(p % MAIL,) + full])
        if r == 1:
            got[(p, 0)].wait_recv()

            def add(i, carry):
                at = (i // 8, (i // 4) % 2, (i // 2) % 2, i % 2, ALL, pl.ds(0, 2 * half))
                a[at] = a[at] + mail[(p % MAIL,) + at]
                return carry

            lax.fori_loop(0, 16, add, 0)
            if p + MAIL < PIECES:
                pl.semaphore_signal(credit, inc=1, device_id=flipped(b, 4), device_id_type=MESH)
            send(1, 3, a.at[:, :, :, 1 - y, :, sides[0]], r1.at[k, 0, :, :, :, :, lanes])
            send(2, 2, a.at[:, :, 1 - x, :, :, sides[1]], r1.at[k, 1, :, :, :, :, lanes])
        if r == 2:
            for h in range(2):
                got[(p, 1 + h)].wait_recv()

                def add(i, carry, h=h):
                    m = (i // 4, (i // 2) % 2, i % 2)
                    full = (m[0], m[1], m[2], y) if h == 0 else (m[0], m[1], x, m[2])
                    at = (k, h) + m + (ALL, lanes)
                    r1[at] = r1[at] + a[full + (ALL, sides[h])]
                    return carry

                lax.fori_loop(0, 8, add, 0)
                send(3 + h, 1, r1.at[k, h, :, 1 - zl, :, :, lanes], r2.at[k, h, :, :, :, lanes])
        if r in (3, 4, 5):
            for h in range(2):
                got[(p, 2 * r - 3 + h)].wait_send()
        if r == 3:
            for h in range(2):
                got[(p, 3 + h)].wait_recv()
                for i in range(2):
                    for j in range(2):
                        r2[k, h, i, j, :, lanes] = r2[k, h, i, j, :, lanes] + r1[k, h, i, zl, j, :, lanes]
                mine = (x, y)[h]
                send(5 + h, 2 + h, r2.at[k, h, :, 1 - mine, :, lanes], r3.at[k, h, :, :, lanes])
        if r == 4:
            for h in range(2):
                got[(p, 5 + h)].wait_recv()
                mine = (x, y)[h]
                for i in range(2):
                    r3[k, h, i, :, lanes] = r3[k, h, i, :, lanes] + r2[k, h, i, mine, :, lanes]
                send(7 + h, 0, r3.at[k, h, 1 - zh, :, lanes], r4.at[k, h, :, lanes])
        if r == 5:
            if p - RING in fins:
                fins.pop(p - RING).wait()
            for h in range(2):
                got[(p, 7 + h)].wait_recv()
                if p < 8 and p % 2 == 1:
                    continue
                fin[k, :, sides[h]] = r3[k, h, zh, :, lanes].astype(f32) + r4[k, h, :, lanes].astype(f32)
            if p >= 9:
                g = p - 9
                for t in range(3):
                    copy(fin.at[k, :, pl.ds(256 * t, 256)], gqkv_o.at[:, pl.ds(1024 * t + 256 * g, 256)], finsem.at[k])
                whole = fin.at[k, :, pl.ds(0, 768)]
                fins[p] = pltpu.make_async_copy(whole, whole, finsem.at[k])
            elif p == 8:
                fins[p] = copy(fin.at[k], gout_o, finsem.at[k])
            elif p % 2 == 0:
                fins[p] = copy(fin.at[k], gdown_o.at[pl.ds(16 * p, 32)], finsem.at[k])
            else:
                put = block_pick(p // 2, True).astype(bf16)
                put = jnp.concatenate([put, put], axis=0)

                def place(g, carry, h):
                    lane = pl.ds(pl.multiple_of(128 * g, 128), 128)
                    parts = jnp.concatenate([r3[k, h, zh, :, lane], r4[k, h, :, lane]], axis=1)
                    at = pl.ds(pl.multiple_of(512 * g + 2048 * h, 512), 512)
                    gup[:, at] = dot(parts, put, NN) if p == 1 else gup[:, at] + dot(parts, put, NN)
                    return carry

                for h in range(2):
                    lax.fori_loop(0, 4, functools.partial(place, h=h), 0)
                if p == 7:
                    fins[p] = copy(gup, gup_o, finsem.at[k])

    def push(p, stages):
        while len(scatters[p]) < stages:
            if p > 0 and not scatters[p - 1]:
                push(p - 1, 1)
            scatter_stage(p, len(scatters[p]))
            scatters[p].append(now[0])

    def free(p):
        if p >= SLOTS:
            push(p - SLOTS, 3)
            for s in range(3):
                got.pop((p - SLOTS, s)).wait_send()

    def keep_all(p, product):
        def one(n, carry):
            value = product(pl.ds(pl.multiple_of(n * 512, 512), 512))
            width = value.shape[1]
            blocks = value.astype(bf16).reshape(2, 2, 2, 2, 32, width)
            for core in range(2):
                stag[p % SLOTS, (core + c) % 2, n, :, :, :, :, pl.ds(0, width)] = blocks[:, :, :, core]
            return carry

        lax.fori_loop(0, 2, one, 0)

    actb, actbt, actc, gpre = act, trans, gbr, dout
    fetch(5, 0)
    fetch(6, 1)
    mix_out.wait()
    cot_in.wait()
    for i in range(4):
        flights[0].wait()
        flights[1].wait()

        def mlp_rows(n, bias_sum):
            r = rows_at(n)
            v = dot(actb[r, :], weight(1), NN) + rows[8 + i : 9 + i, :]
            back = dot(cot[r, :], weight(0), NT)
            cdf = 0.5 * (1.0 + lax.erf(v * 0.7071067811865476))
            slope = cdf + v * jnp.exp(-0.5 * v * v) * 0.3989422804014327
            u = (v * cdf).astype(bf16)
            e = (back * slope).astype(bf16)
            actc[r, :] = u
            gpre[r, :] = e
            if i == 0:
                total[r, :] = dot(u, weight(0), NN)
                gab[r, :] = dot(e, weight(1), NT)
            else:
                total[r, :] += dot(u, weight(0), NN)
                gab[r, :] += dot(e, weight(1), NT)
            return bias_sum + column_sum(e.astype(f32))

        bias_sum = jnp.zeros((1, 1024), f32)
        for n in (0, 2):
            bias_sum = lax.fori_loop(n, n + 2, mlp_rows, bias_sum)
            tick(4.9)
        vsum[4 + i : 5 + i, :] = bias_sum
        if i < 3:
            fetch(7 + 2 * i, 0)
        else:
            fetch(4, 2)
        free(2 * i)
        keep_all(2 * i, lambda r: dot(actc[:, r], cot[...], TN))
        ready[0] = 2 * i + 1
        tick(2.9)
        if i < 3:
            fetch(8 + 2 * i, 1)
        free(2 * i + 1)
        keep_all(2 * i + 1, lambda r: dot(actbt[r, :], gpre[...], NN))
        ready[0] = 2 * i + 2
        tick(2.9)
    assert all(len(issued) == 5 for issued in gathers)
    fetch(0, 0)
    fetch(1, 1)
    mix_in = copy(spill.at[1], trans, insem.at[3])

    def second_norm_back(i, sums):
        r = rows_at(i)
        h = hid[r, :]
        act[r, :] = (h + total[r, :] + rows[5:6, :]).astype(bf16)
        centred, rstd = norm_stats(h)
        e = gab[r, :]
        back, xhat = norm_grad(centred, rstd, rows[3:4, :], e)
        yv = cot[r, :].astype(f32)
        gh = yv + back
        total[r, :] = gh
        gb = gh.astype(bf16)
        gbr[r, :] = gb
        return tuple(s + column_sum(v) for s, v in zip(sums, (e * xhat, e, yv, gb.astype(f32))))

    sums = lax.fori_loop(0, 4, second_norm_back, (jnp.zeros((1, 1024), f32),) * 4)
    for i in range(4):
        vsum[i : i + 1, :] = sums[i]
    ghid, gaa = total, gab
    out_copy = copy(act, out_o, outsem.at[0])
    actt = cot
    actt_in = copy(spill.at[0], actt, insem.at[4])

    tick(4)

    flights[2].wait()

    mix_in.wait()

    def mixed_back(i, carry):
        r = rows_at(i)
        part = dot(weight_rows(2, i), gbr[...], NT).astype(bf16)
        dout[r, :] = part
        share = part.astype(f32) * trans[r, :].astype(f32)
        delta[pl.ds(4 * i, 4), :] = jnp.sum(share.reshape(4, 64, 1024), axis=1)
        return carry

    for i in range(4):
        mixed_back(i, 0)
    tick(2.2)
    free(8)
    keep_all(8, lambda r: dot(trans[r, :], gbr[...], NN))
    ready[0] = 9
    tok = trans
    tok_in = copy(tok_h, tok, insem.at[1])
    actt_in.wait()
    dq, dk, dv = (hid.at[:, pl.ds(256 * i, 256)] for i in range(3))

    def attend_back(g, first, count):
        q, k, v = (qkv.at[g, :, pl.ds(256 * i, 256)] for i in range(3))

        def one(i, carry):
            head = first + i
            mask = head_mask(head, 1024)
            some = mask[:256]
            low = lax.shift_right_logical(lax.broadcasted_iota(jnp.int32, (256, 256), 0), 6) == head
            km = jnp.where(mask, k[...], bf16(0))

            def masked(r):
                qm = jnp.where(some, q[r, :], bf16(0)) * bf16(0.125)
                return qm, jnp.where(low, dout[pl.ds(256 * g, 256), r], bf16(0))

            def score(r):
                qm, dom = masked(r)
                return dot(k[...], qm, NT), dot(v[...], dom, NN)

            def soft(r, s, dp):
                p = jnp.exp(s - level[pl.ds(g * 4 + head, 1), r])
                return p.astype(bf16), (p * (dp - delta[pl.ds(g * 4 + head, 1), r])).astype(bf16)

            def grads(r, p, ds):
                qm, dom = masked(r)
                dq[r, :] = jnp.where(some, dot(ds, km, TN) * 0.125, dq[r, :])
                return dot(ds, qm, NN), dot(p, dom, NT)

            dkh, dvh = 0.0, 0.0
            s = score(quarter_rows[0])
            for j in range(5):
                later = score(quarter_rows[j + 1]) if j < 3 else None
                held = soft(quarter_rows[j], *s) if j < 4 else None
                if j > 0:
                    dk_part, dv_part = grads(quarter_rows[j - 1], *last)
                    dkh, dvh = dkh + dk_part, dvh + dv_part
                last, s = held, later
            dk[...] = jnp.where(mask, dkh, dk[...])
            dv[...] = jnp.where(mask, dvh, dv[...])
            return carry

        lax.fori_loop(0, count, one, 0)

    vec_parts = ((4,), (2,), (3,), (2, 3), (1,), (0,), (0, 1))
    vec_steps = ((0,), (1, 2, 3), (4, 5, 6))
    flying = {}

    def vector_send(part, step):
        lines = pl.ds(8 * part, 8)
        for n in vec_steps[step]:
            flying[(part, n)] = remote(
                vsum.at[lines], vrecv.at[n, lines], ussem.at[part, n], ursem.at[part, n], *vec_parts[n])

    def vector_add(part, step):
        lines = pl.ds(8 * part, 8)
        for n in vec_steps[step]:
            flying[(part, n)].wait()
        for n in vec_steps[step]:
            vsum[lines, :] = vsum[lines, :] + vrecv[n, lines, :]

    def act_back_all(g):
        flights[g % 2].wait()

        def act_back(i, carry):
            r = rows_at(i)
            part = dot(qkv[g, r, :], weight(g % 2, 768), NT)
            if g == 0:
                gaa[r, :] = part
            else:
                gaa[r, :] += part
            return carry

        lax.fori_loop(0, 4, act_back, 0)

    vector_send(0, 0)
    for g in range(4):
        for first in (0, 2):
            if g < 2:
                attend_back(g, first, 2)
                tick(7.1)
            else:
                attend_back(g, first, 1)
                tick(3.6)
                attend_back(g, first + 1, 1)
                tick(3.6)
            if first == 2 and g < 3:
                vector_add(0, g)
                if g < 2:
                    vector_send(0, g + 1)
        for t, part in enumerate((dq, dk, dv)):
            qkv[g, :, 256 * t : 256 * t + 256] = part[...].astype(bf16)
        free(9 + g)
        keep_all(9 + g, lambda r: dot(actt[r, :], qkv[g], NN))
        ready[0] = 10 + g
        tick(2.6)
        at = pl.ds(256 * g, 256)
        vsum[8:9, at] = column_sum(qkv[g, :, 0:256].astype(f32))
        vsum[9:10, at] = column_sum(qkv[g, :, 512:768].astype(f32))
        act_back_all(g)
        if g < 2:
            fetch(g + 2, g % 2)
        tick(2.3)

    out_copy.wait()
    tok_in.wait()

    def first_norm_back(i, sums):
        r = rows_at(i)
        centred, rstd = norm_stats(tok[r, :].astype(f32))
        e = gaa[r, :]
        back, xhat = norm_grad(centred, rstd, rows[0:1, :], e)
        act[r, :] = (ghid[r, :] + back).astype(bf16)
        return tuple(s + column_sum(v) for s, v in zip(sums, (e * xhat, e)))

    sums = (jnp.zeros((1, 1024), f32),) * 2
    for i in (0, 2):
        sums = lax.fori_loop(i, i + 2, first_norm_back, sums)
        tick(1.7)
    gtok_copy = copy(act, gtok_o, outsem.at[1])
    vsum[10:11, :] = sums[0]
    vsum[11:12, :] = sums[1]
    vsum[12:16, :] = jnp.zeros((4, 1024), f32)
    own_index = ((zh * 2 + zl) * 2 + x) * 4 + y * 2 + c
    n = lax.broadcasted_iota(jnp.int32, (1024, 128), 0)
    j = lax.broadcasted_iota(jnp.int32, (1024, 128), 1)

    def cut(value, base):
        pick = jnp.where(n == base + j, 1.0, 0.0)
        return lax.dot_general(value, pick, NN, precision=lax.Precision.HIGHEST, preferred_element_type=f32)

    vector_send(1, 0)
    tick(3.5)
    vector_add(1, 0)
    vector_send(1, 1)
    early = cut(vsum[0:8, :], 32 * own_index)
    for i, at in ((2, 3), (3, 0), (4, 1), (5, 2)):
        vec_o[i : i + 1, :] = early[at : at + 1]
    lane = lax.broadcasted_iota(jnp.int32, (1, 128), 1)
    up = early[4:5]
    for i in range(1, 4):
        up = jnp.where(lax.shift_right_logical(lane, 5) == i, pltpu.roll(early, 32 * i, axis=1)[4 + i : 5 + i], up)
    vec_o[7:8, :] = up
    for p in range(2, PIECES):
        all_sent(p)
    for cp in vec_sent:
        cp.wait_send()
    tick(3.5)
    vector_add(1, 1)
    vector_send(1, 2)
    tick(3.5)
    vector_add(1, 2)
    late = cut(vsum[8:16, :], 32 * own_index)
    middle = cut(vsum[8:16, :], 64 * (own_index % 16))
    vec_o[0:1, :] = late[2:3]
    vec_o[1:2, :] = late[3:4]
    vec_o[6:7, :] = jnp.where(own_index < 16, middle[0:1], middle[1:2])
    while len(scatters[PIECES - 1]) < 6:
        tick(4)
    for p in range(PIECES - SLOTS, PIECES):
        for n in range(3):
            got[(p, n)].wait_send()
    for cp in fins.values():
        cp.wait()
    gtok_copy.wait()


def layer_call(tok, cot, qkv, out, up, down, vectors):
    S = jax.ShapeDtypeStruct
    V = pltpu.VMEM
    sem = pltpu.SemaphoreType.DMA
    big = (2, 2, 2, 2, 2, 32, 1024)
    n = PIECES
    results = pl.pallas_call(
        layer_kernel,
        out_shape=(
            S((1024, 1024), bf16), S((1024, 1024), bf16), S((32, 3072), f32), S((32, 1024), f32), S((32, 4096), f32),
            S((128, 1024), f32), S((8, 128), f32), S((n,) + big, bf16), S((2, 1024, 1024), bf16)),
        in_specs=[HBM] * 6 + [VMEM] * 8,
        out_specs=(HBM,) * 6 + (VMEM, HBM, HBM),
        scratch_shapes=[
            V((2, 2, 2, 2, 2, 8, 128), f32), V((16, 1024), f32), V((128, 1024), f32), V((16, 1024), f32),
            V((4, 1024, 768), bf16), V((5, 1024, 1024), bf16), V((3, 1024, 1024), f32), V((3,) + big, bf16), V((32, 4096), f32),
            V((16, 1024), f32), V((7, 16, 1024), f32),
            V((SLOTS, 2, 2, 2, 2, 2, 32, 1024), bf16), V((MAIL, 2, 2, 2, 2, 32, 1024), bf16), V((RING, 2, 2, 2, 2, 32, 512), bf16),
            V((RING, 2, 2, 2, 32, 512), bf16), V((RING, 2, 2, 32, 512), bf16), V((RING, 2, 32, 512), bf16), V((RING, 32, 1024), f32),
            sem((5,)), sem((n,)), sem((3,)), sem((2,)), sem((2,)), sem((n,)), sem((TURNS, 9)), sem((5,)), sem((5,)),
            sem((RING, 9)), sem((RING, 9)),
            pltpu.SemaphoreType.REGULAR, sem((2, 7)), sem((2, 7)), sem((RING,))],
        compiler_params=pltpu.CompilerParams(collective_id=1, has_side_effects=True, vmem_limit_bytes=64 << 20),
        name="layer",
    )(tok, cot, qkv, out, up, down, *vectors)
    return results[:7]


def finish_kernel(out, gtok, gqkv, gout, gup, gdown, vec, *refs):
    outs, buffers, (into, away) = refs[:14], refs[14:20], refs[20:]
    flights = []
    for src, dst, buffer in zip((out, gtok, gqkv, gout, gup, gdown), outs[:6], buffers):
        parts = max(src.shape[0] // 256, 1)
        size = src.shape[0] // parts
        for i in range(parts):
            at = pl.ds(i * size, size)
            n = len(flights)
            flights.append(
                (pltpu.make_async_copy(src.at[at], buffer.at[at], into.at[n]), pltpu.make_async_copy(buffer.at[at], dst.at[at], away.at[n])))
            flights[-1][0].start()
    for i, o in enumerate(outs[6:]):
        o[...] = vec[i, : o.shape[0]]
    for first, second in flights:
        first.wait()
        second.start()
    for first, second in flights:
        second.wait()


def finish_call(out, gtok, gqkv, gout, gup, gdown, vec):
    S = jax.ShapeDtypeStruct
    arrays = (out, gtok, gqkv, gout, gup, gdown)
    return pl.pallas_call(
        finish_kernel,
        out_shape=tuple(S(a.shape, a.dtype) for a in arrays) + tuple(S((n,), f32) for n in (32, 32, 32, 32, 32, 32, 64, 128)),
        in_specs=[HBM] * 6 + [VMEM],
        out_specs=(HBM,) * 6 + (VMEM,) * 8,
        scratch_shapes=[pltpu.VMEM(a.shape, a.dtype) for a in arrays] + [pltpu.SemaphoreType.DMA((16,))] * 2,
        name="finish",
    )(*arrays, vec)


def layer(
    tokens, attn_gain, attn_shift, qkv_weight, qv_bias, out_weight, out_bias, mlp_gain, mlp_shift, up_weight, up_bias, down_weight,
    down_bias, cotangent,
):
    vectors = (attn_gain, attn_shift, out_bias, mlp_gain, mlp_shift, down_bias, qv_bias, up_bias)
    results = layer_call(tokens, cotangent, qkv_weight, out_weight, up_weight, down_weight, vectors)
    output, gtok, gqkv, gout, gup, gdown, ggain_a, gshift_a, gob, ggain_b, gshift_b, gdb, gqvb, gub = finish_call(*results)
    return output, gtok, ggain_a, gshift_a, gqkv, gqvb, gout, gob, ggain_b, gshift_b, gup, gub, gdown, gdb


def layer_norm(values_in, gain_vec, bias_vec):
    row_mean = jnp.mean(values_in, axis=-1, keepdims=True)
    centred = values_in - row_mean
    spread = jnp.mean(centred * centred, axis=-1, keepdims=True)
    return centred * lax.rsqrt(spread + epsilon) * gain_vec + bias_vec


def gelu_exact(values_in):
    return jax.nn.gelu(values_in, approximate=False)


def norm_backward(values_in, gain_vec, incoming):
    zero_shift = jnp.zeros_like(gain_vec)
    unused, pull_back = jax.vjp(layer_norm, values_in, gain_vec, zero_shift)
    return pull_back(incoming)


def general_layer(
    tokens,
    attn_gain,
    attn_shift,
    qkv_weight,
    qv_bias,
    out_weight,
    out_bias,
    mlp_gain,
    mlp_shift,
    up_weight,
    up_bias,
    down_weight,
    down_bias,
    cotangent,
):
    length, model_width = tokens.shape
    score_scale = HD ** (-0.5)
    gain_a, shift_a, qkv_full, qv_full, out_full, out_bias_full = (
        lax.all_gather(attn_gain, ("wide", "narrow"), axis=0, tiled=True),
        lax.all_gather(attn_shift, ("wide", "narrow"), axis=0, tiled=True),
        lax.all_gather(qkv_weight, ("wide", "narrow"), axis=0, tiled=True),
        lax.all_gather(qv_bias, ("wide", "narrow"), axis=0, tiled=True),
        lax.all_gather(out_weight, ("wide", "narrow"), axis=0, tiled=True),
        lax.all_gather(out_bias, ("wide", "narrow"), axis=0, tiled=True),
    )
    inputs = tokens.astype(jnp.float32)
    act_a = layer_norm(inputs, gain_a.astype(jnp.float32), shift_a.astype(jnp.float32)).astype(
        jnp.bfloat16
    )
    bias_full = jnp.concatenate(
        [qv_full[:model_width], jnp.zeros((model_width,), jnp.bfloat16), qv_full[model_width:]]
    ).astype(jnp.float32)
    projected = (jnp.dot(act_a, qkv_full, preferred_element_type=jnp.float32) + bias_full).astype(
        jnp.bfloat16
    )
    query_rows = projected[:, :model_width].reshape(length, H, HD)
    key_rows = projected[:, model_width : 2 * model_width].reshape(length, H, HD)
    value_rows = projected[:, 2 * model_width :].reshape(length, H, HD)
    block_rows = min(512, length)
    block_count = length // block_rows
    query_blocks = query_rows.reshape(block_count, block_rows, H, HD)

    def attend_block(query_block):
        scores = (
            jnp.einsum("qhe,khe->hqk", query_block, key_rows, preferred_element_type=jnp.float32)
            * score_scale
        )
        row_max = jnp.max(scores, axis=-1, keepdims=True)
        exp_scores = jnp.exp(scores - row_max)
        denominator = jnp.sum(exp_scores, axis=-1, keepdims=True)
        low_probs = (exp_scores / denominator).astype(jnp.bfloat16)
        mixed_block = jnp.einsum(
            "hqk,khe->qhe", low_probs, value_rows, preferred_element_type=jnp.float32
        )
        return (mixed_block, (row_max + jnp.log(denominator))[..., 0])

    mixed_blocks, log_sums = lax.map(attend_block, query_blocks)
    mixed = mixed_blocks.reshape(length, model_width).astype(jnp.bfloat16)
    hidden = (
        inputs
        + jnp.dot(mixed, out_full, preferred_element_type=jnp.float32)
        + out_bias_full.astype(jnp.float32)
    )
    gain_b, shift_b, up_full, up_bias_full, down_full, down_bias_full = (
        lax.all_gather(mlp_gain, ("wide", "narrow"), axis=0, tiled=True),
        lax.all_gather(mlp_shift, ("wide", "narrow"), axis=0, tiled=True),
        lax.all_gather(up_weight, ("wide", "narrow"), axis=0, tiled=True),
        lax.all_gather(up_bias, ("wide", "narrow"), axis=0, tiled=True),
        lax.all_gather(down_weight, ("wide", "narrow"), axis=0, tiled=True),
        lax.all_gather(down_bias, ("wide", "narrow"), axis=0, tiled=True),
    )
    act_b = layer_norm(hidden, gain_b.astype(jnp.float32), shift_b.astype(jnp.float32)).astype(
        jnp.bfloat16
    )
    pre_up = jnp.dot(act_b, up_full, preferred_element_type=jnp.float32) + up_bias_full.astype(
        jnp.float32
    )
    act_c = gelu_exact(pre_up).astype(jnp.bfloat16)
    output = (
        hidden
        + jnp.dot(act_c, down_full, preferred_element_type=jnp.float32)
        + down_bias_full.astype(jnp.float32)
    ).astype(jnp.bfloat16)
    gain_b_back, up_back, down_back = (
        lax.all_gather(mlp_gain, ("wide", "narrow"), axis=0, tiled=True),
        lax.all_gather(up_weight, ("wide", "narrow"), axis=0, tiled=True),
        lax.all_gather(down_weight, ("wide", "narrow"), axis=0, tiled=True),
    )
    grad_y = cotangent.astype(jnp.float32)
    grad_down_weight = jnp.einsum("sf,sd->fd", act_c, cotangent, preferred_element_type=jnp.float32)
    grad_down_bias = jnp.sum(cotangent.astype(jnp.float32), axis=0)
    grad_act = jnp.einsum("sd,fd->sf", cotangent, down_back, preferred_element_type=jnp.float32)
    unused_gelu, gelu_pull = jax.vjp(gelu_exact, pre_up)
    grad_pre = gelu_pull(grad_act)[0].astype(jnp.bfloat16)
    grad_up_weight = jnp.einsum("sd,sf->df", act_b, grad_pre, preferred_element_type=jnp.float32)
    grad_up_bias = jnp.sum(grad_pre.astype(jnp.float32), axis=0)
    grad_act_b = jnp.einsum("sf,df->sd", grad_pre, up_back, preferred_element_type=jnp.float32)
    hidden_part, grad_mlp_gain, grad_mlp_shift = norm_backward(
        hidden, gain_b_back.astype(jnp.float32), grad_act_b
    )
    grad_hidden = grad_y + hidden_part
    mlp_sums = (
        lax.psum_scatter(grad_mlp_gain, ("wide", "narrow"), scatter_dimension=0, tiled=True),
        lax.psum_scatter(grad_mlp_shift, ("wide", "narrow"), scatter_dimension=0, tiled=True),
        lax.psum_scatter(grad_up_weight, ("wide", "narrow"), scatter_dimension=0, tiled=True),
        lax.psum_scatter(grad_up_bias, ("wide", "narrow"), scatter_dimension=0, tiled=True),
        lax.psum_scatter(grad_down_weight, ("wide", "narrow"), scatter_dimension=0, tiled=True),
        lax.psum_scatter(grad_down_bias, ("wide", "narrow"), scatter_dimension=0, tiled=True),
    )
    gain_a_back, qkv_back, out_back = (
        lax.all_gather(attn_gain, ("wide", "narrow"), axis=0, tiled=True),
        lax.all_gather(qkv_weight, ("wide", "narrow"), axis=0, tiled=True),
        lax.all_gather(out_weight, ("wide", "narrow"), axis=0, tiled=True),
    )
    grad_branch = grad_hidden.astype(jnp.bfloat16)
    grad_out_weight = jnp.einsum(
        "sa,sd->ad", mixed, grad_branch, preferred_element_type=jnp.float32
    )
    grad_out_bias = jnp.sum(grad_branch.astype(jnp.float32), axis=0)
    grad_mixed = jnp.einsum(
        "sd,ad->sa", grad_branch, out_back, preferred_element_type=jnp.float32
    ).astype(jnp.bfloat16)
    grad_blocks = grad_mixed.reshape(block_count, block_rows, H, HD)

    def back_block(carry, block_inputs):
        key_total, value_total = carry
        query_block, grad_block, log_block = block_inputs
        scores = (
            jnp.einsum("qhe,khe->hqk", query_block, key_rows, preferred_element_type=jnp.float32)
            * score_scale
        )
        attn_probs = jnp.exp(scores - log_block[..., None])
        grad_probs = jnp.einsum(
            "qhe,khe->hqk", grad_block, value_rows, preferred_element_type=jnp.float32
        )
        row_delta = jnp.sum(grad_probs * attn_probs, axis=-1, keepdims=True)
        grad_scores = (attn_probs * (grad_probs - row_delta)).astype(jnp.bfloat16)
        low_probs = attn_probs.astype(jnp.bfloat16)
        value_total = value_total + jnp.einsum(
            "hqk,qhe->khe", low_probs, grad_block, preferred_element_type=jnp.float32
        )
        key_total = (
            key_total
            + jnp.einsum(
                "hqk,qhe->khe", grad_scores, query_block, preferred_element_type=jnp.float32
            )
            * score_scale
        )
        grad_query = (
            jnp.einsum("hqk,khe->qhe", grad_scores, key_rows, preferred_element_type=jnp.float32)
            * score_scale
        )
        return ((key_total, value_total), grad_query)

    zero_heads = jnp.zeros((length, H, HD), jnp.float32)
    (grad_key, grad_value), grad_query = lax.scan(
        back_block, (zero_heads, zero_heads), (query_blocks, grad_blocks, log_sums)
    )
    grad_projected = jnp.concatenate(
        [
            grad_query.reshape(length, model_width),
            grad_key.reshape(length, model_width),
            grad_value.reshape(length, model_width),
        ],
        axis=1,
    ).astype(jnp.bfloat16)
    grad_qkv_weight = jnp.einsum(
        "sa,sb->ab", act_a, grad_projected, preferred_element_type=jnp.float32
    )
    column_sums = jnp.sum(grad_projected.astype(jnp.float32), axis=0)
    grad_qv_bias = jnp.concatenate([column_sums[:model_width], column_sums[2 * model_width :]])
    grad_act_a = jnp.einsum(
        "sb,ab->sa", grad_projected, qkv_back, preferred_element_type=jnp.float32
    )
    input_part, grad_attn_gain, grad_attn_shift = norm_backward(
        inputs, gain_a_back.astype(jnp.float32), grad_act_a
    )
    grad_tokens = (grad_hidden + input_part).astype(jnp.bfloat16)
    attn_sums = (
        lax.psum_scatter(grad_attn_gain, ("wide", "narrow"), scatter_dimension=0, tiled=True),
        lax.psum_scatter(grad_attn_shift, ("wide", "narrow"), scatter_dimension=0, tiled=True),
        lax.psum_scatter(grad_qkv_weight, ("wide", "narrow"), scatter_dimension=0, tiled=True),
        lax.psum_scatter(grad_qv_bias, ("wide", "narrow"), scatter_dimension=0, tiled=True),
        lax.psum_scatter(grad_out_weight, ("wide", "narrow"), scatter_dimension=0, tiled=True),
        lax.psum_scatter(grad_out_bias, ("wide", "narrow"), scatter_dimension=0, tiled=True),
    )
    return (
        output,
        grad_tokens,
        attn_sums[0],
        attn_sums[1],
        attn_sums[2],
        attn_sums[3],
        attn_sums[4],
        attn_sums[5],
        mlp_sums[0],
        mlp_sums[1],
        mlp_sums[2],
        mlp_sums[3],
        mlp_sums[4],
        mlp_sums[5],
    )


def solution(mesh):
    placed = (
        P(("wide", "narrow"), None),
        P(("wide", "narrow")),
        P(("wide", "narrow")),
        P(("wide", "narrow"), None),
        P(("wide", "narrow")),
        P(("wide", "narrow"), None),
        P(("wide", "narrow")),
        P(("wide", "narrow")),
        P(("wide", "narrow")),
        P(("wide", "narrow"), None),
        P(("wide", "narrow")),
        P(("wide", "narrow"), None),
        P(("wide", "narrow")),
        P(("wide", "narrow"), None),
    )
    return jax.shard_map(
        layer if dict(mesh.shape) == {"wide": 8, "narrow": 4} else general_layer,
        mesh=mesh,
        in_specs=placed,
        out_specs=(
            P(("wide", "narrow"), None),
            P(("wide", "narrow"), None),
            P(("wide", "narrow")),
            P(("wide", "narrow")),
            P(("wide", "narrow"), None),
            P(("wide", "narrow")),
            P(("wide", "narrow"), None),
            P(("wide", "narrow")),
            P(("wide", "narrow")),
            P(("wide", "narrow")),
            P(("wide", "narrow"), None),
            P(("wide", "narrow")),
            P(("wide", "narrow"), None),
            P(("wide", "narrow")),
        ),
        check_vma=False,
    )
```

```python
import functools
import jax
import jax.numpy as jnp
from jax import lax
from jax.experimental import pallas as pl
from jax.experimental.pallas import tpu as pltpu
from jax.sharding import PartitionSpec as P

H = 16
HD = 64
epsilon = 1e-05
bf16 = jnp.bfloat16
f32 = jnp.float32
NN = (((1,), (0,)), ((), ()))
NT = (((1,), (1,)), ((), ()))
TN = (((0,), (0,)), ((), ()))
ALL = slice(None)
MESH = pl.DeviceIdType.MESH
HBM = pl.BlockSpec(memory_space=pltpu.HBM)
VMEM = pl.BlockSpec(memory_space=pltpu.VMEM)

HALVES = ((0, 2, 1, 3), (0, 3, 1, 2))
THIRDS = ((0, 1, 2, 3), (0, 3, 1, 2), (0, 2, 3, 1))
PIECES = 13
SENDINGS = 14
GATHER_START = (0, 0, 0, 0, 22, 24, 28, 33, 38, 44, 50, 56, 62)
GATHER_LAG = (5, 5, 7.5, 7.5)
SCATTER_LAG = (4, 8, 10, 5, 6)
LAST_LAG = (2, 3, 3, 3, 12)
SCATTER_GAP = 7
SLOTS = 4
MAIL = 1
RING = 5
TURNS = 8


def dot(a, b, dims):
    return lax.dot_general(a, b, dims, preferred_element_type=f32)


def device_bits():
    w = lax.axis_index("wide")
    n = lax.axis_index("narrow")
    return (w // 4, (w // 2) % 2, w % 2, n // 2, n % 2)


def flipped(b, *dims):
    t = tuple(1 - v if i in dims else v for i, v in enumerate(b))
    return (t[0] * 4 + t[1] * 2 + t[2], t[3] * 2 + t[4])


def parts_of(width, thirds):
    if thirds:
        third = width // 3
        return [(order, n * third, third, n % 2, n // 2 * third) for n, order in enumerate(THIRDS)]
    return [(order, n * width // 2, width // 2, n, 0) for n, order in enumerate(HALVES)]


def head_mask(head, rows):
    return lax.shift_right_logical(lax.broadcasted_iota(jnp.int32, (rows, 256), 1), 6) == head


def norm_stats(v):
    mean = jnp.mean(v, axis=1, keepdims=True)
    centred = v - mean
    rstd = lax.rsqrt(jnp.mean(centred * centred, axis=1, keepdims=True) + epsilon)
    return centred, rstd


def norm_grad(centred, rstd, gain, e):
    xhat = centred * rstd
    eg = e * gain
    return rstd * (eg - jnp.mean(eg, axis=1, keepdims=True) - xhat * jnp.mean(eg * xhat, axis=1, keepdims=True)), xhat


def column_sum(v):
    return jnp.sum(v, axis=0, keepdims=True)


def block_pick(i, transposed):
    shape = (128, 512) if transposed else (512, 128)
    unit = lax.broadcasted_iota(jnp.int32, shape, 1 if transposed else 0)
    lane = lax.broadcasted_iota(jnp.int32, shape, 0 if transposed else 1)
    return jnp.where(unit == 128 * lax.shift_right_logical(lane, 5) + 32 * i + (lane & 31), 1.0, 0.0)


def layer_kernel(
    tok_h, cot_h, qkv_h, out_h, up_h, down_h, again_v, ashift_v, obias_v, mgain_v, mshift_v, dbias_v, qvbias_v, ubias_v,
    out_o, gtok_o, gqkv_o, gout_o, gup_o, gdown_o, vec_o, gw, spill, spill_f,
    gv, rows, level, delta, qkv, pb, pf, w, gup, vsum, vrecv,
    stag, mail, r1, r2, r3, r4, fin,
    insem, ownsem, wsem, spsem, outsem, ssem, rsem, vssem, vrsem, bssem, brsem, xsem, xssem, xrsem, credit, ussem, ursem, finsem,
):
    b = device_bits()
    zh, zl, x, y, c = b
    barrier = pltpu.get_barrier_semaphore()
    partners = ((0,), (1,), (2,), (3,), (4,), (2, 3), (0, 1))
    for dims in partners:
        pl.semaphore_signal(barrier, inc=1, device_id=flipped(b, *dims), device_id_type=MESH)

    def copy(src, dst, sem):
        cp = pltpu.make_async_copy(src, dst, sem)
        cp.start()
        return cp

    def remote(src, dst, send_sem, recv_sem, *dims):
        cp = pltpu.make_async_remote_copy(
            src_ref=src, dst_ref=dst, send_sem=send_sem, recv_sem=recv_sem, device_id=flipped(b, *dims), device_id_type=MESH)
        cp.start()
        return cp

    def rows_at(i):
        return pl.ds(pl.multiple_of(i * 256, 256), 256)

    quarter_rows = [pl.ds(256 * i, 256) for i in range(4)]
    act, mixed, trans, gbr, dout = (pb.at[i] for i in range(5))
    tok = dout
    hid, total, gab = (pf.at[i] for i in range(3))
    lse = hid.at[:, pl.ds(0, 128)]

    shards = [gbr.at[pl.ds(32 * p, 32), pl.ds(0, 768 if p < 4 else 1024)] for p in range(9)]
    for g in range(4):
        for t in range(3):
            copy(qkv_h.at[:, pl.ds(1024 * t + 256 * g, 256)], gbr.at[pl.ds(32 * g, 32), pl.ds(256 * t, 256)], ownsem.at[g])
    copy(out_h, shards[4], ownsem.at[4])
    for i in range(4):
        copy(down_h.at[pl.ds(32 * i, 32)], shards[5 + i], ownsem.at[5 + 2 * i])
    shards[5:] = [shards[5], w.at[2, 0, 0, 0, 0, 0], shards[6], w.at[2, 0, 0, 0, 0, 1], shards[7], w.at[2, 0, 0, 0, 1, 0], shards[8], w.at[2, 0, 0, 0, 1, 1]]
    own = {}
    for i in range(4):
        copy(up_h.at[:, pl.ds(1024 * i, 1024)], mixed.at[pl.ds(32 * i, 32)], insem.at[0])
    pl.semaphore_wait(barrier, len(partners))
    sent = {}
    arrived = set()

    def store_own(p):
        if p not in own:
            if p < 5 or p % 2 == 1:
                pltpu.make_async_copy(shards[p], shards[p], ownsem.at[p]).wait()
            own[p] = copy(shards[p], gw.at[(p,) + b + (ALL, pl.ds(0, 768 if p < 4 else 1024))], ownsem.at[p])

    def own_stored(p):
        if own[p] is not None:
            own[p].wait()
            own[p] = None

    def gather_stage(p, r):
        if r == 0:
            store_own(p)
        if r == (1 if p < 2 else 0):
            own_stored(p)
        for n, (order, first, width, _, _) in enumerate(parts_of(768 if p < 4 else 1024, p == 0)):
            cols = (ALL, pl.ds(first, width))

            def send(dim, sub, s):
                ref = gw.at[(p,) + sub + cols]
                src = shards[p].at[:, pl.ds(first, width)] if r == 0 and p < 2 else ref
                sem = rsem.at[p % TURNS, 8] if s == 4 else xsem.at[s] if n == 2 else rsem.at[p % TURNS, n * 4 + s]
                sent[(p, n, s)] = remote(src, ref, ssem.at[p], sem, dim)

            if r > 0:
                sent[(p, n, r - 1)].wait_recv()
            held = tuple(ALL if i in order[:r] else b[i] for i in range(5))
            if r < 4:
                send(order[r], held, r)
            if r == 3:
                send(4, held, 4)
            if r == 4:
                late = tuple(ALL if i in order[:3] else (1 - b[i] if i == order[3] else b[i]) for i in range(5))
                send(4, late, 4)

    now = [0.0]
    gathers = [[] for _ in range(PIECES)]
    scatters = [[] for _ in range(SENDINGS)]
    ready = [0]

    def due(issued, lags, share):
        return now[0] >= issued[-1] + share * lags[len(issued) - 1]

    def tick(spent):
        now[0] += spent
        for p, issued in enumerate(gathers):
            while len(issued) < 5 and (due(issued, GATHER_LAG, 0.6 if p < 4 else 1 if p < 10 else 1.3) if issued else now[0] >= GATHER_START[p]):
                gather_stage(p, len(issued))
                issued.append(now[0])
        for p, issued in enumerate(scatters[: ready[0]]):
            if not issued and p > 0 and now[0] < scatters[p - 1][0] + SCATTER_GAP and p < 12:
                break
            while len(issued) < 6 and (not issued or due(issued, SCATTER_LAG if p < 12 else LAST_LAG, 0.4 if p == 11 else 0.75 if p >= 9 else 1)):
                scatter_stage(p, len(issued))
                issued.append(now[0])

    def gather_up_to(stages):
        now[0] += 2.5
        for p, r in stages:
            gather_stage(p, r)
            gathers[p].append(now[0])

    def arrive(p):
        while len(gathers[p]) < 5:
            gather_stage(p, len(gathers[p]))
            gathers[p].append(now[0])
        if p not in arrived:
            half = spill.at[0, pl.ds(0, 512), pl.ds(0, 768 if p < 4 else 1024)]
            pltpu.make_async_copy(half, half, rsem.at[p % TURNS, 8]).wait()
            arrived.add(p)

    def all_sent(p):
        rest = spill.at[0, pl.ds(0, 992), pl.ds(0, 768 if p < 4 else 1024)]
        pltpu.make_async_copy(rest, rest, ssem.at[p]).wait()

    flights = {}

    def fetch(p, slot):
        arrive(p)
        flights[slot] = copy(gw.at[p], w.at[slot], wsem.at[slot])

    def weight(slot, cols=1024):
        return w[slot, :, :, :, :, :, :, pl.ds(0, cols)].reshape(1024, cols)

    def weight_rows(slot, i):
        return w[slot, i // 2, i % 2].reshape(256, 1024)

    vec_steps = (((4,),), ((2,), (3,), (2, 3)), ((1,), (0,), (0, 1)))
    vec_sent = []

    def vec_round(r):
        for cp in vec_sent[-3:] if r > 1 else vec_sent:
            cp.wait_recv()
        if r < 3:
            ref = gv.at[(b, b[:4] + (ALL,), b[:2] + (ALL, ALL, ALL))[r]]
            for dims in vec_steps[r]:
                n = len(vec_sent)
                vec_sent.append(remote(ref, ref, vssem.at[n], vrsem.at[n], *dims))

    gather_up_to([(0, 0)])
    tok_in = copy(tok_h, tok, insem.at[1])
    lines = [jnp.zeros((1, 128), f32)] * 3
    for n, (vector, line, offset) in enumerate((
        (again_v, 0, 0), (ashift_v, 0, 32), (obias_v, 0, 64), (mgain_v, 0, 96), (mshift_v, 1, 0), (dbias_v, 1, 32), (qvbias_v, 1, 64),
        (ubias_v, 2, 0),
    )):
        size = vector.shape[0]
        at = lax.broadcasted_iota(jnp.int32, (size, 128), 0)
        lane = lax.broadcasted_iota(jnp.int32, (size, 128), 1)
        put = jnp.where(lane == at + offset, 1.0, 0.0).astype(bf16)
        lines[line] = lines[line] + dot(vector[...].astype(f32).reshape(1, size).astype(bf16), put, NN)
    gv[b] = jnp.concatenate(lines + [jnp.zeros((5, 128), f32)], axis=0)
    vec_round(0)
    up_shard = mixed.at[pl.ds(0, 128)]
    pltpu.make_async_copy(up_shard, up_shard, insem.at[0]).wait()
    for i in range(4):
        pick = block_pick(i, False).astype(bf16)
        for g in range(8):
            shards[6 + 2 * i][:, 128 * g : 128 * g + 128] = dot(
                mixed[32 * (g // 2) : 32 * (g // 2) + 32, 512 * (g % 2) : 512 * (g % 2) + 512], pick, NN).astype(bf16)
    for p in range(PIECES):
        store_own(p)
    vec_round(1)
    gather_up_to([(0, 1)])
    vec_round(2)
    gather_up_to([(0, 2), (1, 0)])
    vec_round(3)
    table = gv[...].reshape(32, 8, 128)
    sub_index = lax.broadcasted_iota(jnp.int32, (32, 8, 128), 1)
    lines = [jnp.sum(jnp.where(sub_index == r, table, 0.0), axis=1) for r in range(3)]

    def spread(line, offset, log, base):
        j = lax.broadcasted_iota(jnp.int32, (128, 1024), 0)
        n = lax.broadcasted_iota(jnp.int32, (128, 1024), 1)
        pick = jnp.where(j == offset + (n & ((1 << log) - 1)), 1.0, 0.0).astype(bf16)
        broad = dot(line.astype(bf16), pick, NN)
        d = lax.broadcasted_iota(jnp.int32, (32, 1024), 0)
        n = lax.broadcasted_iota(jnp.int32, (32, 1024), 1)
        return column_sum(jnp.where(d == base + lax.shift_right_logical(n, log), broad, 0.0))

    places = [(0, 0, 5, 0), (0, 32, 5, 0), (0, 64, 5, 0), (0, 96, 5, 0), (1, 0, 5, 0), (1, 32, 5, 0), (1, 64, 6, 0), (1, 64, 6, 16)]
    places += [(2, 32 * i, 5, 0) for i in range(4)]
    for i, (line, offset, log, base) in enumerate(places):
        rows[i : i + 1, :] = spread(lines[line], offset, log, base)

    gather_up_to([(0, 3), (1, 1), (2, 0)])

    tok_in.wait()

    def first_norm(i, carry):
        r = rows_at(i)
        centred, rstd = norm_stats(tok[r, :].astype(f32))
        a = (centred * rstd * rows[0:1, :] + rows[1:2, :]).astype(bf16)
        act[r, :] = a
        trans[:, r] = a.T
        return carry

    lax.fori_loop(0, 4, first_norm, 0)
    act_out = copy(trans, spill.at[0], spsem.at[0])
    for p in range(PIECES):
        own_stored(p)
    gather_up_to([(0, 4), (1, 2), (2, 1), (3, 0)])
    lse[...] = jnp.zeros_like(lse)

    def project(g, slot):
        at = pl.ds(256 * g, 256)
        bias = jnp.concatenate([rows[6:7, at], jnp.zeros((1, 256), f32), rows[7:8, at]], axis=1)

        def block(i, carry):
            r = rows_at(i)
            qkv[g, r, :] = (dot(act[r, :], weight(slot, 768), NN) + bias).astype(bf16)
            return carry

        lax.fori_loop(0, 4, block, 0)

    def attend(g, first):
        q, k, v = (qkv.at[g, :, pl.ds(256 * i, 256)] for i in range(3))

        def one(i, carry):
            head = first + i
            mask = head_mask(head, 1024)
            some = mask[:256]
            lane = lax.broadcasted_iota(jnp.int32, (256, 128), 1)
            vm = jnp.where(mask, v[...], bf16(1))

            def score(r):
                return dot(jnp.where(some, q[r, :], bf16(0)) * bf16(0.125), k[...], NT)

            def soft(s):
                m = jnp.max(s, axis=1, keepdims=True)
                e = jnp.exp(s - m)
                return e.astype(bf16), m + jnp.log(jnp.sum(e, axis=1, keepdims=True))

            def mix(r, p, m):
                o = dot(p, vm, NN)
                gab[r, 0:256] = jnp.where(some, o / pltpu.roll(o, 64, axis=1), gab[r, 0:256])
                lse[r, :] = jnp.where(lane == g * 4 + head, m, lse[r, :])

            s = score(quarter_rows[0])
            last = None
            for j, r in enumerate(quarter_rows):
                later = score(quarter_rows[j + 1]) if j < 3 else None
                p = soft(s)
                if last is not None:
                    mix(quarter_rows[j - 1], *last)
                last, s = p, later
            mix(quarter_rows[3], *last)
            return carry

        lax.fori_loop(0, 2, one, 0)

    now[0] = 22.0
    fetch(0, 0)
    for g in range(4):
        flights[g % 2].wait()
        if g == 0:
            tick(0)
        project(g, g % 2)
        tick(2.3)
        attend(g, 0)
        tick(3.6)
        fetch(g + 1, (g + 1) % 2 if g < 3 else 2)
        attend(g, 2)
        tick(3.6)
        mixed[:, 256 * g : 256 * g + 256] = gab[:, 0:256].astype(bf16)
        total[256 * g : 256 * g + 256, :] = gab[:, 0:256].T
        if g == 3:
            mix_out = copy(total, spill_f, spsem.at[1])
            fetch(5, 0)
    act_out.wait()
    flights[2].wait()

    level[...] = lse[...].T[0:16]
    all_sent(0)
    all_sent(1)

    def second_norm(i, carry):
        r = rows_at(i)
        v = tok[r, :].astype(f32) + dot(mixed[r, :], weight(2), NN) + rows[2:3, :]
        hid[r, :] = v
        centred, rstd = norm_stats(v)
        a = (centred * rstd * rows[3:4, :] + rows[4:5, :]).astype(bf16)
        act[r, :] = a
        trans[:, r] = a.T
        return carry

    lax.fori_loop(0, 4, second_norm, 0)
    tick(4.5)
    cot = mixed
    cot_in = copy(cot_h, cot, insem.at[2])

    got = {}
    fins = {}

    def half_of(p):
        return 384 if p >= 9 else 512

    def scatter_stage(p, r):
        width = 384 if p >= 12 else 768 if p >= 9 else 1024
        a = stag.at[p % SLOTS, 0]
        k = p % RING
        parts = parts_of(width, p >= 12)

        def send(s, dim, src, dst, n=0):
            sems = (xssem.at[p - 12, s - 1], xrsem.at[p - 12, s - 1]) if n == 2 else (bssem.at[k, s + 4 * n], brsem.at[k, s + 4 * n])
            got[(p, n, s)] = remote(src, dst, *sems, dim)

        if r == 0:
            if p >= MAIL:
                pl.semaphore_wait(credit, 1)
            full = (ALL, ALL, ALL, ALL, ALL, pl.ds(0, width))
            send(0, 4, stag.at[(p % SLOTS, 1) + full], mail.at[(p % MAIL,) + full])
        if r == 1:
            got[(p, 0, 0)].wait_recv()

            def add(i, carry):
                at = (i // 8, (i // 4) % 2, (i // 2) % 2, i % 2, ALL, pl.ds(0, width))
                a[at] = a[at] + mail[(p % MAIL,) + at]
                return carry

            lax.fori_loop(0, 16, add, 0)
            if p + MAIL < SENDINGS:
                pl.semaphore_signal(credit, inc=1, device_id=flipped(b, 4), device_id_type=MESH)
        for n, (order, first, size, half, off) in enumerate(parts if r > 0 else ()):
            dims = [d for d in range(4) if d not in order[5 - r :]]
            gone = order[4 - r] if r < 5 else None
            cols, lanes = pl.ds(first, size), pl.ds(off, size)
            buffers = (None, r1, r2, r3, r4)

            def block(level, at):
                return buffers[level].at[(k, half) + tuple(at) + (ALL, lanes)]

            if r == 1:
                src = a.at[tuple(1 - b[d] if d == gone else ALL for d in range(4)) + (ALL, cols)]
                send(1, gone, src, block(1, (ALL,) * 3), n)
                continue
            got[(p, n, r - 1)].wait_recv()
            if r > 2:
                got[(p, n, r - 1)].wait_send()
            if r == 5:
                continue
            before = [d for d in range(4) if d not in order[6 - r :]]
            last = order[5 - r]

            def add(i, carry):
                bits = [(i // 2 ** (len(dims) - 1 - m)) % 2 for m in range(len(dims))]
                here = dict(zip(dims, bits))
                here[last] = b[last]
                mine = block(r - 1, bits)
                if r == 2:
                    other = a.at[tuple(here[d] for d in range(4)) + (ALL, cols)]
                else:
                    other = block(r - 2, [here[d] for d in before])
                mine[...] = mine[...] + other[...]
                return carry

            if r == 2:
                lax.fori_loop(0, 8, add, 0)
            else:
                for i in range(2 ** len(dims)):
                    add(i, 0)
            src = block(r - 1, [1 - b[d] if d == gone else ALL for d in dims])
            send(r, gone, src, block(r, (ALL,) * (len(dims) - 1)), n)
        if r == 5:
            if p - RING in fins:
                fins.pop(p - RING).wait()
            for n, (order, first, size, half, off) in enumerate(parts):
                if p < 8 and p % 2 == 1:
                    continue
                lanes = pl.ds(off, size)
                fin[k, :, pl.ds(first, size)] = r3[k, half, zh, :, lanes].astype(f32) + r4[k, half, :, lanes].astype(f32)
            if p >= 9:
                size = width // 3
                column = 768 + 128 * (p - 12) if p >= 12 else 256 * (p - 9)
                for t in range(3):
                    copy(fin.at[k, :, pl.ds(size * t, size)], gqkv_o.at[:, pl.ds(1024 * t + column, size)], finsem.at[k])
                whole = fin.at[k, :, pl.ds(0, width)]
                fins[p] = pltpu.make_async_copy(whole, whole, finsem.at[k])
            elif p == 8:
                fins[p] = copy(fin.at[k], gout_o, finsem.at[k])
            elif p % 2 == 0:
                fins[p] = copy(fin.at[k], gdown_o.at[pl.ds(16 * p, 32)], finsem.at[k])
            else:
                put = block_pick(p // 2, True).astype(bf16)
                put = jnp.concatenate([put, put], axis=0)
                columns = [(g // 4, pl.ds(128 * (g % 4), 128)) for g in range(8)]
                parts = [jnp.concatenate([r3[k, h, zh, :, lane], r4[k, h, :, lane]], axis=1) for h, lane in columns]
                spread_out = dot(jnp.concatenate(parts, axis=0), put, NN)
                for g in range(8):
                    at, value = slice(512 * g, 512 * g + 512), spread_out[32 * g : 32 * g + 32]
                    gup[:, at] = value if p == 1 else gup[:, at] + value
                if p == 7:
                    fins[p] = copy(gup, gup_o, finsem.at[k])

    def push(p, stages):
        while len(scatters[p]) < stages:
            if p > 0 and not scatters[p - 1]:
                push(p - 1, 1)
            scatter_stage(p, len(scatters[p]))
            scatters[p].append(now[0])

    def free(p):
        if p >= SLOTS:
            push(p - SLOTS, 3)
            for key in ((0, 0), (0, 1), (1, 1)):
                got.pop((p - SLOTS,) + key).wait_send()

    def keep_all(p, product):
        def one(n, carry):
            value = product(pl.ds(pl.multiple_of(n * 512, 512), 512))
            width = value.shape[1]
            blocks = value.astype(bf16).reshape(2, 2, 2, 2, 32, width)
            for core in range(2):
                stag[p % SLOTS, (core + c) % 2, n, :, :, :, :, pl.ds(0, width)] = blocks[:, :, :, core]
            return carry

        lax.fori_loop(0, 2, one, 0)

    actb, actbt, actc, gpre = act, trans, gbr, dout
    fetch(6, 1)
    mix_out.wait()
    cot_in.wait()
    for i in range(4):
        flights[0].wait()
        flights[1].wait()

        def mlp_rows(n, bias_sum):
            r = rows_at(n)
            v = dot(actb[r, :], weight(1), NN) + rows[8 + i : 9 + i, :]
            back = dot(cot[r, :], weight(0), NT)
            cdf = 0.5 * (1.0 + lax.erf(v * 0.7071067811865476))
            slope = cdf + v * jnp.exp(-0.5 * v * v) * 0.3989422804014327
            u = (v * cdf).astype(bf16)
            e = (back * slope).astype(bf16)
            actc[r, :] = u
            gpre[r, :] = e
            if i == 0:
                total[r, :] = dot(u, weight(0), NN)
                gab[r, :] = dot(e, weight(1), NT)
            else:
                total[r, :] += dot(u, weight(0), NN)
                gab[r, :] += dot(e, weight(1), NT)
            return bias_sum + column_sum(e.astype(f32))

        bias_sum = jnp.zeros((1, 1024), f32)
        for n in (0, 2):
            bias_sum = lax.fori_loop(n, n + 2, mlp_rows, bias_sum)
            tick(4.9)
        vsum[4 + i : 5 + i, :] = bias_sum
        if i < 3:
            fetch(7 + 2 * i, 0)
        else:
            fetch(4, 2)
        free(2 * i)
        keep_all(2 * i, lambda r: dot(actc[:, r], cot[...], TN))
        ready[0] = 2 * i + 1
        tick(2.9)
        if i < 3:
            fetch(8 + 2 * i, 1)
        free(2 * i + 1)
        keep_all(2 * i + 1, lambda r: dot(actbt[r, :], gpre[...], NN))
        ready[0] = 2 * i + 2
        tick(2.9)
    assert all(len(issued) == 5 for issued in gathers)
    fetch(0, 0)
    fetch(1, 1)

    def second_norm_back(i, sums):
        r = rows_at(i)
        h = hid[r, :]
        act[r, :] = (h + total[r, :] + rows[5:6, :]).astype(bf16)
        centred, rstd = norm_stats(h)
        e = gab[r, :]
        back, xhat = norm_grad(centred, rstd, rows[3:4, :], e)
        yv = cot[r, :].astype(f32)
        gh = yv + back
        total[r, :] = gh
        gb = gh.astype(bf16)
        gbr[r, :] = gb
        return tuple(s + column_sum(v) for s, v in zip(sums, (e * xhat, e, yv, gb.astype(f32))))

    sums = lax.fori_loop(0, 4, second_norm_back, (jnp.zeros((1, 1024), f32),) * 4)
    for i in range(4):
        vsum[i : i + 1, :] = sums[i]
    ghid, gaa = total, gab
    mix_in = copy(spill_f, hid, insem.at[3])
    out_copy = copy(act, out_o, outsem.at[0])
    actt = cot
    actt_in = copy(spill.at[0], actt, insem.at[4])

    tick(4)

    flights[2].wait()
    for i in range(4):
        dout[quarter_rows[i], :] = dot(weight_rows(2, i), gbr[...], NT).astype(bf16)
    mix_in.wait()
    for i in range(4):
        mix_part = hid[quarter_rows[i], :]
        trans[quarter_rows[i], :] = mix_part.astype(bf16)
        share = dout[quarter_rows[i], :].astype(f32) * mix_part
        delta[pl.ds(4 * i, 4), :] = jnp.sum(share.reshape(4, 64, 1024), axis=1)
    tick(2.2)
    free(8)
    keep_all(8, lambda r: dot(trans[r, :], gbr[...], NN))
    ready[0] = 9
    tok = trans
    tok_in = copy(tok_h, tok, insem.at[1])
    actt_in.wait()
    dq, dk, dv = (hid.at[:, pl.ds(256 * i, 256)] for i in range(3))

    def attend_back(g, first, count):
        q, k, v = (qkv.at[g, :, pl.ds(256 * i, 256)] for i in range(3))

        def one(i, carry):
            head = first + i
            mask = head_mask(head, 1024)
            some = mask[:256]
            low = lax.shift_right_logical(lax.broadcasted_iota(jnp.int32, (256, 256), 0), 6) == head
            km = jnp.where(mask, k[...], bf16(0))

            def masked(r):
                qm = jnp.where(some, q[r, :], bf16(0)) * bf16(0.125)
                return qm, jnp.where(low, dout[pl.ds(256 * g, 256), r], bf16(0))

            def score(r):
                qm, dom = masked(r)
                return dot(k[...], qm, NT), dot(v[...], dom, NN)

            def soft(r, s, dp):
                p = jnp.exp(s - level[pl.ds(g * 4 + head, 1), r])
                return p.astype(bf16), (p * (dp - delta[pl.ds(g * 4 + head, 1), r])).astype(bf16)

            def grads(r, p, ds):
                qm, dom = masked(r)
                dq[r, :] = jnp.where(some, dot(ds, km, TN) * 0.125, dq[r, :])
                return dot(ds, qm, NN), dot(p, dom, NT)

            dkh, dvh = 0.0, 0.0
            s = score(quarter_rows[0])
            for j in range(5):
                later = score(quarter_rows[j + 1]) if j < 3 else None
                held = soft(quarter_rows[j], *s) if j < 4 else None
                if j > 0:
                    dk_part, dv_part = grads(quarter_rows[j - 1], *last)
                    dkh, dvh = dkh + dk_part, dvh + dv_part
                last, s = held, later
            dk[...] = jnp.where(mask, dkh, dk[...])
            dv[...] = jnp.where(mask, dvh, dv[...])
            return carry

        lax.fori_loop(0, count, one, 0)

    vec_parts = ((4,), (2,), (3,), (2, 3), (1,), (0,), (0, 1))
    vec_steps = ((0,), (1, 2, 3), (4, 5, 6))
    flying = {}

    def vector_send(part, step):
        lines = pl.ds(8 * part, 8)
        for n in vec_steps[step]:
            flying[(part, n)] = remote(
                vsum.at[lines], vrecv.at[n, lines], ussem.at[part, n], ursem.at[part, n], *vec_parts[n])

    def vector_add(part, step):
        lines = pl.ds(8 * part, 8)
        for n in vec_steps[step]:
            flying[(part, n)].wait()
        for n in vec_steps[step]:
            vsum[lines, :] = vsum[lines, :] + vrecv[n, lines, :]

    def act_back_all(g):
        flights[g % 2].wait()

        def act_back(i, carry):
            r = rows_at(i)
            part = dot(qkv[g, r, :], weight(g % 2, 768), NT)
            if g == 0:
                gaa[r, :] = part
            else:
                gaa[r, :] += part
            return carry

        lax.fori_loop(0, 4, act_back, 0)

    def hand_over(g, p, first, width):
        for t, part in enumerate((dq, dk, dv)):
            qkv[g, :, 256 * t + first : 256 * t + first + width] = part[:, first : first + width].astype(bf16)
        free(p)

        def grads():
            return jnp.concatenate([qkv[g, :, 256 * t + first : 256 * t + first + width] for t in range(3)], axis=1)

        keep_all(p, lambda r: dot(actt[r, :], grads(), NN))
        ready[0] = p + 1

    vector_send(0, 0)
    for g in range(4):
        for first in (0, 2):
            if g < 2:
                attend_back(g, first, 2)
                tick(5.9)
            else:
                attend_back(g, first, 1)
                tick(3)
                attend_back(g, first + 1, 1)
                tick(3)
            if first == 2 and g < 3:
                vector_add(0, g)
                if g < 2:
                    vector_send(0, g + 1)
            if g == 3:
                hand_over(3, 12 + first // 2, 64 * first, 128)
                tick(1.2)
        if g < 3:
            hand_over(g, 9 + g, 0, 256)
            tick(2.2)
        at = pl.ds(256 * g, 256)
        vsum[8:9, at] = column_sum(qkv[g, :, 0:256].astype(f32))
        vsum[9:10, at] = column_sum(qkv[g, :, 512:768].astype(f32))
        act_back_all(g)
        if g < 2:
            fetch(g + 2, g % 2)
        tick(2.4)

    out_copy.wait()
    tok_in.wait()

    def first_norm_back(i, sums):
        r = rows_at(i)
        centred, rstd = norm_stats(tok[r, :].astype(f32))
        e = gaa[r, :]
        back, xhat = norm_grad(centred, rstd, rows[0:1, :], e)
        act[r, :] = (ghid[r, :] + back).astype(bf16)
        return tuple(s + column_sum(v) for s, v in zip(sums, (e * xhat, e)))

    sums = (jnp.zeros((1, 1024), f32),) * 2
    for i in (0, 2):
        sums = lax.fori_loop(i, i + 2, first_norm_back, sums)
        tick(1.7)
    gtok_copy = copy(act, gtok_o, outsem.at[1])
    vsum[10:11, :] = sums[0]
    vsum[11:12, :] = sums[1]
    vsum[12:16, :] = jnp.zeros((4, 1024), f32)
    own_index = ((zh * 2 + zl) * 2 + x) * 4 + y * 2 + c
    n = lax.broadcasted_iota(jnp.int32, (1024, 128), 0)
    j = lax.broadcasted_iota(jnp.int32, (1024, 128), 1)

    def cut(value, base):
        pick = jnp.where(n == base + j, 1.0, 0.0)
        return lax.dot_general(value, pick, NN, precision=lax.Precision.HIGHEST, preferred_element_type=f32)

    vector_send(1, 0)
    tick(3.5)
    vector_add(1, 0)
    vector_send(1, 1)
    early = cut(vsum[0:8, :], 32 * own_index)
    for i, at in ((2, 3), (3, 0), (4, 1), (5, 2)):
        vec_o[i : i + 1, :] = early[at : at + 1]
    lane = lax.broadcasted_iota(jnp.int32, (1, 128), 1)
    up = early[4:5]
    for i in range(1, 4):
        up = jnp.where(lax.shift_right_logical(lane, 5) == i, pltpu.roll(early, 32 * i, axis=1)[4 + i : 5 + i], up)
    vec_o[7:8, :] = up
    for p in range(2, PIECES):
        all_sent(p)
    for cp in vec_sent:
        cp.wait_send()
    tick(3.5)
    vector_add(1, 1)
    vector_send(1, 2)
    tick(3.5)
    vector_add(1, 2)
    late = cut(vsum[8:16, :], 32 * own_index)
    middle = cut(vsum[8:16, :], 64 * (own_index % 16))
    vec_o[0:1, :] = late[2:3]
    vec_o[1:2, :] = late[3:4]
    vec_o[6:7, :] = jnp.where(own_index < 16, middle[0:1], middle[1:2])
    while len(scatters[SENDINGS - 1]) < 6:
        tick(4)
    for p in range(SENDINGS - SLOTS, SENDINGS):
        for key in ((0, 0), (0, 1), (1, 1)) + (((2, 1),) if p >= 12 else ()):
            got[(p,) + key].wait_send()
    for cp in fins.values():
        cp.wait()
    gtok_copy.wait()


def layer_call(tok, cot, qkv, out, up, down, vectors):
    S = jax.ShapeDtypeStruct
    V = pltpu.VMEM
    sem = pltpu.SemaphoreType.DMA
    big = (2, 2, 2, 2, 2, 32, 1024)
    n = PIECES
    results = pl.pallas_call(
        layer_kernel,
        out_shape=(
            S((1024, 1024), bf16), S((1024, 1024), bf16), S((32, 3072), f32), S((32, 1024), f32), S((32, 4096), f32),
            S((128, 1024), f32), S((8, 128), f32), S((n,) + big, bf16), S((1, 1024, 1024), bf16),
            S((1024, 1024), f32)),
        in_specs=[HBM] * 6 + [VMEM] * 8,
        out_specs=(HBM,) * 6 + (VMEM, HBM, HBM, HBM),
        scratch_shapes=[
            V((2, 2, 2, 2, 2, 8, 128), f32), V((16, 1024), f32), V((16, 1024), f32), V((16, 1024), f32),
            V((4, 1024, 768), bf16), V((5, 1024, 1024), bf16), V((3, 1024, 1024), f32), V((3,) + big, bf16), V((32, 4096), f32),
            V((16, 1024), f32), V((7, 16, 1024), f32),
            V((SLOTS, 2, 2, 2, 2, 2, 32, 1024), bf16), V((MAIL, 2, 2, 2, 2, 32, 1024), bf16), V((RING, 2, 2, 2, 2, 32, 512), bf16),
            V((RING, 2, 2, 2, 32, 512), bf16), V((RING, 2, 2, 32, 512), bf16), V((RING, 2, 32, 512), bf16), V((RING, 32, 1024), f32),
            sem((5,)), sem((n,)), sem((3,)), sem((2,)), sem((2,)), sem((n,)), sem((TURNS, 9)), sem((7,)), sem((7,)),
            sem((RING, 9)), sem((RING, 9)), sem((4,)), sem((2, 4)), sem((2, 4)),
            pltpu.SemaphoreType.REGULAR, sem((2, 7)), sem((2, 7)), sem((RING,))],
        compiler_params=pltpu.CompilerParams(collective_id=1, has_side_effects=True, vmem_limit_bytes=64 << 20),
        name="layer",
    )(tok, cot, qkv, out, up, down, *vectors)
    return results[:7]


def finish_kernel(out, gtok, gqkv, gout, gup, gdown, vec, *refs):
    outs, buffers, (into, away) = refs[:14], refs[14:20], refs[20:]
    flights = []
    for src, dst, buffer in zip((out, gtok, gqkv, gout, gup, gdown), outs[:6], buffers):
        parts = max(src.shape[0] // 256, 1)
        size = src.shape[0] // parts
        for i in range(parts):
            at = pl.ds(i * size, size)
            n = len(flights)
            flights.append(
                (pltpu.make_async_copy(src.at[at], buffer.at[at], into.at[n]), pltpu.make_async_copy(buffer.at[at], dst.at[at], away.at[n])))
            flights[-1][0].start()
    for i, o in enumerate(outs[6:]):
        o[...] = vec[i, : o.shape[0]]
    for first, second in flights:
        first.wait()
        second.start()
    for first, second in flights:
        second.wait()


def finish_call(out, gtok, gqkv, gout, gup, gdown, vec):
    S = jax.ShapeDtypeStruct
    arrays = (out, gtok, gqkv, gout, gup, gdown)
    return pl.pallas_call(
        finish_kernel,
        out_shape=tuple(S(a.shape, a.dtype) for a in arrays) + tuple(S((n,), f32) for n in (32, 32, 32, 32, 32, 32, 64, 128)),
        in_specs=[HBM] * 6 + [VMEM],
        out_specs=(HBM,) * 6 + (VMEM,) * 8,
        scratch_shapes=[pltpu.VMEM(a.shape, a.dtype) for a in arrays] + [pltpu.SemaphoreType.DMA((16,))] * 2,
        name="finish",
    )(*arrays, vec)


def layer(
    tokens, attn_gain, attn_shift, qkv_weight, qv_bias, out_weight, out_bias, mlp_gain, mlp_shift, up_weight, up_bias, down_weight,
    down_bias, cotangent,
):
    vectors = (attn_gain, attn_shift, out_bias, mlp_gain, mlp_shift, down_bias, qv_bias, up_bias)
    results = layer_call(tokens, cotangent, qkv_weight, out_weight, up_weight, down_weight, vectors)
    output, gtok, gqkv, gout, gup, gdown, ggain_a, gshift_a, gob, ggain_b, gshift_b, gdb, gqvb, gub = finish_call(*results)
    return output, gtok, ggain_a, gshift_a, gqkv, gqvb, gout, gob, ggain_b, gshift_b, gup, gub, gdown, gdb


def layer_norm(values_in, gain_vec, bias_vec):
    row_mean = jnp.mean(values_in, axis=-1, keepdims=True)
    centred = values_in - row_mean
    spread = jnp.mean(centred * centred, axis=-1, keepdims=True)
    return centred * lax.rsqrt(spread + epsilon) * gain_vec + bias_vec


def gelu_exact(values_in):
    return jax.nn.gelu(values_in, approximate=False)


def norm_backward(values_in, gain_vec, incoming):
    zero_shift = jnp.zeros_like(gain_vec)
    unused, pull_back = jax.vjp(layer_norm, values_in, gain_vec, zero_shift)
    return pull_back(incoming)


def general_layer(
    tokens,
    attn_gain,
    attn_shift,
    qkv_weight,
    qv_bias,
    out_weight,
    out_bias,
    mlp_gain,
    mlp_shift,
    up_weight,
    up_bias,
    down_weight,
    down_bias,
    cotangent,
):
    length, model_width = tokens.shape
    score_scale = HD ** (-0.5)
    gain_a, shift_a, qkv_full, qv_full, out_full, out_bias_full = (
        lax.all_gather(attn_gain, ("wide", "narrow"), axis=0, tiled=True),
        lax.all_gather(attn_shift, ("wide", "narrow"), axis=0, tiled=True),
        lax.all_gather(qkv_weight, ("wide", "narrow"), axis=0, tiled=True),
        lax.all_gather(qv_bias, ("wide", "narrow"), axis=0, tiled=True),
        lax.all_gather(out_weight, ("wide", "narrow"), axis=0, tiled=True),
        lax.all_gather(out_bias, ("wide", "narrow"), axis=0, tiled=True),
    )
    inputs = tokens.astype(jnp.float32)
    act_a = layer_norm(inputs, gain_a.astype(jnp.float32), shift_a.astype(jnp.float32)).astype(
        jnp.bfloat16
    )
    bias_full = jnp.concatenate(
        [qv_full[:model_width], jnp.zeros((model_width,), jnp.bfloat16), qv_full[model_width:]]
    ).astype(jnp.float32)
    projected = (jnp.dot(act_a, qkv_full, preferred_element_type=jnp.float32) + bias_full).astype(
        jnp.bfloat16
    )
    query_rows = projected[:, :model_width].reshape(length, H, HD)
    key_rows = projected[:, model_width : 2 * model_width].reshape(length, H, HD)
    value_rows = projected[:, 2 * model_width :].reshape(length, H, HD)
    block_rows = min(512, length)
    block_count = length // block_rows
    query_blocks = query_rows.reshape(block_count, block_rows, H, HD)

    def attend_block(query_block):
        scores = (
            jnp.einsum("qhe,khe->hqk", query_block, key_rows, preferred_element_type=jnp.float32)
            * score_scale
        )
        row_max = jnp.max(scores, axis=-1, keepdims=True)
        exp_scores = jnp.exp(scores - row_max)
        denominator = jnp.sum(exp_scores, axis=-1, keepdims=True)
        low_probs = (exp_scores / denominator).astype(jnp.bfloat16)
        mixed_block = jnp.einsum(
            "hqk,khe->qhe", low_probs, value_rows, preferred_element_type=jnp.float32
        )
        return (mixed_block, (row_max + jnp.log(denominator))[..., 0])

    mixed_blocks, log_sums = lax.map(attend_block, query_blocks)
    mixed = mixed_blocks.reshape(length, model_width).astype(jnp.bfloat16)
    hidden = (
        inputs
        + jnp.dot(mixed, out_full, preferred_element_type=jnp.float32)
        + out_bias_full.astype(jnp.float32)
    )
    gain_b, shift_b, up_full, up_bias_full, down_full, down_bias_full = (
        lax.all_gather(mlp_gain, ("wide", "narrow"), axis=0, tiled=True),
        lax.all_gather(mlp_shift, ("wide", "narrow"), axis=0, tiled=True),
        lax.all_gather(up_weight, ("wide", "narrow"), axis=0, tiled=True),
        lax.all_gather(up_bias, ("wide", "narrow"), axis=0, tiled=True),
        lax.all_gather(down_weight, ("wide", "narrow"), axis=0, tiled=True),
        lax.all_gather(down_bias, ("wide", "narrow"), axis=0, tiled=True),
    )
    act_b = layer_norm(hidden, gain_b.astype(jnp.float32), shift_b.astype(jnp.float32)).astype(
        jnp.bfloat16
    )
    pre_up = jnp.dot(act_b, up_full, preferred_element_type=jnp.float32) + up_bias_full.astype(
        jnp.float32
    )
    act_c = gelu_exact(pre_up).astype(jnp.bfloat16)
    output = (
        hidden
        + jnp.dot(act_c, down_full, preferred_element_type=jnp.float32)
        + down_bias_full.astype(jnp.float32)
    ).astype(jnp.bfloat16)
    gain_b_back, up_back, down_back = (
        lax.all_gather(mlp_gain, ("wide", "narrow"), axis=0, tiled=True),
        lax.all_gather(up_weight, ("wide", "narrow"), axis=0, tiled=True),
        lax.all_gather(down_weight, ("wide", "narrow"), axis=0, tiled=True),
    )
    grad_y = cotangent.astype(jnp.float32)
    grad_down_weight = jnp.einsum("sf,sd->fd", act_c, cotangent, preferred_element_type=jnp.float32)
    grad_down_bias = jnp.sum(cotangent.astype(jnp.float32), axis=0)
    grad_act = jnp.einsum("sd,fd->sf", cotangent, down_back, preferred_element_type=jnp.float32)
    unused_gelu, gelu_pull = jax.vjp(gelu_exact, pre_up)
    grad_pre = gelu_pull(grad_act)[0].astype(jnp.bfloat16)
    grad_up_weight = jnp.einsum("sd,sf->df", act_b, grad_pre, preferred_element_type=jnp.float32)
    grad_up_bias = jnp.sum(grad_pre.astype(jnp.float32), axis=0)
    grad_act_b = jnp.einsum("sf,df->sd", grad_pre, up_back, preferred_element_type=jnp.float32)
    hidden_part, grad_mlp_gain, grad_mlp_shift = norm_backward(
        hidden, gain_b_back.astype(jnp.float32), grad_act_b
    )
    grad_hidden = grad_y + hidden_part
    mlp_sums = (
        lax.psum_scatter(grad_mlp_gain, ("wide", "narrow"), scatter_dimension=0, tiled=True),
        lax.psum_scatter(grad_mlp_shift, ("wide", "narrow"), scatter_dimension=0, tiled=True),
        lax.psum_scatter(grad_up_weight, ("wide", "narrow"), scatter_dimension=0, tiled=True),
        lax.psum_scatter(grad_up_bias, ("wide", "narrow"), scatter_dimension=0, tiled=True),
        lax.psum_scatter(grad_down_weight, ("wide", "narrow"), scatter_dimension=0, tiled=True),
        lax.psum_scatter(grad_down_bias, ("wide", "narrow"), scatter_dimension=0, tiled=True),
    )
    gain_a_back, qkv_back, out_back = (
        lax.all_gather(attn_gain, ("wide", "narrow"), axis=0, tiled=True),
        lax.all_gather(qkv_weight, ("wide", "narrow"), axis=0, tiled=True),
        lax.all_gather(out_weight, ("wide", "narrow"), axis=0, tiled=True),
    )
    grad_branch = grad_hidden.astype(jnp.bfloat16)
    grad_out_weight = jnp.einsum(
        "sa,sd->ad", mixed, grad_branch, preferred_element_type=jnp.float32
    )
    grad_out_bias = jnp.sum(grad_branch.astype(jnp.float32), axis=0)
    grad_mixed = jnp.einsum(
        "sd,ad->sa", grad_branch, out_back, preferred_element_type=jnp.float32
    ).astype(jnp.bfloat16)
    grad_blocks = grad_mixed.reshape(block_count, block_rows, H, HD)

    def back_block(carry, block_inputs):
        key_total, value_total = carry
        query_block, grad_block, log_block = block_inputs
        scores = (
            jnp.einsum("qhe,khe->hqk", query_block, key_rows, preferred_element_type=jnp.float32)
            * score_scale
        )
        attn_probs = jnp.exp(scores - log_block[..., None])
        grad_probs = jnp.einsum(
            "qhe,khe->hqk", grad_block, value_rows, preferred_element_type=jnp.float32
        )
        row_delta = jnp.sum(grad_probs * attn_probs, axis=-1, keepdims=True)
        grad_scores = (attn_probs * (grad_probs - row_delta)).astype(jnp.bfloat16)
        low_probs = attn_probs.astype(jnp.bfloat16)
        value_total = value_total + jnp.einsum(
            "hqk,qhe->khe", low_probs, grad_block, preferred_element_type=jnp.float32
        )
        key_total = (
            key_total
            + jnp.einsum(
                "hqk,qhe->khe", grad_scores, query_block, preferred_element_type=jnp.float32
            )
            * score_scale
        )
        grad_query = (
            jnp.einsum("hqk,khe->qhe", grad_scores, key_rows, preferred_element_type=jnp.float32)
            * score_scale
        )
        return ((key_total, value_total), grad_query)

    zero_heads = jnp.zeros((length, H, HD), jnp.float32)
    (grad_key, grad_value), grad_query = lax.scan(
        back_block, (zero_heads, zero_heads), (query_blocks, grad_blocks, log_sums)
    )
    grad_projected = jnp.concatenate(
        [
            grad_query.reshape(length, model_width),
            grad_key.reshape(length, model_width),
            grad_value.reshape(length, model_width),
        ],
        axis=1,
    ).astype(jnp.bfloat16)
    grad_qkv_weight = jnp.einsum(
        "sa,sb->ab", act_a, grad_projected, preferred_element_type=jnp.float32
    )
    column_sums = jnp.sum(grad_projected.astype(jnp.float32), axis=0)
    grad_qv_bias = jnp.concatenate([column_sums[:model_width], column_sums[2 * model_width :]])
    grad_act_a = jnp.einsum(
        "sb,ab->sa", grad_projected, qkv_back, preferred_element_type=jnp.float32
    )
    input_part, grad_attn_gain, grad_attn_shift = norm_backward(
        inputs, gain_a_back.astype(jnp.float32), grad_act_a
    )
    grad_tokens = (grad_hidden + input_part).astype(jnp.bfloat16)
    attn_sums = (
        lax.psum_scatter(grad_attn_gain, ("wide", "narrow"), scatter_dimension=0, tiled=True),
        lax.psum_scatter(grad_attn_shift, ("wide", "narrow"), scatter_dimension=0, tiled=True),
        lax.psum_scatter(grad_qkv_weight, ("wide", "narrow"), scatter_dimension=0, tiled=True),
        lax.psum_scatter(grad_qv_bias, ("wide", "narrow"), scatter_dimension=0, tiled=True),
        lax.psum_scatter(grad_out_weight, ("wide", "narrow"), scatter_dimension=0, tiled=True),
        lax.psum_scatter(grad_out_bias, ("wide", "narrow"), scatter_dimension=0, tiled=True),
    )
    return (
        output,
        grad_tokens,
        attn_sums[0],
        attn_sums[1],
        attn_sums[2],
        attn_sums[3],
        attn_sums[4],
        attn_sums[5],
        mlp_sums[0],
        mlp_sums[1],
        mlp_sums[2],
        mlp_sums[3],
        mlp_sums[4],
        mlp_sums[5],
    )


def solution(mesh):
    placed = (
        P(("wide", "narrow"), None),
        P(("wide", "narrow")),
        P(("wide", "narrow")),
        P(("wide", "narrow"), None),
        P(("wide", "narrow")),
        P(("wide", "narrow"), None),
        P(("wide", "narrow")),
        P(("wide", "narrow")),
        P(("wide", "narrow")),
        P(("wide", "narrow"), None),
        P(("wide", "narrow")),
        P(("wide", "narrow"), None),
        P(("wide", "narrow")),
        P(("wide", "narrow"), None),
    )
    return jax.shard_map(
        layer if dict(mesh.shape) == {"wide": 8, "narrow": 4} else general_layer,
        mesh=mesh,
        in_specs=placed,
        out_specs=(
            P(("wide", "narrow"), None),
            P(("wide", "narrow"), None),
            P(("wide", "narrow")),
            P(("wide", "narrow")),
            P(("wide", "narrow"), None),
            P(("wide", "narrow")),
            P(("wide", "narrow"), None),
            P(("wide", "narrow")),
            P(("wide", "narrow")),
            P(("wide", "narrow")),
            P(("wide", "narrow"), None),
            P(("wide", "narrow")),
            P(("wide", "narrow"), None),
            P(("wide", "narrow")),
        ),
        check_vma=False,
    )
```

```python
import functools
import jax
import jax.numpy as jnp
from jax import lax
from jax.experimental import pallas as pl
from jax.experimental.pallas import tpu as pltpu
from jax.sharding import PartitionSpec as P

H = 16
HD = 64
epsilon = 1e-05
bf16 = jnp.bfloat16
f32 = jnp.float32
NN = (((1,), (0,)), ((), ()))
NT = (((1,), (1,)), ((), ()))
TN = (((0,), (0,)), ((), ()))
ALL = slice(None)
MESH = pl.DeviceIdType.MESH
HBM = pl.BlockSpec(memory_space=pltpu.HBM)
VMEM = pl.BlockSpec(memory_space=pltpu.VMEM)

HALVES = ((0, 2, 1, 3), (0, 3, 1, 2))
THIRDS = ((0, 1, 2, 3), (0, 3, 1, 2), (0, 2, 3, 1))
PIECES = 13
SENDINGS = 14
GATHER_START = (0, 0, 0, 0, 22, 23, 31, 34, 43, 45, 51, 48, 67)
GATHER_LAG = (
    (3, 3, 4.5, 4.5), (10, 16, 11, 16), (16, 7, 5, 4.5), (8, 5, 4.5, 8.5),
    (3, 3, 9.5, 8.5), (7, 3, 9.5, 8.5), (4, 5, 8.5, 5.5), (5, 7, 8.5, 8.5),
    (6, 3, 6.5, 10.5), (3, 6, 6.5, 13.5), (3, 5, 6.5, 15), (5, 10, 5, 14),
    (7, 3, 10.5, 7.5))
SCATTER_LAG = (4, 8, 10, 5, 6)
LAST_LAG = (2, 3, 3, 3, 12)
SCATTER_GAP = 7
SLOTS = 4
MAIL = 1
RING = 5
TURNS = 8


def dot(a, b, dims):
    return lax.dot_general(a, b, dims, preferred_element_type=f32)


def device_bits():
    w = lax.axis_index("wide")
    n = lax.axis_index("narrow")
    return (w // 4, (w // 2) % 2, w % 2, n // 2, n % 2)


def flipped(b, *dims):
    t = tuple(1 - v if i in dims else v for i, v in enumerate(b))
    return (t[0] * 4 + t[1] * 2 + t[2], t[3] * 2 + t[4])


def parts_of(width, thirds):
    if thirds:
        third = width // 3
        return [(order, n * third, third, n % 2, n // 2 * third) for n, order in enumerate(THIRDS)]
    return [(order, n * width // 2, width // 2, n, 0) for n, order in enumerate(HALVES)]


def head_mask(head, rows):
    return lax.shift_right_logical(lax.broadcasted_iota(jnp.int32, (rows, 256), 1), 6) == head


def norm_stats(v):
    mean = jnp.mean(v, axis=1, keepdims=True)
    centred = v - mean
    rstd = lax.rsqrt(jnp.mean(centred * centred, axis=1, keepdims=True) + epsilon)
    return centred, rstd


def norm_grad(centred, rstd, gain, e):
    xhat = centred * rstd
    eg = e * gain
    return rstd * (eg - jnp.mean(eg, axis=1, keepdims=True) - xhat * jnp.mean(eg * xhat, axis=1, keepdims=True)), xhat


def column_sum(v):
    return jnp.sum(v, axis=0, keepdims=True)


def block_pick(i, transposed):
    shape = (128, 512) if transposed else (512, 128)
    unit = lax.broadcasted_iota(jnp.int32, shape, 1 if transposed else 0)
    lane = lax.broadcasted_iota(jnp.int32, shape, 0 if transposed else 1)
    return jnp.where(unit == 128 * lax.shift_right_logical(lane, 5) + 32 * i + (lane & 31), 1.0, 0.0)


def layer_kernel(
    tok_h, cot_h, qkv_h, out_h, up_h, down_h, again_v, ashift_v, obias_v, mgain_v, mshift_v, dbias_v, qvbias_v, ubias_v,
    out_o, gtok_o, gqkv_o, gout_o, gup_o, gdown_o, vec_o, gw, spill, spill_f,
    gv, rows, level, delta, qkv, pb, pf, w, gup, vsum, vrecv,
    stag, mail, r1, r2, r3, r4, fin,
    insem, ownsem, wsem, spsem, outsem, ssem, rsem, vssem, vrsem, bssem, brsem, xsem, xssem, xrsem, credit, ussem, ursem, finsem,
):
    b = device_bits()
    zh, zl, x, y, c = b
    barrier = pltpu.get_barrier_semaphore()
    partners = ((0,), (1,), (2,), (3,), (4,), (2, 3), (0, 1))
    for dims in partners:
        pl.semaphore_signal(barrier, inc=1, device_id=flipped(b, *dims), device_id_type=MESH)

    def copy(src, dst, sem):
        cp = pltpu.make_async_copy(src, dst, sem)
        cp.start()
        return cp

    def remote(src, dst, send_sem, recv_sem, *dims):
        cp = pltpu.make_async_remote_copy(
            src_ref=src, dst_ref=dst, send_sem=send_sem, recv_sem=recv_sem, device_id=flipped(b, *dims), device_id_type=MESH)
        cp.start()
        return cp

    def rows_at(i):
        return pl.ds(pl.multiple_of(i * 256, 256), 256)

    quarter_rows = [pl.ds(256 * i, 256) for i in range(4)]
    act, mixed, trans, gbr, dout = (pb.at[i] for i in range(5))
    tok = dout
    hid, total, gab = (pf.at[i] for i in range(3))
    lse = hid.at[:, pl.ds(0, 128)]

    shards = [gbr.at[pl.ds(32 * p, 32), pl.ds(0, 768 if p < 4 else 1024)] for p in range(9)]
    for g in range(4):
        for t in range(3):
            copy(qkv_h.at[:, pl.ds(1024 * t + 256 * g, 256)], gbr.at[pl.ds(32 * g, 32), pl.ds(256 * t, 256)], ownsem.at[g])
    copy(out_h, shards[4], ownsem.at[4])
    for i in range(4):
        copy(down_h.at[pl.ds(32 * i, 32)], shards[5 + i], ownsem.at[5 + 2 * i])
    shards[5:] = [shards[5], w.at[2, 0, 0, 0, 0, 0], shards[6], w.at[2, 0, 0, 0, 0, 1], shards[7], w.at[2, 0, 0, 0, 1, 0], shards[8], w.at[2, 0, 0, 0, 1, 1]]
    own = {}
    for i in range(4):
        copy(up_h.at[:, pl.ds(1024 * i, 1024)], mixed.at[pl.ds(32 * i, 32)], insem.at[0])
    pl.semaphore_wait(barrier, len(partners))
    sent = {}
    arrived = set()

    def store_own(p):
        if p not in own:
            if p < 5 or p % 2 == 1:
                pltpu.make_async_copy(shards[p], shards[p], ownsem.at[p]).wait()
            own[p] = copy(shards[p], gw.at[(p,) + b + (ALL, pl.ds(0, 768 if p < 4 else 1024))], ownsem.at[p])

    def own_stored(p):
        if own[p] is not None:
            own[p].wait()
            own[p] = None

    def gather_stage(p, r):
        if r == 0:
            store_own(p)
        if r == (1 if p < 2 else 0):
            own_stored(p)
        for n, (order, first, width, _, _) in enumerate(parts_of(768 if p < 4 else 1024, p == 0)):
            cols = (ALL, pl.ds(first, width))

            def send(dim, sub, s):
                ref = gw.at[(p,) + sub + cols]
                src = shards[p].at[:, pl.ds(first, width)] if r == 0 and p < 2 else ref
                sem = rsem.at[p % TURNS, 8] if s == 4 else xsem.at[s] if n == 2 else rsem.at[p % TURNS, n * 4 + s]
                sent[(p, n, s)] = remote(src, ref, ssem.at[p], sem, dim)

            if r > 0:
                sent[(p, n, r - 1)].wait_recv()
            held = tuple(ALL if i in order[:r] else b[i] for i in range(5))
            if r < 4:
                send(order[r], held, r)
            if r == 3:
                send(4, held, 4)
            if r == 4:
                late = tuple(ALL if i in order[:3] else (1 - b[i] if i == order[3] else b[i]) for i in range(5))
                send(4, late, 4)

    now = [0.0]
    gathers = [[] for _ in range(PIECES)]
    scatters = [[] for _ in range(SENDINGS)]
    ready = [0]

    def due(issued, lags, share):
        return now[0] >= issued[-1] + share * lags[len(issued) - 1]

    def tick(spent):
        now[0] += spent
        for p, issued in enumerate(gathers):
            while len(issued) < 5 and (due(issued, GATHER_LAG[p], 1) if issued else now[0] >= GATHER_START[p]):
                gather_stage(p, len(issued))
                issued.append(now[0])
        for p, issued in enumerate(scatters[: ready[0]]):
            if not issued and p > 0 and now[0] < scatters[p - 1][0] + SCATTER_GAP and p < 12:
                break
            while len(issued) < 6 and (not issued or due(issued, SCATTER_LAG if p < 12 else LAST_LAG, 0.4 if p == 11 else 0.75 if p >= 9 else 1)):
                scatter_stage(p, len(issued))
                issued.append(now[0])

    def gather_up_to(stages):
        now[0] += 2.5
        for p, r in stages:
            gather_stage(p, r)
            gathers[p].append(now[0])

    def arrive(p):
        while len(gathers[p]) < 5:
            gather_stage(p, len(gathers[p]))
            gathers[p].append(now[0])
        if p not in arrived:
            half = spill.at[0, pl.ds(0, 512), pl.ds(0, 768 if p < 4 else 1024)]
            pltpu.make_async_copy(half, half, rsem.at[p % TURNS, 8]).wait()
            arrived.add(p)

    def all_sent(p):
        rest = spill.at[0, pl.ds(0, 992), pl.ds(0, 768 if p < 4 else 1024)]
        pltpu.make_async_copy(rest, rest, ssem.at[p]).wait()

    flights = {}

    def fetch(p, slot):
        arrive(p)
        flights[slot] = copy(gw.at[p], w.at[slot], wsem.at[slot])

    def weight(slot, cols=1024):
        return w[slot, :, :, :, :, :, :, pl.ds(0, cols)].reshape(1024, cols)

    def weight_rows(slot, i):
        return w[slot, i // 2, i % 2].reshape(256, 1024)

    vec_steps = (((4,),), ((2,), (3,), (2, 3)), ((1,), (0,), (0, 1)))
    vec_sent = []

    def vec_round(r):
        for cp in vec_sent[-3:] if r > 1 else vec_sent:
            cp.wait_recv()
        if r < 3:
            ref = gv.at[(b, b[:4] + (ALL,), b[:2] + (ALL, ALL, ALL))[r]]
            for dims in vec_steps[r]:
                n = len(vec_sent)
                vec_sent.append(remote(ref, ref, vssem.at[n], vrsem.at[n], *dims))

    gather_up_to([(0, 0)])
    tok_in = copy(tok_h, tok, insem.at[1])
    lines = [jnp.zeros((1, 128), f32)] * 3
    for n, (vector, line, offset) in enumerate((
        (again_v, 0, 0), (ashift_v, 0, 32), (obias_v, 0, 64), (mgain_v, 0, 96), (mshift_v, 1, 0), (dbias_v, 1, 32), (qvbias_v, 1, 64),
        (ubias_v, 2, 0),
    )):
        size = vector.shape[0]
        at = lax.broadcasted_iota(jnp.int32, (size, 128), 0)
        lane = lax.broadcasted_iota(jnp.int32, (size, 128), 1)
        put = jnp.where(lane == at + offset, 1.0, 0.0).astype(bf16)
        lines[line] = lines[line] + dot(vector[...].astype(f32).reshape(1, size).astype(bf16), put, NN)
    gv[b] = jnp.concatenate(lines + [jnp.zeros((5, 128), f32)], axis=0)
    vec_round(0)
    up_shard = mixed.at[pl.ds(0, 128)]
    pltpu.make_async_copy(up_shard, up_shard, insem.at[0]).wait()
    for i in range(4):
        pick = block_pick(i, False).astype(bf16)
        for g in range(8):
            shards[6 + 2 * i][:, 128 * g : 128 * g + 128] = dot(
                mixed[32 * (g // 2) : 32 * (g // 2) + 32, 512 * (g % 2) : 512 * (g % 2) + 512], pick, NN).astype(bf16)
    for p in range(PIECES):
        store_own(p)
    vec_round(1)
    gather_up_to([(0, 1)])
    vec_round(2)
    gather_up_to([(0, 2), (1, 0)])
    vec_round(3)
    table = gv[...].reshape(32, 8, 128)
    sub_index = lax.broadcasted_iota(jnp.int32, (32, 8, 128), 1)
    lines = [jnp.sum(jnp.where(sub_index == r, table, 0.0), axis=1) for r in range(3)]

    def spread(line, offset, log, base):
        j = lax.broadcasted_iota(jnp.int32, (128, 1024), 0)
        n = lax.broadcasted_iota(jnp.int32, (128, 1024), 1)
        pick = jnp.where(j == offset + (n & ((1 << log) - 1)), 1.0, 0.0).astype(bf16)
        broad = dot(line.astype(bf16), pick, NN)
        d = lax.broadcasted_iota(jnp.int32, (32, 1024), 0)
        n = lax.broadcasted_iota(jnp.int32, (32, 1024), 1)
        return column_sum(jnp.where(d == base + lax.shift_right_logical(n, log), broad, 0.0))

    places = [(0, 0, 5, 0), (0, 32, 5, 0), (0, 64, 5, 0), (0, 96, 5, 0), (1, 0, 5, 0), (1, 32, 5, 0), (1, 64, 6, 0), (1, 64, 6, 16)]
    places += [(2, 32 * i, 5, 0) for i in range(4)]
    for i, (line, offset, log, base) in enumerate(places):
        rows[i : i + 1, :] = spread(lines[line], offset, log, base)

    gather_up_to([(0, 3), (1, 1), (2, 0)])

    tok_in.wait()

    def first_norm(i, carry):
        r = rows_at(i)
        centred, rstd = norm_stats(tok[r, :].astype(f32))
        a = (centred * rstd * rows[0:1, :] + rows[1:2, :]).astype(bf16)
        act[r, :] = a
        trans[:, r] = a.T
        return carry

    lax.fori_loop(0, 4, first_norm, 0)
    act_out = copy(trans, spill.at[0], spsem.at[0])
    for p in range(PIECES):
        own_stored(p)
    gather_up_to([(0, 4), (1, 2), (2, 1), (3, 0)])
    lse[...] = jnp.zeros_like(lse)

    def project(g, slot):
        at = pl.ds(256 * g, 256)
        bias = jnp.concatenate([rows[6:7, at], jnp.zeros((1, 256), f32), rows[7:8, at]], axis=1)

        def block(i, carry):
            r = rows_at(i)
            qkv[g, r, :] = (dot(act[r, :], weight(slot, 768), NN) + bias).astype(bf16)
            return carry

        lax.fori_loop(0, 4, block, 0)

    def attend(g, first):
        q, k, v = (qkv.at[g, :, pl.ds(256 * i, 256)] for i in range(3))

        def one(i, carry):
            head = first + i
            mask = head_mask(head, 1024)
            some = mask[:256]
            lane = lax.broadcasted_iota(jnp.int32, (256, 128), 1)
            vm = jnp.where(mask, v[...], bf16(1))

            def score(r):
                return dot(jnp.where(some, q[r, :], bf16(0)) * bf16(0.125), k[...], NT)

            def soft(s):
                m = jnp.max(s, axis=1, keepdims=True)
                e = jnp.exp(s - m)
                return e.astype(bf16), m + jnp.log(jnp.sum(e, axis=1, keepdims=True))

            def mix(r, p, m):
                o = dot(p, vm, NN)
                gab[r, 0:256] = jnp.where(some, o / pltpu.roll(o, 64, axis=1), gab[r, 0:256])
                lse[r, :] = jnp.where(lane == g * 4 + head, m, lse[r, :])

            s = score(quarter_rows[0])
            last = None
            for j, r in enumerate(quarter_rows):
                later = score(quarter_rows[j + 1]) if j < 3 else None
                p = soft(s)
                if last is not None:
                    mix(quarter_rows[j - 1], *last)
                last, s = p, later
            mix(quarter_rows[3], *last)
            return carry

        lax.fori_loop(0, 2, one, 0)

    now[0] = 22.0
    fetch(0, 0)
    for g in range(4):
        flights[g % 2].wait()
        if g == 0:
            tick(0)
        project(g, g % 2)
        tick(2.3)
        attend(g, 0)
        tick(3.6)
        fetch(g + 1, (g + 1) % 2 if g < 3 else 2)
        attend(g, 2)
        tick(3.6)
        mixed[:, 256 * g : 256 * g + 256] = gab[:, 0:256].astype(bf16)
        total[256 * g : 256 * g + 256, :] = gab[:, 0:256].T
        if g == 3:
            mix_out = copy(total, spill_f, spsem.at[1])
            fetch(5, 0)
    act_out.wait()
    flights[2].wait()

    level[...] = lse[...].T[0:16]
    all_sent(0)
    all_sent(1)

    def second_norm(i, carry):
        r = rows_at(i)
        v = tok[r, :].astype(f32) + dot(mixed[r, :], weight(2), NN) + rows[2:3, :]
        hid[r, :] = v
        centred, rstd = norm_stats(v)
        a = (centred * rstd * rows[3:4, :] + rows[4:5, :]).astype(bf16)
        act[r, :] = a
        trans[:, r] = a.T
        return carry

    lax.fori_loop(0, 4, second_norm, 0)
    tick(4.5)
    cot = mixed
    cot_in = copy(cot_h, cot, insem.at[2])

    got = {}
    fins = {}

    def half_of(p):
        return 384 if p >= 9 else 512

    def scatter_stage(p, r):
        width = 384 if p >= 12 else 768 if p >= 9 else 1024
        a = stag.at[p % SLOTS, 0]
        k = p % RING
        parts = parts_of(width, p >= 12)

        def send(s, dim, src, dst, n=0):
            sems = (xssem.at[p - 12, s - 1], xrsem.at[p - 12, s - 1]) if n == 2 else (bssem.at[k, s + 4 * n], brsem.at[k, s + 4 * n])
            got[(p, n, s)] = remote(src, dst, *sems, dim)

        if r == 0:
            if p >= MAIL:
                pl.semaphore_wait(credit, 1)
            full = (ALL, ALL, ALL, ALL, ALL, pl.ds(0, width))
            send(0, 4, stag.at[(p % SLOTS, 1) + full], mail.at[(p % MAIL,) + full])
        if r == 1:
            got[(p, 0, 0)].wait_recv()

            def add(i, carry):
                at = (i // 8, (i // 4) % 2, (i // 2) % 2, i % 2, ALL, pl.ds(0, width))
                a[at] = a[at] + mail[(p % MAIL,) + at]
                return carry

            lax.fori_loop(0, 16, add, 0)
            if p + MAIL < SENDINGS:
                pl.semaphore_signal(credit, inc=1, device_id=flipped(b, 4), device_id_type=MESH)
        for n, (order, first, size, half, off) in enumerate(parts if r > 0 else ()):
            dims = [d for d in range(4) if d not in order[5 - r :]]
            gone = order[4 - r] if r < 5 else None
            cols, lanes = pl.ds(first, size), pl.ds(off, size)
            buffers = (None, r1, r2, r3, r4)

            def block(level, at):
                return buffers[level].at[(k, half) + tuple(at) + (ALL, lanes)]

            if r == 1:
                src = a.at[tuple(1 - b[d] if d == gone else ALL for d in range(4)) + (ALL, cols)]
                send(1, gone, src, block(1, (ALL,) * 3), n)
                continue
            got[(p, n, r - 1)].wait_recv()
            if r > 2:
                got[(p, n, r - 1)].wait_send()
            if r == 5:
                continue
            before = [d for d in range(4) if d not in order[6 - r :]]
            last = order[5 - r]

            def add(i, carry):
                bits = [(i // 2 ** (len(dims) - 1 - m)) % 2 for m in range(len(dims))]
                here = dict(zip(dims, bits))
                here[last] = b[last]
                mine = block(r - 1, bits)
                if r == 2:
                    other = a.at[tuple(here[d] for d in range(4)) + (ALL, cols)]
                else:
                    other = block(r - 2, [here[d] for d in before])
                mine[...] = mine[...] + other[...]
                return carry

            if r == 2:
                lax.fori_loop(0, 8, add, 0)
            else:
                for i in range(2 ** len(dims)):
                    add(i, 0)
            src = block(r - 1, [1 - b[d] if d == gone else ALL for d in dims])
            send(r, gone, src, block(r, (ALL,) * (len(dims) - 1)), n)
        if r == 5:
            if p - RING in fins:
                fins.pop(p - RING).wait()
            for n, (order, first, size, half, off) in enumerate(parts):
                if p < 8 and p % 2 == 1:
                    continue
                lanes = pl.ds(off, size)
                fin[k, :, pl.ds(first, size)] = r3[k, half, zh, :, lanes].astype(f32) + r4[k, half, :, lanes].astype(f32)
            if p >= 9:
                size = width // 3
                column = 768 + 128 * (p - 12) if p >= 12 else 256 * (p - 9)
                for t in range(3):
                    copy(fin.at[k, :, pl.ds(size * t, size)], gqkv_o.at[:, pl.ds(1024 * t + column, size)], finsem.at[k])
                whole = fin.at[k, :, pl.ds(0, width)]
                fins[p] = pltpu.make_async_copy(whole, whole, finsem.at[k])
            elif p == 8:
                fins[p] = copy(fin.at[k], gout_o, finsem.at[k])
            elif p % 2 == 0:
                fins[p] = copy(fin.at[k], gdown_o.at[pl.ds(16 * p, 32)], finsem.at[k])
            else:
                put = block_pick(p // 2, True).astype(bf16)
                put = jnp.concatenate([put, put], axis=0)
                columns = [(g // 4, pl.ds(128 * (g % 4), 128)) for g in range(8)]
                parts = [jnp.concatenate([r3[k, h, zh, :, lane], r4[k, h, :, lane]], axis=1) for h, lane in columns]
                spread_out = dot(jnp.concatenate(parts, axis=0), put, NN)
                for g in range(8):
                    at, value = slice(512 * g, 512 * g + 512), spread_out[32 * g : 32 * g + 32]
                    gup[:, at] = value if p == 1 else gup[:, at] + value
                if p == 7:
                    fins[p] = copy(gup, gup_o, finsem.at[k])

    def push(p, stages):
        while len(scatters[p]) < stages:
            if p > 0 and not scatters[p - 1]:
                push(p - 1, 1)
            scatter_stage(p, len(scatters[p]))
            scatters[p].append(now[0])

    def free(p):
        if p >= SLOTS:
            push(p - SLOTS, 3)
            for key in ((0, 0), (0, 1), (1, 1)):
                got.pop((p - SLOTS,) + key).wait_send()

    def keep_all(p, product):
        def one(n, carry):
            value = product(pl.ds(pl.multiple_of(n * 512, 512), 512))
            width = value.shape[1]
            blocks = value.astype(bf16).reshape(2, 2, 2, 2, 32, width)
            for core in range(2):
                stag[p % SLOTS, (core + c) % 2, n, :, :, :, :, pl.ds(0, width)] = blocks[:, :, :, core]
            return carry

        lax.fori_loop(0, 2, one, 0)

    actb, actbt, actc, gpre = act, trans, gbr, dout
    fetch(6, 1)
    mix_out.wait()
    cot_in.wait()
    for i in range(4):
        flights[0].wait()
        flights[1].wait()

        def mlp_rows(n, bias_sum):
            r = rows_at(n)
            v = dot(actb[r, :], weight(1), NN) + rows[8 + i : 9 + i, :]
            back = dot(cot[r, :], weight(0), NT)
            cdf = 0.5 * (1.0 + lax.erf(v * 0.7071067811865476))
            slope = cdf + v * jnp.exp(-0.5 * v * v) * 0.3989422804014327
            u = (v * cdf).astype(bf16)
            e = (back * slope).astype(bf16)
            actc[r, :] = u
            gpre[r, :] = e
            if i == 0:
                total[r, :] = dot(u, weight(0), NN)
                gab[r, :] = dot(e, weight(1), NT)
            else:
                total[r, :] += dot(u, weight(0), NN)
                gab[r, :] += dot(e, weight(1), NT)
            return bias_sum + column_sum(e.astype(f32))

        bias_sum = jnp.zeros((1, 1024), f32)
        for n in (0, 2):
            bias_sum = lax.fori_loop(n, n + 2, mlp_rows, bias_sum)
            tick(4.9)
        vsum[4 + i : 5 + i, :] = bias_sum
        if i < 3:
            fetch(7 + 2 * i, 0)
        else:
            fetch(4, 2)
        free(2 * i)
        keep_all(2 * i, lambda r: dot(actc[:, r], cot[...], TN))
        ready[0] = 2 * i + 1
        tick(2.9)
        if i < 3:
            fetch(8 + 2 * i, 1)
        free(2 * i + 1)
        keep_all(2 * i + 1, lambda r: dot(actbt[r, :], gpre[...], NN))
        ready[0] = 2 * i + 2
        tick(2.9)
    assert all(len(issued) == 5 for issued in gathers)
    fetch(0, 0)
    fetch(1, 1)

    def second_norm_back(i, sums):
        r = rows_at(i)
        h = hid[r, :]
        act[r, :] = (h + total[r, :] + rows[5:6, :]).astype(bf16)
        centred, rstd = norm_stats(h)
        e = gab[r, :]
        back, xhat = norm_grad(centred, rstd, rows[3:4, :], e)
        yv = cot[r, :].astype(f32)
        gh = yv + back
        total[r, :] = gh
        gb = gh.astype(bf16)
        gbr[r, :] = gb
        return tuple(s + column_sum(v) for s, v in zip(sums, (e * xhat, e, yv, gb.astype(f32))))

    sums = lax.fori_loop(0, 4, second_norm_back, (jnp.zeros((1, 1024), f32),) * 4)
    for i in range(4):
        vsum[i : i + 1, :] = sums[i]
    ghid, gaa = total, gab
    mix_in = copy(spill_f, hid, insem.at[3])
    out_copy = copy(act, out_o, outsem.at[0])
    actt = cot
    actt_in = copy(spill.at[0], actt, insem.at[4])

    tick(4)

    flights[2].wait()
    for i in range(4):
        dout[quarter_rows[i], :] = dot(weight_rows(2, i), gbr[...], NT).astype(bf16)
    mix_in.wait()
    for i in range(4):
        mix_part = hid[quarter_rows[i], :]
        trans[quarter_rows[i], :] = mix_part.astype(bf16)
        share = dout[quarter_rows[i], :].astype(f32) * mix_part
        delta[pl.ds(4 * i, 4), :] = jnp.sum(share.reshape(4, 64, 1024), axis=1)
    tick(2.2)
    free(8)
    keep_all(8, lambda r: dot(trans[r, :], gbr[...], NN))
    ready[0] = 9
    tok = trans
    tok_in = copy(tok_h, tok, insem.at[1])
    actt_in.wait()
    dq, dk, dv = (hid.at[:, pl.ds(256 * i, 256)] for i in range(3))

    def attend_back(g, first, count):
        q, k, v = (qkv.at[g, :, pl.ds(256 * i, 256)] for i in range(3))

        def one(i, carry):
            head = first + i
            mask = head_mask(head, 1024)
            some = mask[:256]
            low = lax.shift_right_logical(lax.broadcasted_iota(jnp.int32, (256, 256), 0), 6) == head
            km = jnp.where(mask, k[...], bf16(0))

            def masked(r):
                qm = jnp.where(some, q[r, :], bf16(0)) * bf16(0.125)
                return qm, jnp.where(low, dout[pl.ds(256 * g, 256), r], bf16(0))

            def score(r):
                qm, dom = masked(r)
                return dot(k[...], qm, NT), dot(v[...], dom, NN)

            def soft(r, s, dp):
                p = jnp.exp(s - level[pl.ds(g * 4 + head, 1), r])
                return p.astype(bf16), (p * (dp - delta[pl.ds(g * 4 + head, 1), r])).astype(bf16)

            def grads(r, p, ds):
                qm, dom = masked(r)
                dq[r, :] = jnp.where(some, dot(ds, km, TN) * 0.125, dq[r, :])
                return dot(ds, qm, NN), dot(p, dom, NT)

            dkh, dvh = 0.0, 0.0
            s = score(quarter_rows[0])
            for j in range(5):
                later = score(quarter_rows[j + 1]) if j < 3 else None
                held = soft(quarter_rows[j], *s) if j < 4 else None
                if j > 0:
                    dk_part, dv_part = grads(quarter_rows[j - 1], *last)
                    dkh, dvh = dkh + dk_part, dvh + dv_part
                last, s = held, later
            dk[...] = jnp.where(mask, dkh, dk[...])
            dv[...] = jnp.where(mask, dvh, dv[...])
            return carry

        lax.fori_loop(0, count, one, 0)

    vec_parts = ((4,), (2,), (3,), (2, 3), (1,), (0,), (0, 1))
    vec_steps = ((0,), (1, 2, 3), (4, 5, 6))
    flying = {}

    def vector_send(part, step):
        lines = pl.ds(8 * part, 8)
        for n in vec_steps[step]:
            flying[(part, n)] = remote(
                vsum.at[lines], vrecv.at[n, lines], ussem.at[part, n], ursem.at[part, n], *vec_parts[n])

    def vector_add(part, step):
        lines = pl.ds(8 * part, 8)
        for n in vec_steps[step]:
            flying[(part, n)].wait()
        for n in vec_steps[step]:
            vsum[lines, :] = vsum[lines, :] + vrecv[n, lines, :]

    def act_back_all(g):
        flights[g % 2].wait()

        def act_back(i, carry):
            r = rows_at(i)
            part = dot(qkv[g, r, :], weight(g % 2, 768), NT)
            if g == 0:
                gaa[r, :] = part
            else:
                gaa[r, :] += part
            return carry

        lax.fori_loop(0, 4, act_back, 0)

    def hand_over(g, p, first, width):
        for t, part in enumerate((dq, dk, dv)):
            qkv[g, :, 256 * t + first : 256 * t + first + width] = part[:, first : first + width].astype(bf16)
        free(p)

        def grads():
            return jnp.concatenate([qkv[g, :, 256 * t + first : 256 * t + first + width] for t in range(3)], axis=1)

        keep_all(p, lambda r: dot(actt[r, :], grads(), NN))
        ready[0] = p + 1

    vector_send(0, 0)
    for g in range(4):
        for first in (0, 2):
            if g < 2:
                attend_back(g, first, 2)
                tick(5.9)
            else:
                attend_back(g, first, 1)
                tick(3)
                attend_back(g, first + 1, 1)
                tick(3)
            if first == 2 and g < 3:
                vector_add(0, g)
                if g < 2:
                    vector_send(0, g + 1)
            if g == 3:
                hand_over(3, 12 + first // 2, 64 * first, 128)
                tick(1.2)
        if g < 3:
            hand_over(g, 9 + g, 0, 256)
            tick(2.2)
        at = pl.ds(256 * g, 256)
        vsum[8:9, at] = column_sum(qkv[g, :, 0:256].astype(f32))
        vsum[9:10, at] = column_sum(qkv[g, :, 512:768].astype(f32))
        act_back_all(g)
        if g < 2:
            fetch(g + 2, g % 2)
        tick(2.4)

    out_copy.wait()
    tok_in.wait()

    def first_norm_back(i, sums):
        r = rows_at(i)
        centred, rstd = norm_stats(tok[r, :].astype(f32))
        e = gaa[r, :]
        back, xhat = norm_grad(centred, rstd, rows[0:1, :], e)
        act[r, :] = (ghid[r, :] + back).astype(bf16)
        return tuple(s + column_sum(v) for s, v in zip(sums, (e * xhat, e)))

    sums = (jnp.zeros((1, 1024), f32),) * 2
    sums = lax.fori_loop(0, 2, first_norm_back, sums)
    tick(1.7)
    sums = lax.fori_loop(2, 4, first_norm_back, sums)
    gtok_copy = copy(act, gtok_o, outsem.at[1])
    vsum[10:11, :] = sums[0]
    vsum[11:12, :] = sums[1]
    vsum[12:16, :] = jnp.zeros((4, 1024), f32)
    own_index = ((zh * 2 + zl) * 2 + x) * 4 + y * 2 + c
    n = lax.broadcasted_iota(jnp.int32, (1024, 128), 0)
    j = lax.broadcasted_iota(jnp.int32, (1024, 128), 1)

    def cut(value, base):
        pick = jnp.where(n == base + j, 1.0, 0.0)
        return lax.dot_general(value, pick, NN, precision=lax.Precision.HIGHEST, preferred_element_type=f32)

    vector_send(1, 0)
    tick(1.7)
    vector_add(1, 0)
    vector_send(1, 1)
    early = cut(vsum[0:8, :], 32 * own_index)
    for i, at in ((2, 3), (3, 0), (4, 1), (5, 2)):
        vec_o[i : i + 1, :] = early[at : at + 1]
    lane = lax.broadcasted_iota(jnp.int32, (1, 128), 1)
    up = early[4:5]
    for i in range(1, 4):
        up = jnp.where(lax.shift_right_logical(lane, 5) == i, pltpu.roll(early, 32 * i, axis=1)[4 + i : 5 + i], up)
    vec_o[7:8, :] = up
    for p in range(2, PIECES):
        all_sent(p)
    for cp in vec_sent:
        cp.wait_send()
    tick(3.5)
    vector_add(1, 1)
    vector_send(1, 2)
    tick(3.5)
    vector_add(1, 2)
    late = cut(vsum[8:16, :], 32 * own_index)
    middle = cut(vsum[8:16, :], 64 * (own_index % 16))
    vec_o[0:1, :] = late[2:3]
    vec_o[1:2, :] = late[3:4]
    vec_o[6:7, :] = jnp.where(own_index < 16, middle[0:1], middle[1:2])
    while len(scatters[SENDINGS - 1]) < 6:
        tick(4)
    for p in range(SENDINGS - SLOTS, SENDINGS):
        for key in ((0, 0), (0, 1), (1, 1)) + (((2, 1),) if p >= 12 else ()):
            got[(p,) + key].wait_send()
    for cp in fins.values():
        cp.wait()
    gtok_copy.wait()


def layer_call(tok, cot, qkv, out, up, down, vectors):
    S = jax.ShapeDtypeStruct
    V = pltpu.VMEM
    sem = pltpu.SemaphoreType.DMA
    big = (2, 2, 2, 2, 2, 32, 1024)
    n = PIECES
    results = pl.pallas_call(
        layer_kernel,
        out_shape=(
            S((1024, 1024), bf16), S((1024, 1024), bf16), S((32, 3072), f32), S((32, 1024), f32), S((32, 4096), f32),
            S((128, 1024), f32), S((8, 128), f32), S((n,) + big, bf16), S((1, 1024, 1024), bf16),
            S((1024, 1024), f32)),
        in_specs=[HBM] * 6 + [VMEM] * 8,
        out_specs=(HBM,) * 6 + (VMEM, HBM, HBM, HBM),
        scratch_shapes=[
            V((2, 2, 2, 2, 2, 8, 128), f32), V((16, 1024), f32), V((16, 1024), f32), V((16, 1024), f32),
            V((4, 1024, 768), bf16), V((5, 1024, 1024), bf16), V((3, 1024, 1024), f32), V((3,) + big, bf16), V((32, 4096), f32),
            V((16, 1024), f32), V((7, 16, 1024), f32),
            V((SLOTS, 2, 2, 2, 2, 2, 32, 1024), bf16), V((MAIL, 2, 2, 2, 2, 32, 1024), bf16), V((RING, 2, 2, 2, 2, 32, 512), bf16),
            V((RING, 2, 2, 2, 32, 512), bf16), V((RING, 2, 2, 32, 512), bf16), V((RING, 2, 32, 512), bf16), V((RING, 32, 1024), f32),
            sem((5,)), sem((n,)), sem((3,)), sem((2,)), sem((2,)), sem((n,)), sem((TURNS, 9)), sem((7,)), sem((7,)),
            sem((RING, 9)), sem((RING, 9)), sem((4,)), sem((2, 4)), sem((2, 4)),
            pltpu.SemaphoreType.REGULAR, sem((2, 7)), sem((2, 7)), sem((RING,))],
        compiler_params=pltpu.CompilerParams(collective_id=1, has_side_effects=True, vmem_limit_bytes=64 << 20),
        name="layer",
    )(tok, cot, qkv, out, up, down, *vectors)
    return results[:7]


def finish_kernel(*refs):
    for src, dst in zip(refs[:6], refs[7:13]):
        dst[...] = src[...]
    for i, o in enumerate(refs[13:]):
        o[...] = refs[6][i, : o.shape[0]]


def finish_call(out, gtok, gqkv, gout, gup, gdown, vec):
    S = jax.ShapeDtypeStruct
    arrays = (out, gtok, gqkv, gout, gup, gdown)
    blocks = []
    for a in arrays:
        rows, cols = a.shape
        if rows > 32:
            blocks.append(pl.BlockSpec((rows // 2, cols), lambda i: (i, 0)))
        else:
            blocks.append(pl.BlockSpec((rows, cols // 2), lambda i: (0, i)))
    lengths = (32, 32, 32, 32, 32, 32, 64, 128)
    return pl.pallas_call(
        finish_kernel,
        grid=(2,),
        out_shape=tuple(S(a.shape, a.dtype) for a in arrays) + tuple(S((n,), f32) for n in lengths),
        in_specs=blocks + [pl.BlockSpec((8, 128), lambda i: (0, 0))],
        out_specs=tuple(blocks) + tuple(pl.BlockSpec((n,), lambda i: (0,)) for n in lengths),
        compiler_params=pltpu.CompilerParams(vmem_limit_bytes=62 << 20),
        name="finish",
    )(*arrays, vec)


def layer(
    tokens, attn_gain, attn_shift, qkv_weight, qv_bias, out_weight, out_bias, mlp_gain, mlp_shift, up_weight, up_bias, down_weight,
    down_bias, cotangent,
):
    vectors = (attn_gain, attn_shift, out_bias, mlp_gain, mlp_shift, down_bias, qv_bias, up_bias)
    results = layer_call(tokens, cotangent, qkv_weight, out_weight, up_weight, down_weight, vectors)
    output, gtok, gqkv, gout, gup, gdown, ggain_a, gshift_a, gob, ggain_b, gshift_b, gdb, gqvb, gub = finish_call(*results)
    return output, gtok, ggain_a, gshift_a, gqkv, gqvb, gout, gob, ggain_b, gshift_b, gup, gub, gdown, gdb


def layer_norm(values_in, gain_vec, bias_vec):
    row_mean = jnp.mean(values_in, axis=-1, keepdims=True)
    centred = values_in - row_mean
    spread = jnp.mean(centred * centred, axis=-1, keepdims=True)
    return centred * lax.rsqrt(spread + epsilon) * gain_vec + bias_vec


def gelu_exact(values_in):
    return jax.nn.gelu(values_in, approximate=False)


def norm_backward(values_in, gain_vec, incoming):
    zero_shift = jnp.zeros_like(gain_vec)
    unused, pull_back = jax.vjp(layer_norm, values_in, gain_vec, zero_shift)
    return pull_back(incoming)


def general_layer(
    tokens,
    attn_gain,
    attn_shift,
    qkv_weight,
    qv_bias,
    out_weight,
    out_bias,
    mlp_gain,
    mlp_shift,
    up_weight,
    up_bias,
    down_weight,
    down_bias,
    cotangent,
):
    length, model_width = tokens.shape
    score_scale = HD ** (-0.5)
    gain_a, shift_a, qkv_full, qv_full, out_full, out_bias_full = (
        lax.all_gather(attn_gain, ("wide", "narrow"), axis=0, tiled=True),
        lax.all_gather(attn_shift, ("wide", "narrow"), axis=0, tiled=True),
        lax.all_gather(qkv_weight, ("wide", "narrow"), axis=0, tiled=True),
        lax.all_gather(qv_bias, ("wide", "narrow"), axis=0, tiled=True),
        lax.all_gather(out_weight, ("wide", "narrow"), axis=0, tiled=True),
        lax.all_gather(out_bias, ("wide", "narrow"), axis=0, tiled=True),
    )
    inputs = tokens.astype(jnp.float32)
    act_a = layer_norm(inputs, gain_a.astype(jnp.float32), shift_a.astype(jnp.float32)).astype(
        jnp.bfloat16
    )
    bias_full = jnp.concatenate(
        [qv_full[:model_width], jnp.zeros((model_width,), jnp.bfloat16), qv_full[model_width:]]
    ).astype(jnp.float32)
    projected = (jnp.dot(act_a, qkv_full, preferred_element_type=jnp.float32) + bias_full).astype(
        jnp.bfloat16
    )
    query_rows = projected[:, :model_width].reshape(length, H, HD)
    key_rows = projected[:, model_width : 2 * model_width].reshape(length, H, HD)
    value_rows = projected[:, 2 * model_width :].reshape(length, H, HD)
    block_rows = min(512, length)
    block_count = length // block_rows
    query_blocks = query_rows.reshape(block_count, block_rows, H, HD)

    def attend_block(query_block):
        scores = (
            jnp.einsum("qhe,khe->hqk", query_block, key_rows, preferred_element_type=jnp.float32)
            * score_scale
        )
        row_max = jnp.max(scores, axis=-1, keepdims=True)
        exp_scores = jnp.exp(scores - row_max)
        denominator = jnp.sum(exp_scores, axis=-1, keepdims=True)
        low_probs = (exp_scores / denominator).astype(jnp.bfloat16)
        mixed_block = jnp.einsum(
            "hqk,khe->qhe", low_probs, value_rows, preferred_element_type=jnp.float32
        )
        return (mixed_block, (row_max + jnp.log(denominator))[..., 0])

    mixed_blocks, log_sums = lax.map(attend_block, query_blocks)
    mixed = mixed_blocks.reshape(length, model_width).astype(jnp.bfloat16)
    hidden = (
        inputs
        + jnp.dot(mixed, out_full, preferred_element_type=jnp.float32)
        + out_bias_full.astype(jnp.float32)
    )
    gain_b, shift_b, up_full, up_bias_full, down_full, down_bias_full = (
        lax.all_gather(mlp_gain, ("wide", "narrow"), axis=0, tiled=True),
        lax.all_gather(mlp_shift, ("wide", "narrow"), axis=0, tiled=True),
        lax.all_gather(up_weight, ("wide", "narrow"), axis=0, tiled=True),
        lax.all_gather(up_bias, ("wide", "narrow"), axis=0, tiled=True),
        lax.all_gather(down_weight, ("wide", "narrow"), axis=0, tiled=True),
        lax.all_gather(down_bias, ("wide", "narrow"), axis=0, tiled=True),
    )
    act_b = layer_norm(hidden, gain_b.astype(jnp.float32), shift_b.astype(jnp.float32)).astype(
        jnp.bfloat16
    )
    pre_up = jnp.dot(act_b, up_full, preferred_element_type=jnp.float32) + up_bias_full.astype(
        jnp.float32
    )
    act_c = gelu_exact(pre_up).astype(jnp.bfloat16)
    output = (
        hidden
        + jnp.dot(act_c, down_full, preferred_element_type=jnp.float32)
        + down_bias_full.astype(jnp.float32)
    ).astype(jnp.bfloat16)
    gain_b_back, up_back, down_back = (
        lax.all_gather(mlp_gain, ("wide", "narrow"), axis=0, tiled=True),
        lax.all_gather(up_weight, ("wide", "narrow"), axis=0, tiled=True),
        lax.all_gather(down_weight, ("wide", "narrow"), axis=0, tiled=True),
    )
    grad_y = cotangent.astype(jnp.float32)
    grad_down_weight = jnp.einsum("sf,sd->fd", act_c, cotangent, preferred_element_type=jnp.float32)
    grad_down_bias = jnp.sum(cotangent.astype(jnp.float32), axis=0)
    grad_act = jnp.einsum("sd,fd->sf", cotangent, down_back, preferred_element_type=jnp.float32)
    unused_gelu, gelu_pull = jax.vjp(gelu_exact, pre_up)
    grad_pre = gelu_pull(grad_act)[0].astype(jnp.bfloat16)
    grad_up_weight = jnp.einsum("sd,sf->df", act_b, grad_pre, preferred_element_type=jnp.float32)
    grad_up_bias = jnp.sum(grad_pre.astype(jnp.float32), axis=0)
    grad_act_b = jnp.einsum("sf,df->sd", grad_pre, up_back, preferred_element_type=jnp.float32)
    hidden_part, grad_mlp_gain, grad_mlp_shift = norm_backward(
        hidden, gain_b_back.astype(jnp.float32), grad_act_b
    )
    grad_hidden = grad_y + hidden_part
    mlp_sums = (
        lax.psum_scatter(grad_mlp_gain, ("wide", "narrow"), scatter_dimension=0, tiled=True),
        lax.psum_scatter(grad_mlp_shift, ("wide", "narrow"), scatter_dimension=0, tiled=True),
        lax.psum_scatter(grad_up_weight, ("wide", "narrow"), scatter_dimension=0, tiled=True),
        lax.psum_scatter(grad_up_bias, ("wide", "narrow"), scatter_dimension=0, tiled=True),
        lax.psum_scatter(grad_down_weight, ("wide", "narrow"), scatter_dimension=0, tiled=True),
        lax.psum_scatter(grad_down_bias, ("wide", "narrow"), scatter_dimension=0, tiled=True),
    )
    gain_a_back, qkv_back, out_back = (
        lax.all_gather(attn_gain, ("wide", "narrow"), axis=0, tiled=True),
        lax.all_gather(qkv_weight, ("wide", "narrow"), axis=0, tiled=True),
        lax.all_gather(out_weight, ("wide", "narrow"), axis=0, tiled=True),
    )
    grad_branch = grad_hidden.astype(jnp.bfloat16)
    grad_out_weight = jnp.einsum(
        "sa,sd->ad", mixed, grad_branch, preferred_element_type=jnp.float32
    )
    grad_out_bias = jnp.sum(grad_branch.astype(jnp.float32), axis=0)
    grad_mixed = jnp.einsum(
        "sd,ad->sa", grad_branch, out_back, preferred_element_type=jnp.float32
    ).astype(jnp.bfloat16)
    grad_blocks = grad_mixed.reshape(block_count, block_rows, H, HD)

    def back_block(carry, block_inputs):
        key_total, value_total = carry
        query_block, grad_block, log_block = block_inputs
        scores = (
            jnp.einsum("qhe,khe->hqk", query_block, key_rows, preferred_element_type=jnp.float32)
            * score_scale
        )
        attn_probs = jnp.exp(scores - log_block[..., None])
        grad_probs = jnp.einsum(
            "qhe,khe->hqk", grad_block, value_rows, preferred_element_type=jnp.float32
        )
        row_delta = jnp.sum(grad_probs * attn_probs, axis=-1, keepdims=True)
        grad_scores = (attn_probs * (grad_probs - row_delta)).astype(jnp.bfloat16)
        low_probs = attn_probs.astype(jnp.bfloat16)
        value_total = value_total + jnp.einsum(
            "hqk,qhe->khe", low_probs, grad_block, preferred_element_type=jnp.float32
        )
        key_total = (
            key_total
            + jnp.einsum(
                "hqk,qhe->khe", grad_scores, query_block, preferred_element_type=jnp.float32
            )
            * score_scale
        )
        grad_query = (
            jnp.einsum("hqk,khe->qhe", grad_scores, key_rows, preferred_element_type=jnp.float32)
            * score_scale
        )
        return ((key_total, value_total), grad_query)

    zero_heads = jnp.zeros((length, H, HD), jnp.float32)
    (grad_key, grad_value), grad_query = lax.scan(
        back_block, (zero_heads, zero_heads), (query_blocks, grad_blocks, log_sums)
    )
    grad_projected = jnp.concatenate(
        [
            grad_query.reshape(length, model_width),
            grad_key.reshape(length, model_width),
            grad_value.reshape(length, model_width),
        ],
        axis=1,
    ).astype(jnp.bfloat16)
    grad_qkv_weight = jnp.einsum(
        "sa,sb->ab", act_a, grad_projected, preferred_element_type=jnp.float32
    )
    column_sums = jnp.sum(grad_projected.astype(jnp.float32), axis=0)
    grad_qv_bias = jnp.concatenate([column_sums[:model_width], column_sums[2 * model_width :]])
    grad_act_a = jnp.einsum(
        "sb,ab->sa", grad_projected, qkv_back, preferred_element_type=jnp.float32
    )
    input_part, grad_attn_gain, grad_attn_shift = norm_backward(
        inputs, gain_a_back.astype(jnp.float32), grad_act_a
    )
    grad_tokens = (grad_hidden + input_part).astype(jnp.bfloat16)
    attn_sums = (
        lax.psum_scatter(grad_attn_gain, ("wide", "narrow"), scatter_dimension=0, tiled=True),
        lax.psum_scatter(grad_attn_shift, ("wide", "narrow"), scatter_dimension=0, tiled=True),
        lax.psum_scatter(grad_qkv_weight, ("wide", "narrow"), scatter_dimension=0, tiled=True),
        lax.psum_scatter(grad_qv_bias, ("wide", "narrow"), scatter_dimension=0, tiled=True),
        lax.psum_scatter(grad_out_weight, ("wide", "narrow"), scatter_dimension=0, tiled=True),
        lax.psum_scatter(grad_out_bias, ("wide", "narrow"), scatter_dimension=0, tiled=True),
    )
    return (
        output,
        grad_tokens,
        attn_sums[0],
        attn_sums[1],
        attn_sums[2],
        attn_sums[3],
        attn_sums[4],
        attn_sums[5],
        mlp_sums[0],
        mlp_sums[1],
        mlp_sums[2],
        mlp_sums[3],
        mlp_sums[4],
        mlp_sums[5],
    )


def solution(mesh):
    placed = (
        P(("wide", "narrow"), None),
        P(("wide", "narrow")),
        P(("wide", "narrow")),
        P(("wide", "narrow"), None),
        P(("wide", "narrow")),
        P(("wide", "narrow"), None),
        P(("wide", "narrow")),
        P(("wide", "narrow")),
        P(("wide", "narrow")),
        P(("wide", "narrow"), None),
        P(("wide", "narrow")),
        P(("wide", "narrow"), None),
        P(("wide", "narrow")),
        P(("wide", "narrow"), None),
    )
    return jax.shard_map(
        layer if dict(mesh.shape) == {"wide": 8, "narrow": 4} else general_layer,
        mesh=mesh,
        in_specs=placed,
        out_specs=(
            P(("wide", "narrow"), None),
            P(("wide", "narrow"), None),
            P(("wide", "narrow")),
            P(("wide", "narrow")),
            P(("wide", "narrow"), None),
            P(("wide", "narrow")),
            P(("wide", "narrow"), None),
            P(("wide", "narrow")),
            P(("wide", "narrow")),
            P(("wide", "narrow")),
            P(("wide", "narrow"), None),
            P(("wide", "narrow")),
            P(("wide", "narrow"), None),
            P(("wide", "narrow")),
        ),
        check_vma=False,
    )
```

```python
import functools
import jax
import jax.numpy as jnp
from jax import lax
from jax.experimental import pallas as pl
from jax.experimental.pallas import tpu as pltpu
from jax.sharding import PartitionSpec as P

H = 16
HD = 64
epsilon = 1e-05
bf16 = jnp.bfloat16
f32 = jnp.float32
NN = (((1,), (0,)), ((), ()))
NT = (((1,), (1,)), ((), ()))
TN = (((0,), (0,)), ((), ()))
ALL = slice(None)
MESH = pl.DeviceIdType.MESH
HBM = pl.BlockSpec(memory_space=pltpu.HBM)
VMEM = pl.BlockSpec(memory_space=pltpu.VMEM)

HALVES = ((0, 2, 1, 3), (0, 3, 1, 2))
THIRDS = ((0, 1, 2, 3), (0, 3, 1, 2), (0, 2, 3, 1))
PIECES = 13
SENDINGS = 14
GATHER_START = (0, 0, 0, 0, 22, 23, 31, 34, 43, 45, 51, 48, 67)
GATHER_LAG = (
    (3, 3, 4.5, 4.5), (10, 16, 11, 16), (16, 7, 5, 4.5), (8, 5, 4.5, 8.5),
    (3, 3, 9.5, 8.5), (7, 3, 9.5, 8.5), (4, 5, 8.5, 5.5), (5, 7, 8.5, 8.5),
    (6, 3, 6.5, 10.5), (3, 6, 6.5, 13.5), (3, 5, 6.5, 15), (5, 10, 5, 14),
    (7, 3, 10.5, 7.5))
SCATTER_LAG = (4, 8, 10, 5, 6)
LAST_LAG = (2, 3, 3, 3, 12)
SCATTER_GAP = 7
SLOTS = 4
MAIL = 1
RING = 5
TURNS = 8


def dot(a, b, dims):
    return lax.dot_general(a, b, dims, preferred_element_type=f32)


def device_bits():
    w = lax.axis_index("wide")
    n = lax.axis_index("narrow")
    return (w // 4, (w // 2) % 2, w % 2, n // 2, n % 2)


def flipped(b, *dims):
    t = tuple(1 - v if i in dims else v for i, v in enumerate(b))
    return (t[0] * 4 + t[1] * 2 + t[2], t[3] * 2 + t[4])


def parts_of(width, thirds):
    if thirds:
        third = width // 3
        return [(order, n * third, third, n % 2, n // 2 * third) for n, order in enumerate(THIRDS)]
    return [(order, n * width // 2, width // 2, n, 0) for n, order in enumerate(HALVES)]


def head_mask(head, rows):
    return lax.shift_right_logical(lax.broadcasted_iota(jnp.int32, (rows, 256), 1), 6) == head


def norm_stats(v):
    mean = jnp.mean(v, axis=1, keepdims=True)
    centred = v - mean
    rstd = lax.rsqrt(jnp.mean(centred * centred, axis=1, keepdims=True) + epsilon)
    return centred, rstd


def norm_grad(centred, rstd, gain, e):
    xhat = centred * rstd
    eg = e * gain
    return rstd * (eg - jnp.mean(eg, axis=1, keepdims=True) - xhat * jnp.mean(eg * xhat, axis=1, keepdims=True)), xhat


def column_sum(v):
    return jnp.sum(v, axis=0, keepdims=True)


def block_pick(i, transposed):
    shape = (128, 512) if transposed else (512, 128)
    unit = lax.broadcasted_iota(jnp.int32, shape, 1 if transposed else 0)
    lane = lax.broadcasted_iota(jnp.int32, shape, 0 if transposed else 1)
    return jnp.where(unit == 128 * lax.shift_right_logical(lane, 5) + 32 * i + (lane & 31), 1.0, 0.0)


def layer_kernel(
    tok_h, cot_h, qkv_h, out_h, up_h, down_h, again_v, ashift_v, obias_v, mgain_v, mshift_v, dbias_v, qvbias_v, ubias_v,
    out_o, gtok_o, gqkv_o, gout_o, gup_o, gdown_o, vec_o, gw, spill, spill_f,
    gv, rows, level, delta, qkv, pb, pf, w, gup, vsum, vrecv,
    stag, mail, r1, r2, r3, r4, fin,
    insem, ownsem, wsem, spsem, outsem, ssem, rsem, vssem, vrsem, bssem, brsem, xsem, xssem, xrsem, credit, ussem, ursem, finsem,
):
    b = device_bits()
    zh, zl, x, y, c = b
    barrier = pltpu.get_barrier_semaphore()
    partners = ((0,), (1,), (2,), (3,), (4,), (2, 3), (0, 1))
    for dims in partners:
        pl.semaphore_signal(barrier, inc=1, device_id=flipped(b, *dims), device_id_type=MESH)

    def copy(src, dst, sem):
        cp = pltpu.make_async_copy(src, dst, sem)
        cp.start()
        return cp

    def remote(src, dst, send_sem, recv_sem, *dims):
        cp = pltpu.make_async_remote_copy(
            src_ref=src, dst_ref=dst, send_sem=send_sem, recv_sem=recv_sem, device_id=flipped(b, *dims), device_id_type=MESH)
        cp.start()
        return cp

    def rows_at(i):
        return pl.ds(pl.multiple_of(i * 256, 256), 256)

    quarter_rows = [pl.ds(256 * i, 256) for i in range(4)]
    act, mixed, trans, gbr, dout = (pb.at[i] for i in range(5))
    tok = dout
    hid, total, gab = (pf.at[i] for i in range(3))
    lse = hid.at[:, pl.ds(0, 128)]

    shards = [gbr.at[pl.ds(32 * p, 32), pl.ds(0, 768 if p < 4 else 1024)] for p in range(9)]
    for g in range(4):
        for t in range(3):
            copy(qkv_h.at[:, pl.ds(1024 * t + 256 * g, 256)], gbr.at[pl.ds(32 * g, 32), pl.ds(256 * t, 256)], ownsem.at[g])
    copy(out_h, shards[4], ownsem.at[4])
    for i in range(4):
        copy(down_h.at[pl.ds(32 * i, 32)], shards[5 + i], ownsem.at[5 + 2 * i])
    shards[5:] = [shards[5], w.at[2, 0, 0, 0, 0, 0], shards[6], w.at[2, 0, 0, 0, 0, 1], shards[7], w.at[2, 0, 0, 0, 1, 0], shards[8], w.at[2, 0, 0, 0, 1, 1]]
    own = {}
    for i in range(4):
        copy(up_h.at[:, pl.ds(1024 * i, 1024)], mixed.at[pl.ds(32 * i, 32)], insem.at[0])
    pl.semaphore_wait(barrier, len(partners))
    sent = {}
    arrived = set()

    def store_own(p):
        if p not in own:
            if p < 5 or p % 2 == 1:
                pltpu.make_async_copy(shards[p], shards[p], ownsem.at[p]).wait()
            own[p] = copy(shards[p], gw.at[(p,) + b + (ALL, pl.ds(0, 768 if p < 4 else 1024))], ownsem.at[p])

    def own_stored(p):
        if own[p] is not None:
            own[p].wait()
            own[p] = None

    def gather_stage(p, r):
        if r == 0:
            store_own(p)
        if r == (1 if p < 2 else 0):
            own_stored(p)
        for n, (order, first, width, _, _) in enumerate(parts_of(768 if p < 4 else 1024, p == 0)):
            cols = (ALL, pl.ds(first, width))

            def send(dim, sub, s):
                ref = gw.at[(p,) + sub + cols]
                src = shards[p].at[:, pl.ds(first, width)] if r == 0 and p < 2 else ref
                sem = rsem.at[p % TURNS, 8] if s == 4 else xsem.at[s] if n == 2 else rsem.at[p % TURNS, n * 4 + s]
                sent[(p, n, s)] = remote(src, ref, ssem.at[p], sem, dim)

            if r > 0:
                sent[(p, n, r - 1)].wait_recv()
            held = tuple(ALL if i in order[:r] else b[i] for i in range(5))
            if r < 4:
                send(order[r], held, r)
            if r == 3:
                send(4, held, 4)
            if r == 4:
                late = tuple(ALL if i in order[:3] else (1 - b[i] if i == order[3] else b[i]) for i in range(5))
                send(4, late, 4)

    now = [0.0]
    gathers = [[] for _ in range(PIECES)]
    scatters = [[] for _ in range(SENDINGS)]
    ready = [0]

    def due(issued, lags, share):
        return now[0] >= issued[-1] + share * lags[len(issued) - 1]

    def tick(spent):
        now[0] += spent
        for p, issued in enumerate(gathers):
            while len(issued) < 5 and (due(issued, GATHER_LAG[p], 1) if issued else now[0] >= GATHER_START[p]):
                gather_stage(p, len(issued))
                issued.append(now[0])
        for p, issued in enumerate(scatters[: ready[0]]):
            if not issued and p > 0 and now[0] < scatters[p - 1][0] + SCATTER_GAP and p < 12:
                break
            while len(issued) < 6 and (not issued or due(issued, SCATTER_LAG if p < 12 else LAST_LAG, 0.4 if p == 11 else 0.75 if p >= 9 else 1)):
                scatter_stage(p, len(issued))
                issued.append(now[0])

    def gather_up_to(stages):
        now[0] += 2.5
        for p, r in stages:
            gather_stage(p, r)
            gathers[p].append(now[0])

    def arrive(p):
        while len(gathers[p]) < 5:
            gather_stage(p, len(gathers[p]))
            gathers[p].append(now[0])
        if p not in arrived:
            half = spill.at[0, pl.ds(0, 512), pl.ds(0, 768 if p < 4 else 1024)]
            pltpu.make_async_copy(half, half, rsem.at[p % TURNS, 8]).wait()
            arrived.add(p)

    def all_sent(p):
        rest = spill.at[0, pl.ds(0, 992), pl.ds(0, 768 if p < 4 else 1024)]
        pltpu.make_async_copy(rest, rest, ssem.at[p]).wait()

    flights = {}

    def fetch(p, slot):
        arrive(p)
        flights[slot] = copy(gw.at[p], w.at[slot], wsem.at[slot])

    def weight(slot, cols=1024):
        return w[slot, :, :, :, :, :, :, pl.ds(0, cols)].reshape(1024, cols)

    def weight_rows(slot, i):
        return w[slot, i // 2, i % 2].reshape(256, 1024)

    vec_steps = (((4,),), ((2,), (3,), (2, 3)), ((1,), (0,), (0, 1)))
    vec_sent = []

    def vec_round(r):
        for cp in vec_sent[-3:] if r > 1 else vec_sent:
            cp.wait_recv()
        if r < 3:
            ref = gv.at[(b, b[:4] + (ALL,), b[:2] + (ALL, ALL, ALL))[r]]
            for dims in vec_steps[r]:
                n = len(vec_sent)
                vec_sent.append(remote(ref, ref, vssem.at[n], vrsem.at[n], *dims))

    gather_up_to([(0, 0)])
    tok_in = copy(tok_h, tok, insem.at[1])
    lines = [jnp.zeros((1, 128), f32)] * 3
    for n, (vector, line, offset) in enumerate((
        (again_v, 0, 0), (ashift_v, 0, 32), (obias_v, 0, 64), (mgain_v, 0, 96), (mshift_v, 1, 0), (dbias_v, 1, 32), (qvbias_v, 1, 64),
        (ubias_v, 2, 0),
    )):
        size = vector.shape[0]
        at = lax.broadcasted_iota(jnp.int32, (size, 128), 0)
        lane = lax.broadcasted_iota(jnp.int32, (size, 128), 1)
        put = jnp.where(lane == at + offset, 1.0, 0.0).astype(bf16)
        lines[line] = lines[line] + dot(vector[...].astype(f32).reshape(1, size).astype(bf16), put, NN)
    gv[b] = jnp.concatenate(lines + [jnp.zeros((5, 128), f32)], axis=0)
    vec_round(0)
    up_shard = mixed.at[pl.ds(0, 128)]
    pltpu.make_async_copy(up_shard, up_shard, insem.at[0]).wait()
    for i in range(4):
        pick = block_pick(i, False).astype(bf16)
        for g in range(8):
            shards[6 + 2 * i][:, 128 * g : 128 * g + 128] = dot(
                mixed[32 * (g // 2) : 32 * (g // 2) + 32, 512 * (g % 2) : 512 * (g % 2) + 512], pick, NN).astype(bf16)
    for p in range(PIECES):
        store_own(p)
    vec_round(1)
    gather_up_to([(0, 1)])
    vec_round(2)
    gather_up_to([(0, 2), (1, 0)])
    vec_round(3)
    table = gv[...].reshape(32, 8, 128)
    sub_index = lax.broadcasted_iota(jnp.int32, (32, 8, 128), 1)
    lines = [jnp.sum(jnp.where(sub_index == r, table, 0.0), axis=1) for r in range(3)]

    def spread(line, offset, log, base):
        j = lax.broadcasted_iota(jnp.int32, (128, 1024), 0)
        n = lax.broadcasted_iota(jnp.int32, (128, 1024), 1)
        pick = jnp.where(j == offset + (n & ((1 << log) - 1)), 1.0, 0.0).astype(bf16)
        broad = dot(line.astype(bf16), pick, NN)
        d = lax.broadcasted_iota(jnp.int32, (32, 1024), 0)
        n = lax.broadcasted_iota(jnp.int32, (32, 1024), 1)
        return column_sum(jnp.where(d == base + lax.shift_right_logical(n, log), broad, 0.0))

    places = [(0, 0, 5, 0), (0, 32, 5, 0), (0, 64, 5, 0), (0, 96, 5, 0), (1, 0, 5, 0), (1, 32, 5, 0), (1, 64, 6, 0), (1, 64, 6, 16)]
    places += [(2, 32 * i, 5, 0) for i in range(4)]
    for i, (line, offset, log, base) in enumerate(places):
        rows[i : i + 1, :] = spread(lines[line], offset, log, base)

    gather_up_to([(0, 3), (1, 1), (2, 0)])

    tok_in.wait()

    def first_norm(i, carry):
        r = rows_at(i)
        centred, rstd = norm_stats(tok[r, :].astype(f32))
        a = (centred * rstd * rows[0:1, :] + rows[1:2, :]).astype(bf16)
        act[r, :] = a
        trans[:, r] = a.T
        return carry

    lax.fori_loop(0, 4, first_norm, 0)
    act_out = copy(trans, spill.at[0], spsem.at[0])
    for p in range(PIECES):
        own_stored(p)
    gather_up_to([(0, 4), (1, 2), (2, 1), (3, 0)])
    lse[...] = jnp.zeros_like(lse)

    def project(g, slot):
        at = pl.ds(256 * g, 256)
        bias = jnp.concatenate([rows[6:7, at], jnp.zeros((1, 256), f32), rows[7:8, at]], axis=1)

        def block(i, carry):
            r = rows_at(i)
            qkv[g, r, :] = (dot(act[r, :], weight(slot, 768), NN) + bias).astype(bf16)
            return carry

        lax.fori_loop(0, 4, block, 0)

    def attend(g, first):
        q, k, v = (qkv.at[g, :, pl.ds(256 * i, 256)] for i in range(3))

        def one(i, carry):
            head = first + i
            mask = head_mask(head, 1024)
            some = mask[:256]
            lane = lax.broadcasted_iota(jnp.int32, (256, 128), 1)
            vm = jnp.where(mask, v[...], bf16(1))

            def score(r):
                return dot(jnp.where(some, q[r, :], bf16(0)) * bf16(0.125), k[...], NT)

            def soft(s):
                m = jnp.max(s, axis=1, keepdims=True)
                e = jnp.exp(s - m)
                return e.astype(bf16), m + jnp.log(jnp.sum(e, axis=1, keepdims=True))

            def mix(r, p, m):
                o = dot(p, vm, NN)
                gab[r, 0:256] = jnp.where(some, o / pltpu.roll(o, 64, axis=1), gab[r, 0:256])
                lse[r, :] = jnp.where(lane == g * 4 + head, m, lse[r, :])

            s = score(quarter_rows[0])
            last = None
            for j, r in enumerate(quarter_rows):
                later = score(quarter_rows[j + 1]) if j < 3 else None
                p = soft(s)
                if last is not None:
                    mix(quarter_rows[j - 1], *last)
                last, s = p, later
            mix(quarter_rows[3], *last)
            return carry

        lax.fori_loop(0, 2, one, 0)

    now[0] = 22.0
    fetch(0, 0)
    for g in range(4):
        flights[g % 2].wait()
        if g == 0:
            tick(0)
        project(g, g % 2)
        tick(2.3)
        attend(g, 0)
        tick(3.6)
        fetch(g + 1, (g + 1) % 2 if g < 3 else 2)
        attend(g, 2)
        tick(3.6)
        mixed[:, 256 * g : 256 * g + 256] = gab[:, 0:256].astype(bf16)
        total[256 * g : 256 * g + 256, :] = gab[:, 0:256].T
        if g == 3:
            mix_out = copy(total, spill_f, spsem.at[1])
            fetch(5, 0)
    act_out.wait()
    flights[2].wait()

    level[...] = lse[...].T[0:16]
    all_sent(0)
    all_sent(1)

    def second_norm(i, carry):
        r = rows_at(i)
        v = tok[r, :].astype(f32) + dot(mixed[r, :], weight(2), NN) + rows[2:3, :]
        hid[r, :] = v
        centred, rstd = norm_stats(v)
        a = (centred * rstd * rows[3:4, :] + rows[4:5, :]).astype(bf16)
        act[r, :] = a
        trans[:, r] = a.T
        return carry

    lax.fori_loop(0, 4, second_norm, 0)
    tick(4.5)
    cot = mixed
    cot_in = copy(cot_h, cot, insem.at[2])

    got = {}
    fins = {}

    def half_of(p):
        return 384 if p >= 9 else 512

    def scatter_stage(p, r):
        width = 384 if p >= 12 else 768 if p >= 9 else 1024
        a = stag.at[p % SLOTS, 0]
        k = p % RING
        parts = parts_of(width, p >= 12)

        def send(s, dim, src, dst, n=0):
            sems = (xssem.at[p - 12, s - 1], xrsem.at[p - 12, s - 1]) if n == 2 else (bssem.at[k, s + 4 * n], brsem.at[k, s + 4 * n])
            got[(p, n, s)] = remote(src, dst, *sems, dim)

        if r == 0:
            if p >= MAIL:
                pl.semaphore_wait(credit, 1)
            full = (ALL, ALL, ALL, ALL, ALL, pl.ds(0, width))
            send(0, 4, stag.at[(p % SLOTS, 1) + full], mail.at[(p % MAIL,) + full])
        if r == 1:
            got[(p, 0, 0)].wait_recv()

            def add(i, carry):
                at = (i // 8, (i // 4) % 2, (i // 2) % 2, i % 2, ALL, pl.ds(0, width))
                a[at] = a[at] + mail[(p % MAIL,) + at]
                return carry

            lax.fori_loop(0, 16, add, 0)
            if p + MAIL < SENDINGS:
                pl.semaphore_signal(credit, inc=1, device_id=flipped(b, 4), device_id_type=MESH)
        for n, (order, first, size, half, off) in enumerate(parts if r > 0 else ()):
            dims = [d for d in range(4) if d not in order[5 - r :]]
            gone = order[4 - r] if r < 5 else None
            cols, lanes = pl.ds(first, size), pl.ds(off, size)
            buffers = (None, r1, r2, r3, r4)

            def block(level, at):
                return buffers[level].at[(k, half) + tuple(at) + (ALL, lanes)]

            if r == 1:
                src = a.at[tuple(1 - b[d] if d == gone else ALL for d in range(4)) + (ALL, cols)]
                send(1, gone, src, block(1, (ALL,) * 3), n)
                continue
            got[(p, n, r - 1)].wait_recv()
            if r > 2:
                got[(p, n, r - 1)].wait_send()
            if r == 5:
                continue
            before = [d for d in range(4) if d not in order[6 - r :]]
            last = order[5 - r]

            def add(i, carry):
                bits = [(i // 2 ** (len(dims) - 1 - m)) % 2 for m in range(len(dims))]
                here = dict(zip(dims, bits))
                here[last] = b[last]
                mine = block(r - 1, bits)
                if r == 2:
                    other = a.at[tuple(here[d] for d in range(4)) + (ALL, cols)]
                else:
                    other = block(r - 2, [here[d] for d in before])
                mine[...] = mine[...] + other[...]
                return carry

            if r == 2:
                lax.fori_loop(0, 8, add, 0)
            else:
                for i in range(2 ** len(dims)):
                    add(i, 0)
            src = block(r - 1, [1 - b[d] if d == gone else ALL for d in dims])
            send(r, gone, src, block(r, (ALL,) * (len(dims) - 1)), n)
        if r == 5:
            if p - RING in fins:
                fins.pop(p - RING).wait()
            for n, (order, first, size, half, off) in enumerate(parts):
                if p < 8 and p % 2 == 1:
                    continue
                lanes = pl.ds(off, size)
                fin[k, :, pl.ds(first, size)] = r3[k, half, zh, :, lanes].astype(f32) + r4[k, half, :, lanes].astype(f32)
            if p >= 9:
                size = width // 3
                column = 768 + 128 * (p - 12) if p >= 12 else 256 * (p - 9)
                for t in range(3):
                    copy(fin.at[k, :, pl.ds(size * t, size)], gqkv_o.at[:, pl.ds(1024 * t + column, size)], finsem.at[k])
                whole = fin.at[k, :, pl.ds(0, width)]
                fins[p] = pltpu.make_async_copy(whole, whole, finsem.at[k])
            elif p == 8:
                fins[p] = copy(fin.at[k], gout_o, finsem.at[k])
            elif p % 2 == 0:
                fins[p] = copy(fin.at[k], gdown_o.at[pl.ds(16 * p, 32)], finsem.at[k])
            else:
                put = block_pick(p // 2, True).astype(bf16)
                put = jnp.concatenate([put, put], axis=0)
                columns = [(g // 4, pl.ds(128 * (g % 4), 128)) for g in range(8)]
                parts = [jnp.concatenate([r3[k, h, zh, :, lane], r4[k, h, :, lane]], axis=1) for h, lane in columns]
                spread_out = dot(jnp.concatenate(parts, axis=0), put, NN)
                for g in range(8):
                    at, value = slice(512 * g, 512 * g + 512), spread_out[32 * g : 32 * g + 32]
                    gup[:, at] = value if p == 1 else gup[:, at] + value
                if p == 7:
                    fins[p] = copy(gup, gup_o, finsem.at[k])

    def push(p, stages):
        while len(scatters[p]) < stages:
            if p > 0 and not scatters[p - 1]:
                push(p - 1, 1)
            scatter_stage(p, len(scatters[p]))
            scatters[p].append(now[0])

    def free(p):
        if p >= SLOTS:
            push(p - SLOTS, 3)
            for key in ((0, 0), (0, 1), (1, 1)):
                got.pop((p - SLOTS,) + key).wait_send()

    def keep_all(p, product):
        def one(n, carry):
            value = product(pl.ds(pl.multiple_of(n * 512, 512), 512))
            width = value.shape[1]
            blocks = value.astype(bf16).reshape(2, 2, 2, 2, 32, width)
            for core in range(2):
                stag[p % SLOTS, (core + c) % 2, n, :, :, :, :, pl.ds(0, width)] = blocks[:, :, :, core]
            return carry

        lax.fori_loop(0, 2, one, 0)

    actb, actbt, actc, gpre = act, trans, gbr, dout
    fetch(6, 1)
    mix_out.wait()
    cot_in.wait()
    for i in range(4):
        flights[0].wait()
        flights[1].wait()

        def mlp_rows(n, bias_sum):
            r = rows_at(n)
            v = dot(actb[r, :], weight(1), NN) + rows[8 + i : 9 + i, :]
            back = dot(cot[r, :], weight(0), NT)
            cdf = 0.5 * (1.0 + lax.erf(v * 0.7071067811865476))
            slope = cdf + v * jnp.exp(-0.5 * v * v) * 0.3989422804014327
            u = (v * cdf).astype(bf16)
            e = (back * slope).astype(bf16)
            actc[r, :] = u
            gpre[r, :] = e
            if i == 0:
                total[r, :] = dot(u, weight(0), NN)
                gab[r, :] = dot(e, weight(1), NT)
            else:
                total[r, :] += dot(u, weight(0), NN)
                gab[r, :] += dot(e, weight(1), NT)
            return bias_sum + column_sum(e.astype(f32))

        bias_sum = jnp.zeros((1, 1024), f32)
        for n in (0, 2):
            bias_sum = lax.fori_loop(n, n + 2, mlp_rows, bias_sum)
            tick(4.9)
        vsum[4 + i : 5 + i, :] = bias_sum
        if i < 3:
            fetch(7 + 2 * i, 0)
        else:
            fetch(4, 2)
        free(2 * i)
        keep_all(2 * i, lambda r: dot(actc[:, r], cot[...], TN))
        ready[0] = 2 * i + 1
        tick(2.9)
        if i < 3:
            fetch(8 + 2 * i, 1)
        free(2 * i + 1)
        keep_all(2 * i + 1, lambda r: dot(actbt[r, :], gpre[...], NN))
        ready[0] = 2 * i + 2
        tick(2.9)
    assert all(len(issued) == 5 for issued in gathers)
    fetch(0, 0)
    fetch(1, 1)

    def second_norm_back(i, sums):
        r = rows_at(i)
        h = hid[r, :]
        act[r, :] = (h + total[r, :] + rows[5:6, :]).astype(bf16)
        centred, rstd = norm_stats(h)
        e = gab[r, :]
        back, xhat = norm_grad(centred, rstd, rows[3:4, :], e)
        yv = cot[r, :].astype(f32)
        gh = yv + back
        total[r, :] = gh
        gb = gh.astype(bf16)
        gbr[r, :] = gb
        return tuple(s + column_sum(v) for s, v in zip(sums, (e * xhat, e, yv, gb.astype(f32))))

    sums = lax.fori_loop(0, 4, second_norm_back, (jnp.zeros((1, 1024), f32),) * 4)
    for i in range(4):
        vsum[i : i + 1, :] = sums[i]
    ghid, gaa = total, gab
    mix_in = copy(spill_f, hid, insem.at[3])
    out_copy = copy(act, out_o, outsem.at[0])
    actt = cot
    actt_in = copy(spill.at[0], actt, insem.at[4])

    tick(4)

    flights[2].wait()
    for i in range(4):
        dout[quarter_rows[i], :] = dot(weight_rows(2, i), gbr[...], NT).astype(bf16)
    mix_in.wait()
    for i in range(4):
        mix_part = hid[quarter_rows[i], :]
        trans[quarter_rows[i], :] = mix_part.astype(bf16)
        share = dout[quarter_rows[i], :].astype(f32) * mix_part
        delta[pl.ds(4 * i, 4), :] = jnp.sum(share.reshape(4, 64, 1024), axis=1)
    tick(2.2)
    free(8)
    keep_all(8, lambda r: dot(trans[r, :], gbr[...], NN))
    ready[0] = 9
    tok = trans
    tok_in = copy(tok_h, tok, insem.at[1])
    actt_in.wait()
    dq, dk, dv = (hid.at[:, pl.ds(256 * i, 256)] for i in range(3))

    def attend_back(g, first, count):
        q, k, v = (qkv.at[g, :, pl.ds(256 * i, 256)] for i in range(3))

        def one(i, carry):
            head = first + i
            mask = head_mask(head, 1024)
            some = mask[:256]
            low = lax.shift_right_logical(lax.broadcasted_iota(jnp.int32, (256, 256), 0), 6) == head
            km = jnp.where(mask, k[...], bf16(0))

            def masked(r):
                qm = jnp.where(some, q[r, :], bf16(0)) * bf16(0.125)
                return qm, jnp.where(low, dout[pl.ds(256 * g, 256), r], bf16(0))

            def score(r):
                qm, dom = masked(r)
                return dot(k[...], qm, NT), dot(v[...], dom, NN)

            def soft(r, s, dp):
                p = jnp.exp(s - level[pl.ds(g * 4 + head, 1), r])
                return p.astype(bf16), (p * (dp - delta[pl.ds(g * 4 + head, 1), r])).astype(bf16)

            def grads(r, p, ds):
                qm, dom = masked(r)
                dq[r, :] = jnp.where(some, dot(ds, km, TN) * 0.125, dq[r, :])
                return dot(ds, qm, NN), dot(p, dom, NT)

            dkh, dvh = 0.0, 0.0
            s = score(quarter_rows[0])
            for j in range(5):
                later = score(quarter_rows[j + 1]) if j < 3 else None
                held = soft(quarter_rows[j], *s) if j < 4 else None
                if j > 0:
                    dk_part, dv_part = grads(quarter_rows[j - 1], *last)
                    dkh, dvh = dkh + dk_part, dvh + dv_part
                last, s = held, later
            dk[...] = jnp.where(mask, dkh, dk[...])
            dv[...] = jnp.where(mask, dvh, dv[...])
            return carry

        lax.fori_loop(0, count, one, 0)

    vec_parts = ((4,), (2,), (3,), (2, 3), (1,), (0,), (0, 1))
    vec_steps = ((0,), (1, 2, 3), (4, 5, 6))
    flying = {}

    def vector_send(part, step):
        lines = pl.ds(8 * part, 8)
        for n in vec_steps[step]:
            flying[(part, n)] = remote(
                vsum.at[lines], vrecv.at[n, lines], ussem.at[part, n], ursem.at[part, n], *vec_parts[n])

    def vector_add(part, step):
        lines = pl.ds(8 * part, 8)
        for n in vec_steps[step]:
            flying[(part, n)].wait()
        for n in vec_steps[step]:
            vsum[lines, :] = vsum[lines, :] + vrecv[n, lines, :]

    def act_back_all(g):
        flights[g % 2].wait()

        def act_back(i, carry):
            r = rows_at(i)
            part = dot(qkv[g, r, :], weight(g % 2, 768), NT)
            if g == 0:
                gaa[r, :] = part
            else:
                gaa[r, :] += part
            return carry

        lax.fori_loop(0, 4, act_back, 0)

    def hand_over(g, p, first, width):
        for t, part in enumerate((dq, dk, dv)):
            qkv[g, :, 256 * t + first : 256 * t + first + width] = part[:, first : first + width].astype(bf16)
        free(p)

        def grads():
            return jnp.concatenate([qkv[g, :, 256 * t + first : 256 * t + first + width] for t in range(3)], axis=1)

        keep_all(p, lambda r: dot(actt[r, :], grads(), NN))
        ready[0] = p + 1

    vector_send(0, 0)
    for g in range(4):
        for first in (0, 2):
            attend_back(g, first, 2)
            tick(5.9)
            if first == 2 and g < 3:
                vector_add(0, g)
                if g < 2:
                    vector_send(0, g + 1)
            if g == 3:
                hand_over(3, 12 + first // 2, 64 * first, 128)
                tick(1.2)
        if g < 3:
            hand_over(g, 9 + g, 0, 256)
            tick(2.2)
        at = pl.ds(256 * g, 256)
        vsum[8:9, at] = column_sum(qkv[g, :, 0:256].astype(f32))
        vsum[9:10, at] = column_sum(qkv[g, :, 512:768].astype(f32))
        act_back_all(g)
        if g < 2:
            fetch(g + 2, g % 2)
        tick(2.4)

    out_copy.wait()
    tok_in.wait()

    def first_norm_back(i, sums):
        r = rows_at(i)
        centred, rstd = norm_stats(tok[r, :].astype(f32))
        e = gaa[r, :]
        back, xhat = norm_grad(centred, rstd, rows[0:1, :], e)
        act[r, :] = (ghid[r, :] + back).astype(bf16)
        return tuple(s + column_sum(v) for s, v in zip(sums, (e * xhat, e)))

    sums = (jnp.zeros((1, 1024), f32),) * 2
    sums = lax.fori_loop(0, 2, first_norm_back, sums)
    tick(1.7)
    sums = lax.fori_loop(2, 4, first_norm_back, sums)
    gtok_copy = copy(act, gtok_o, outsem.at[1])
    vsum[10:11, :] = sums[0]
    vsum[11:12, :] = sums[1]
    vsum[12:16, :] = jnp.zeros((4, 1024), f32)
    own_index = ((zh * 2 + zl) * 2 + x) * 4 + y * 2 + c
    n = lax.broadcasted_iota(jnp.int32, (1024, 128), 0)
    j = lax.broadcasted_iota(jnp.int32, (1024, 128), 1)

    def cut(value, base):
        pick = jnp.where(n == base + j, 1.0, 0.0)
        return lax.dot_general(value, pick, NN, precision=lax.Precision.HIGHEST, preferred_element_type=f32)

    vector_send(1, 0)
    tick(1.7)
    vector_add(1, 0)
    vector_send(1, 1)
    early = cut(vsum[0:8, :], 32 * own_index)
    for i, at in ((2, 3), (3, 0), (4, 1), (5, 2)):
        vec_o[i : i + 1, :] = early[at : at + 1]
    lane = lax.broadcasted_iota(jnp.int32, (1, 128), 1)
    up = early[4:5]
    for i in range(1, 4):
        up = jnp.where(lax.shift_right_logical(lane, 5) == i, pltpu.roll(early, 32 * i, axis=1)[4 + i : 5 + i], up)
    vec_o[7:8, :] = up
    for p in range(2, PIECES):
        all_sent(p)
    for cp in vec_sent:
        cp.wait_send()
    tick(3.5)
    vector_add(1, 1)
    vector_send(1, 2)
    tick(3.5)
    vector_add(1, 2)
    late = cut(vsum[8:16, :], 32 * own_index)
    middle = cut(vsum[8:16, :], 64 * (own_index % 16))
    vec_o[0:1, :] = late[2:3]
    vec_o[1:2, :] = late[3:4]
    vec_o[6:7, :] = jnp.where(own_index < 16, middle[0:1], middle[1:2])
    while len(scatters[SENDINGS - 1]) < 6:
        tick(4)
    for p in range(SENDINGS - SLOTS, SENDINGS):
        for key in ((0, 0), (0, 1), (1, 1)) + (((2, 1),) if p >= 12 else ()):
            got[(p,) + key].wait_send()
    for cp in fins.values():
        cp.wait()
    gtok_copy.wait()


def layer_call(tok, cot, qkv, out, up, down, vectors):
    S = jax.ShapeDtypeStruct
    V = pltpu.VMEM
    sem = pltpu.SemaphoreType.DMA
    big = (2, 2, 2, 2, 2, 32, 1024)
    n = PIECES
    results = pl.pallas_call(
        layer_kernel,
        out_shape=(
            S((1024, 1024), bf16), S((1024, 1024), bf16), S((32, 3072), f32), S((32, 1024), f32), S((32, 4096), f32),
            S((128, 1024), f32), S((8, 128), f32), S((n,) + big, bf16), S((1, 1024, 1024), bf16),
            S((1024, 1024), f32)),
        in_specs=[HBM] * 6 + [VMEM] * 8,
        out_specs=(HBM,) * 6 + (VMEM, HBM, HBM, HBM),
        scratch_shapes=[
            V((2, 2, 2, 2, 2, 8, 128), f32), V((16, 1024), f32), V((16, 1024), f32), V((16, 1024), f32),
            V((4, 1024, 768), bf16), V((5, 1024, 1024), bf16), V((3, 1024, 1024), f32), V((3,) + big, bf16), V((32, 4096), f32),
            V((16, 1024), f32), V((7, 16, 1024), f32),
            V((SLOTS, 2, 2, 2, 2, 2, 32, 1024), bf16), V((MAIL, 2, 2, 2, 2, 32, 1024), bf16), V((RING, 2, 2, 2, 2, 32, 512), bf16),
            V((RING, 2, 2, 2, 32, 512), bf16), V((RING, 2, 2, 32, 512), bf16), V((RING, 2, 32, 512), bf16), V((RING, 32, 1024), f32),
            sem((5,)), sem((n,)), sem((3,)), sem((2,)), sem((2,)), sem((n,)), sem((TURNS, 9)), sem((7,)), sem((7,)),
            sem((RING, 9)), sem((RING, 9)), sem((4,)), sem((2, 4)), sem((2, 4)),
            pltpu.SemaphoreType.REGULAR, sem((2, 7)), sem((2, 7)), sem((RING,))],
        compiler_params=pltpu.CompilerParams(collective_id=1, has_side_effects=True, vmem_limit_bytes=64 << 20),
        name="layer",
    )(tok, cot, qkv, out, up, down, *vectors)
    return results[:7]


def finish_kernel(*refs):
    for src, dst in zip(refs[:6], refs[7:13]):
        dst[...] = src[...]
    for i, o in enumerate(refs[13:]):
        o[...] = refs[6][i, : o.shape[0]]


def finish_call(out, gtok, gqkv, gout, gup, gdown, vec):
    S = jax.ShapeDtypeStruct
    arrays = (out, gtok, gqkv, gout, gup, gdown)
    blocks = []
    for a in arrays:
        rows, cols = a.shape
        if rows > 32:
            blocks.append(pl.BlockSpec((rows // 2, cols), lambda i: (i, 0)))
        else:
            blocks.append(pl.BlockSpec((rows, cols // 2), lambda i: (0, i)))
    lengths = (32, 32, 32, 32, 32, 32, 64, 128)
    return pl.pallas_call(
        finish_kernel,
        grid=(2,),
        out_shape=tuple(S(a.shape, a.dtype) for a in arrays) + tuple(S((n,), f32) for n in lengths),
        in_specs=blocks + [pl.BlockSpec((8, 128), lambda i: (0, 0))],
        out_specs=tuple(blocks) + tuple(pl.BlockSpec((n,), lambda i: (0,)) for n in lengths),
        compiler_params=pltpu.CompilerParams(vmem_limit_bytes=62 << 20),
        name="finish",
    )(*arrays, vec)


def layer(
    tokens, attn_gain, attn_shift, qkv_weight, qv_bias, out_weight, out_bias, mlp_gain, mlp_shift, up_weight, up_bias, down_weight,
    down_bias, cotangent,
):
    vectors = (attn_gain, attn_shift, out_bias, mlp_gain, mlp_shift, down_bias, qv_bias, up_bias)
    results = layer_call(tokens, cotangent, qkv_weight, out_weight, up_weight, down_weight, vectors)
    output, gtok, gqkv, gout, gup, gdown, ggain_a, gshift_a, gob, ggain_b, gshift_b, gdb, gqvb, gub = finish_call(*results)
    return output, gtok, ggain_a, gshift_a, gqkv, gqvb, gout, gob, ggain_b, gshift_b, gup, gub, gdown, gdb


def layer_norm(values_in, gain_vec, bias_vec):
    row_mean = jnp.mean(values_in, axis=-1, keepdims=True)
    centred = values_in - row_mean
    spread = jnp.mean(centred * centred, axis=-1, keepdims=True)
    return centred * lax.rsqrt(spread + epsilon) * gain_vec + bias_vec


def gelu_exact(values_in):
    return jax.nn.gelu(values_in, approximate=False)


def norm_backward(values_in, gain_vec, incoming):
    zero_shift = jnp.zeros_like(gain_vec)
    unused, pull_back = jax.vjp(layer_norm, values_in, gain_vec, zero_shift)
    return pull_back(incoming)


def general_layer(
    tokens,
    attn_gain,
    attn_shift,
    qkv_weight,
    qv_bias,
    out_weight,
    out_bias,
    mlp_gain,
    mlp_shift,
    up_weight,
    up_bias,
    down_weight,
    down_bias,
    cotangent,
):
    length, model_width = tokens.shape
    score_scale = HD ** (-0.5)
    gain_a, shift_a, qkv_full, qv_full, out_full, out_bias_full = (
        lax.all_gather(attn_gain, ("wide", "narrow"), axis=0, tiled=True),
        lax.all_gather(attn_shift, ("wide", "narrow"), axis=0, tiled=True),
        lax.all_gather(qkv_weight, ("wide", "narrow"), axis=0, tiled=True),
        lax.all_gather(qv_bias, ("wide", "narrow"), axis=0, tiled=True),
        lax.all_gather(out_weight, ("wide", "narrow"), axis=0, tiled=True),
        lax.all_gather(out_bias, ("wide", "narrow"), axis=0, tiled=True),
    )
    inputs = tokens.astype(jnp.float32)
    act_a = layer_norm(inputs, gain_a.astype(jnp.float32), shift_a.astype(jnp.float32)).astype(
        jnp.bfloat16
    )
    bias_full = jnp.concatenate(
        [qv_full[:model_width], jnp.zeros((model_width,), jnp.bfloat16), qv_full[model_width:]]
    ).astype(jnp.float32)
    projected = (jnp.dot(act_a, qkv_full, preferred_element_type=jnp.float32) + bias_full).astype(
        jnp.bfloat16
    )
    query_rows = projected[:, :model_width].reshape(length, H, HD)
    key_rows = projected[:, model_width : 2 * model_width].reshape(length, H, HD)
    value_rows = projected[:, 2 * model_width :].reshape(length, H, HD)
    block_rows = min(512, length)
    block_count = length // block_rows
    query_blocks = query_rows.reshape(block_count, block_rows, H, HD)

    def attend_block(query_block):
        scores = (
            jnp.einsum("qhe,khe->hqk", query_block, key_rows, preferred_element_type=jnp.float32)
            * score_scale
        )
        row_max = jnp.max(scores, axis=-1, keepdims=True)
        exp_scores = jnp.exp(scores - row_max)
        denominator = jnp.sum(exp_scores, axis=-1, keepdims=True)
        low_probs = (exp_scores / denominator).astype(jnp.bfloat16)
        mixed_block = jnp.einsum(
            "hqk,khe->qhe", low_probs, value_rows, preferred_element_type=jnp.float32
        )
        return (mixed_block, (row_max + jnp.log(denominator))[..., 0])

    mixed_blocks, log_sums = lax.map(attend_block, query_blocks)
    mixed = mixed_blocks.reshape(length, model_width).astype(jnp.bfloat16)
    hidden = (
        inputs
        + jnp.dot(mixed, out_full, preferred_element_type=jnp.float32)
        + out_bias_full.astype(jnp.float32)
    )
    gain_b, shift_b, up_full, up_bias_full, down_full, down_bias_full = (
        lax.all_gather(mlp_gain, ("wide", "narrow"), axis=0, tiled=True),
        lax.all_gather(mlp_shift, ("wide", "narrow"), axis=0, tiled=True),
        lax.all_gather(up_weight, ("wide", "narrow"), axis=0, tiled=True),
        lax.all_gather(up_bias, ("wide", "narrow"), axis=0, tiled=True),
        lax.all_gather(down_weight, ("wide", "narrow"), axis=0, tiled=True),
        lax.all_gather(down_bias, ("wide", "narrow"), axis=0, tiled=True),
    )
    act_b = layer_norm(hidden, gain_b.astype(jnp.float32), shift_b.astype(jnp.float32)).astype(
        jnp.bfloat16
    )
    pre_up = jnp.dot(act_b, up_full, preferred_element_type=jnp.float32) + up_bias_full.astype(
        jnp.float32
    )
    act_c = gelu_exact(pre_up).astype(jnp.bfloat16)
    output = (
        hidden
        + jnp.dot(act_c, down_full, preferred_element_type=jnp.float32)
        + down_bias_full.astype(jnp.float32)
    ).astype(jnp.bfloat16)
    gain_b_back, up_back, down_back = (
        lax.all_gather(mlp_gain, ("wide", "narrow"), axis=0, tiled=True),
        lax.all_gather(up_weight, ("wide", "narrow"), axis=0, tiled=True),
        lax.all_gather(down_weight, ("wide", "narrow"), axis=0, tiled=True),
    )
    grad_y = cotangent.astype(jnp.float32)
    grad_down_weight = jnp.einsum("sf,sd->fd", act_c, cotangent, preferred_element_type=jnp.float32)
    grad_down_bias = jnp.sum(cotangent.astype(jnp.float32), axis=0)
    grad_act = jnp.einsum("sd,fd->sf", cotangent, down_back, preferred_element_type=jnp.float32)
    unused_gelu, gelu_pull = jax.vjp(gelu_exact, pre_up)
    grad_pre = gelu_pull(grad_act)[0].astype(jnp.bfloat16)
    grad_up_weight = jnp.einsum("sd,sf->df", act_b, grad_pre, preferred_element_type=jnp.float32)
    grad_up_bias = jnp.sum(grad_pre.astype(jnp.float32), axis=0)
    grad_act_b = jnp.einsum("sf,df->sd", grad_pre, up_back, preferred_element_type=jnp.float32)
    hidden_part, grad_mlp_gain, grad_mlp_shift = norm_backward(
        hidden, gain_b_back.astype(jnp.float32), grad_act_b
    )
    grad_hidden = grad_y + hidden_part
    mlp_sums = (
        lax.psum_scatter(grad_mlp_gain, ("wide", "narrow"), scatter_dimension=0, tiled=True),
        lax.psum_scatter(grad_mlp_shift, ("wide", "narrow"), scatter_dimension=0, tiled=True),
        lax.psum_scatter(grad_up_weight, ("wide", "narrow"), scatter_dimension=0, tiled=True),
        lax.psum_scatter(grad_up_bias, ("wide", "narrow"), scatter_dimension=0, tiled=True),
        lax.psum_scatter(grad_down_weight, ("wide", "narrow"), scatter_dimension=0, tiled=True),
        lax.psum_scatter(grad_down_bias, ("wide", "narrow"), scatter_dimension=0, tiled=True),
    )
    gain_a_back, qkv_back, out_back = (
        lax.all_gather(attn_gain, ("wide", "narrow"), axis=0, tiled=True),
        lax.all_gather(qkv_weight, ("wide", "narrow"), axis=0, tiled=True),
        lax.all_gather(out_weight, ("wide", "narrow"), axis=0, tiled=True),
    )
    grad_branch = grad_hidden.astype(jnp.bfloat16)
    grad_out_weight = jnp.einsum(
        "sa,sd->ad", mixed, grad_branch, preferred_element_type=jnp.float32
    )
    grad_out_bias = jnp.sum(grad_branch.astype(jnp.float32), axis=0)
    grad_mixed = jnp.einsum(
        "sd,ad->sa", grad_branch, out_back, preferred_element_type=jnp.float32
    ).astype(jnp.bfloat16)
    grad_blocks = grad_mixed.reshape(block_count, block_rows, H, HD)

    def back_block(carry, block_inputs):
        key_total, value_total = carry
        query_block, grad_block, log_block = block_inputs
        scores = (
            jnp.einsum("qhe,khe->hqk", query_block, key_rows, preferred_element_type=jnp.float32)
            * score_scale
        )
        attn_probs = jnp.exp(scores - log_block[..., None])
        grad_probs = jnp.einsum(
            "qhe,khe->hqk", grad_block, value_rows, preferred_element_type=jnp.float32
        )
        row_delta = jnp.sum(grad_probs * attn_probs, axis=-1, keepdims=True)
        grad_scores = (attn_probs * (grad_probs - row_delta)).astype(jnp.bfloat16)
        low_probs = attn_probs.astype(jnp.bfloat16)
        value_total = value_total + jnp.einsum(
            "hqk,qhe->khe", low_probs, grad_block, preferred_element_type=jnp.float32
        )
        key_total = (
            key_total
            + jnp.einsum(
                "hqk,qhe->khe", grad_scores, query_block, preferred_element_type=jnp.float32
            )
            * score_scale
        )
        grad_query = (
            jnp.einsum("hqk,khe->qhe", grad_scores, key_rows, preferred_element_type=jnp.float32)
            * score_scale
        )
        return ((key_total, value_total), grad_query)

    zero_heads = jnp.zeros((length, H, HD), jnp.float32)
    (grad_key, grad_value), grad_query = lax.scan(
        back_block, (zero_heads, zero_heads), (query_blocks, grad_blocks, log_sums)
    )
    grad_projected = jnp.concatenate(
        [
            grad_query.reshape(length, model_width),
            grad_key.reshape(length, model_width),
            grad_value.reshape(length, model_width),
        ],
        axis=1,
    ).astype(jnp.bfloat16)
    grad_qkv_weight = jnp.einsum(
        "sa,sb->ab", act_a, grad_projected, preferred_element_type=jnp.float32
    )
    column_sums = jnp.sum(grad_projected.astype(jnp.float32), axis=0)
    grad_qv_bias = jnp.concatenate([column_sums[:model_width], column_sums[2 * model_width :]])
    grad_act_a = jnp.einsum(
        "sb,ab->sa", grad_projected, qkv_back, preferred_element_type=jnp.float32
    )
    input_part, grad_attn_gain, grad_attn_shift = norm_backward(
        inputs, gain_a_back.astype(jnp.float32), grad_act_a
    )
    grad_tokens = (grad_hidden + input_part).astype(jnp.bfloat16)
    attn_sums = (
        lax.psum_scatter(grad_attn_gain, ("wide", "narrow"), scatter_dimension=0, tiled=True),
        lax.psum_scatter(grad_attn_shift, ("wide", "narrow"), scatter_dimension=0, tiled=True),
        lax.psum_scatter(grad_qkv_weight, ("wide", "narrow"), scatter_dimension=0, tiled=True),
        lax.psum_scatter(grad_qv_bias, ("wide", "narrow"), scatter_dimension=0, tiled=True),
        lax.psum_scatter(grad_out_weight, ("wide", "narrow"), scatter_dimension=0, tiled=True),
        lax.psum_scatter(grad_out_bias, ("wide", "narrow"), scatter_dimension=0, tiled=True),
    )
    return (
        output,
        grad_tokens,
        attn_sums[0],
        attn_sums[1],
        attn_sums[2],
        attn_sums[3],
        attn_sums[4],
        attn_sums[5],
        mlp_sums[0],
        mlp_sums[1],
        mlp_sums[2],
        mlp_sums[3],
        mlp_sums[4],
        mlp_sums[5],
    )


def solution(mesh):
    placed = (
        P(("wide", "narrow"), None),
        P(("wide", "narrow")),
        P(("wide", "narrow")),
        P(("wide", "narrow"), None),
        P(("wide", "narrow")),
        P(("wide", "narrow"), None),
        P(("wide", "narrow")),
        P(("wide", "narrow")),
        P(("wide", "narrow")),
        P(("wide", "narrow"), None),
        P(("wide", "narrow")),
        P(("wide", "narrow"), None),
        P(("wide", "narrow")),
        P(("wide", "narrow"), None),
    )
    return jax.shard_map(
        layer if dict(mesh.shape) == {"wide": 8, "narrow": 4} else general_layer,
        mesh=mesh,
        in_specs=placed,
        out_specs=(
            P(("wide", "narrow"), None),
            P(("wide", "narrow"), None),
            P(("wide", "narrow")),
            P(("wide", "narrow")),
            P(("wide", "narrow"), None),
            P(("wide", "narrow")),
            P(("wide", "narrow"), None),
            P(("wide", "narrow")),
            P(("wide", "narrow")),
            P(("wide", "narrow")),
            P(("wide", "narrow"), None),
            P(("wide", "narrow")),
            P(("wide", "narrow"), None),
            P(("wide", "narrow")),
        ),
        check_vma=False,
    )
```
